256 devices in a mesh: mem: 64 (over y, z, core), dp: 4 (over x).
Axes of the slice: x: 4, y: 4, z: 8, core: 2. Of those that a mesh axis runs over, the one named last changes fastest.
Arguments:
- picks: int32 [81920, 4], P(('mem', 'dp')), may hold values from 0 to 32767, as said below
- pick_weights: bfloat16 [81920, 4], P(('mem', 'dp')), may hold values from -4 to 4
- token_grads: bfloat16 [81920, 2048], P(('mem', 'dp')), may hold values from -6 to 6
- values: bfloat16 [32768, 512], P('mem'), may hold values from -6 to 6
- first_moment: float32 [32768, 512], P(('mem', 'dp')), may hold values from -1.5 to 1.5
- second_moment: float32 [32768, 512], P(('mem', 'dp')), may hold values from 0.01 to 1
- projectors: bfloat16 [4, 512, 2048], replicated, may hold values from -0.25 to 0.25
Outputs:
- layer_out: bfloat16 [81920, 2048], P(('mem', 'dp'))
- new_values: bfloat16 [32768, 512], P('mem')
- new_first: float32 [32768, 512], P(('mem', 'dp'))
- new_second: float32 [32768, 512], P(('mem', 'dp'))
The draws below stay inside these ranges and needn't reach their ends.
Inputs may be any that keep to these rules, and one draw needn't show every extreme that they name: Among the picks of one device's tokens (rows of the same aligned block of 320 tokens) at most 40 fall into one range of 512 rows [o * 512, (o + 1) * 512); in every draw one such range receives exactly 40 picks from every block.
All inputs are finite; a program needn't handle non-finite values.
Results may differ from the reference program's by a relative error of at most 0.0055.
Values may be sent and summed in bfloat16 or wider, within the bound.
No kernel may reach another device: no remote copies, remote signals or barrier semaphores. Data moves between devices by JAX's collectives and lax.ppermute only.
A program may use at most 128 MiB of HBM per device.

```python
import math
import jax
import jax.numpy as jnp
from jax import lax

D = 512
DM = 2048
NPROJ = 4
M = 4
TOK_DEV = 320
ROWS_DEV = 512
TOKENS = 81920
VALUE_ROWS = 32768
CAP = 40


def draw_picks(key, part):
    key = jax.random.fold_in(key, 11)
    owners_count = VALUE_ROWS // ROWS_DEV
    block_count = TOKENS // TOK_DEV
    picks_block = TOK_DEV * M
    busiest = jax.random.randint(jax.random.fold_in(key, 1), (), 0, owners_count)
    block_keys = jax.random.split(jax.random.fold_in(key, 2), block_count)

    def one_block(block_key):
        key_slots, key_shuffle, key_rows = jax.random.split(block_key, 3)
        shuffled = jax.random.permutation(key_slots, owners_count * CAP)
        owner_of = shuffled // CAP
        ranking = jnp.where(owner_of == busiest, 0, 1 + jnp.arange(owners_count * CAP, dtype=jnp.int32))
        chosen = shuffled[jnp.argsort(ranking, stable=True)][:picks_block] // CAP
        chosen = jax.random.permutation(key_shuffle, chosen)
        row_ids = jax.random.randint(key_rows, (picks_block,), 0, ROWS_DEV)
        return (chosen * ROWS_DEV + row_ids).astype(jnp.int32)
    return jax.vmap(one_block)(block_keys).reshape(TOKENS, M)


def levels(own_key, extent, cuts, smallest, largest):
    def one(position, shards_of):
        steps = jax.random.uniform(jax.random.fold_in(jax.random.fold_in(own_key, 6), position), (shards_of,), jnp.float32, smallest / len(cuts), largest / len(cuts))
        return jnp.repeat(jnp.exp(steps), extent[position] // shards_of).reshape((-1,) + (1,) * (len(extent) - position - 1))

    factor_of = one(*cuts[0])
    for cut in cuts[1:]:
        factor_of = factor_of * one(*cut)
    return factor_of


def scatter_about(rng, shape, spread, reach, shards=(), kind=jnp.bfloat16):
    drawn = spread * jax.random.normal(rng, shape, jnp.float32)
    if shards:
        drawn = drawn * levels(rng, shape, shards, -0.22, 0.18)
    return jnp.clip(drawn, -reach, reach).astype(kind)


def setup_inputs(seed: int = 0) -> dict:
    arg_keys = jax.random.split(jax.random.key(seed), 8)
    picks = draw_picks(jax.random.fold_in(arg_keys[7], 71), 0)
    pick_weights = scatter_about(arg_keys[1], (TOKENS, M), 1.0, 4.0, ((0, 256),))
    token_grads = scatter_about(arg_keys[2], (TOKENS, DM), 1.0, 6.0, ((0, 256),))
    values = scatter_about(arg_keys[3], (VALUE_ROWS, D), 1.0, 6.0, ((0, 64),))
    first_moment = scatter_about(arg_keys[4], (VALUE_ROWS, D), 0.1, 1.5, ((0, 256),), jnp.float32)
    second_moment = jnp.clip(jnp.exp(math.log(1.0) - 4.6051702 * jax.random.uniform(arg_keys[5], (VALUE_ROWS, D), jnp.float32) ** levels(arg_keys[5], (VALUE_ROWS, D), ((0, 256),), -0.2, 0.2)), 0.01, 1.0)
    projectors = scatter_about(arg_keys[6], (NPROJ, D, DM), D ** -0.5, 0.25)
    return {"picks": picks, "pick_weights": pick_weights, "token_grads": token_grads, "values": values, "first_moment": first_moment, "second_moment": second_moment, "projectors": projectors}


beta_one = 0.9
beta_two = 0.999
corr_one = 1.0 - 0.9 ** 50
corr_two = 1.0 - 0.999 ** 50
learn_rate = 0.05
adam_eps = 1e-08

def reference(picks, pick_weights, token_grads, values, first_moment, second_moment, projectors):
    flat_proj = projectors.reshape(NPROJ * D, DM)
    block_count = TOKENS // TOK_DEV
    block_items = (picks.reshape(block_count, TOK_DEV, M), pick_weights.reshape(block_count, TOK_DEV, M), token_grads.reshape(block_count, TOK_DEV, DM))

    def one_block(grad_acc, items):
        pick_ids, pick_wts, grad_rows = items
        picked = values[pick_ids].astype(jnp.float32)
        proj_ids = pick_ids % NPROJ
        mixing = jnp.where(proj_ids[..., None] == jnp.arange(NPROJ, dtype=jnp.int32), pick_wts.astype(jnp.float32)[..., None], jnp.float32(0.0))
        proj_sums = jnp.einsum('tjp,tjd->tpd', mixing, picked).astype(jnp.bfloat16)
        layer_out = jnp.dot(proj_sums.reshape(TOK_DEV, NPROJ * D), flat_proj, preferred_element_type=jnp.float32).astype(jnp.bfloat16)
        back_grads = jnp.dot(grad_rows, flat_proj.T, preferred_element_type=jnp.float32)
        back_grads = back_grads.astype(jnp.bfloat16).reshape(TOK_DEV, NPROJ, D)
        chosen = back_grads[jnp.arange(TOK_DEV, dtype=jnp.int32)[:, None], proj_ids]
        weighted = pick_wts.astype(jnp.float32)[..., None] * chosen.astype(jnp.float32)
        grad_acc = grad_acc.at[pick_ids.reshape(-1)].add(weighted.reshape(-1, D))
        return (grad_acc, layer_out)
    slab_grad, layers = lax.scan(one_block, jnp.zeros((VALUE_ROWS, D), jnp.float32), block_items)
    new_first = beta_one * first_moment + (1.0 - beta_one) * slab_grad
    new_second = beta_two * second_moment + (1.0 - beta_two) * slab_grad * slab_grad
    update_step = new_first / corr_one / (jnp.sqrt(new_second / corr_two) + adam_eps)
    new_values = (values.astype(jnp.float32) - learn_rate * update_step).astype(jnp.bfloat16)
    return (layers.reshape(TOKENS, DM), new_values, new_first, new_second)
```

```python
import functools

import jax
import jax.numpy as jnp
from jax import lax
from jax.experimental import pallas as pl
from jax.experimental.pallas import tpu as pltpu
from jax.sharding import Mesh
from jax.sharding import PartitionSpec as P

beta_one = 0.9
beta_two = 0.999
corr_one = 1.0 - 0.9**50
corr_two = 1.0 - 0.999**50
learn_rate = 0.05
adam_eps = 1e-08

Z_CHIPS = 8
CORES = 2
CAP = 80
LANES = 128
FLAG_ROWS = 16
VMEM = 56 * 1024 * 1024
BF = jnp.bfloat16
F32 = jnp.float32
NT = (((1,), (1,)), ((), ()))


def adam_rows(old_rows, slab_grad, first_moment, second_moment):
    new_first = beta_one * first_moment + (1.0 - beta_one) * slab_grad
    new_second = beta_two * second_moment + (1.0 - beta_two) * slab_grad * slab_grad
    update_step = new_first / corr_one / (jnp.sqrt(new_second / corr_two) + adam_eps)
    updated = (old_rows.astype(jnp.float32) - learn_rate * update_step).astype(jnp.bfloat16)
    return (new_first, new_second, updated)


def long_way(picks, pick_weights, token_grads, values, first_moment, second_moment, projectors):
    mem = ("y", "z", "c")
    owners = lax.axis_size(mem)
    rows_dev = values.shape[0]
    width = values.shape[1]
    tok_count, per_token = picks.shape
    proj_count = projectors.shape[0]
    out_width = projectors.shape[2]
    total_picks = tok_count * per_token
    capacity = 2 * total_picks // owners
    flat_picks = picks.reshape(-1)
    owner_ids = flat_picks // rows_dev
    local_rows = flat_picks - owner_ids * rows_dev
    member = (owner_ids[:, None] == jnp.arange(owners, dtype=jnp.int32)[None, :]).astype(jnp.int32)
    before = jnp.cumsum(member, axis=0) - member
    slot_ids = owner_ids * capacity + jnp.sum(before * member, axis=1)
    proj_ids = picks % proj_count
    flat_proj = projectors.reshape(proj_count * width, out_width)
    requests = jnp.zeros((owners * capacity,), jnp.int32).at[slot_ids].set(local_rows)
    requests = requests.reshape(owners, capacity)
    received = lax.all_to_all(requests, mem, split_axis=0, concat_axis=0, tiled=True)
    looked = values[received]
    returned = lax.all_to_all(looked, mem, split_axis=0, concat_axis=0, tiled=True)
    back_grads = lax.dot_general(token_grads, flat_proj, NT, preferred_element_type=jnp.float32)
    back_grads = back_grads.astype(jnp.bfloat16).reshape(tok_count, proj_count, width)
    chosen = back_grads[jnp.arange(tok_count, dtype=jnp.int32)[:, None], proj_ids].reshape(
        total_picks, width
    )
    grad_rows = jnp.zeros((owners * capacity, width), jnp.bfloat16).at[slot_ids].set(chosen)
    grad_wts = (
        jnp.zeros((owners * capacity,), jnp.bfloat16).at[slot_ids].set(pick_weights.reshape(-1))
    )
    got_rows = lax.all_to_all(
        grad_rows.reshape(owners, capacity, width), mem, split_axis=0, concat_axis=0, tiled=True
    )
    got_wts = lax.all_to_all(
        grad_wts.reshape(owners, capacity), mem, split_axis=0, concat_axis=0, tiled=True
    )
    picked = returned.reshape(owners * capacity, width)[slot_ids].reshape(
        tok_count, per_token, width
    )
    mixing = jnp.where(
        proj_ids[..., None] == jnp.arange(proj_count, dtype=jnp.int32),
        pick_weights[..., None],
        jnp.zeros((), jnp.bfloat16),
    )
    proj_sums = jnp.einsum(
        "tjp,tjd->tpd", mixing, picked, preferred_element_type=jnp.float32
    ).astype(jnp.bfloat16)
    layer_out = jnp.dot(
        proj_sums.reshape(tok_count, proj_count * width),
        flat_proj,
        preferred_element_type=jnp.float32,
    ).astype(jnp.bfloat16)
    weighted = got_wts.astype(jnp.float32)[..., None] * got_rows.astype(jnp.float32)
    slab_grad = (
        jnp.zeros((rows_dev, width), jnp.float32)
        .at[received.reshape(-1)]
        .add(weighted.reshape(-1, width))
    )
    quarter = first_moment.shape[0]
    start = lax.axis_index("x") * quarter
    share = lax.psum_scatter(slab_grad, "x", scatter_dimension=0, tiled=True)
    old_rows = lax.dynamic_slice_in_dim(values, start, quarter, 0)
    new_first, new_second, new_part = adam_rows(old_rows, share, first_moment, second_moment)
    new_values = lax.all_gather(new_part, "x", axis=0, tiled=True)
    return (layer_out, new_values, new_first, new_second)


def call(kernel, out_shape, grid=None, in_specs=None, out_specs=None, scratch=(), cost=None):
    extra = {} if grid is None else {"grid": grid}
    if in_specs is not None:
        extra["in_specs"] = in_specs
    if out_specs is not None:
        extra["out_specs"] = out_specs
    return pl.pallas_call(
        kernel,
        out_shape=out_shape,
        scratch_shapes=list(scratch),
        compiler_params=pltpu.CompilerParams(vmem_limit_bytes=VMEM),
        cost_estimate=cost,
        **extra,
    )


def cost(flops, nbytes):
    return pl.CostEstimate(flops=flops, bytes_accessed=nbytes, transcendentals=0)


def rank_kernel(cells, block, cell_ref, trow_ref, rank_ref, req_ref):
    count = cell_ref.shape[1]
    below = lax.broadcasted_iota(jnp.int32, (block, block), 0) < lax.broadcasted_iota(
        jnp.int32, (block, block), 1
    )
    below = below.astype(F32).astype(BF)
    carry = jnp.zeros((cells, 1), F32)
    asked = jnp.zeros((3 * cells, LANES), F32)
    for b in range(count // block):
        span = pl.ds(b * block, block)
        cell = cell_ref[:, span]
        trow = trow_ref[:, span]
        here = (lax.broadcasted_iota(jnp.int32, (cells, block), 0) == cell).astype(F32)
        before = jnp.dot(here.astype(BF), below, preferred_element_type=F32) + carry
        carry = carry + jnp.sum(here, axis=1, keepdims=True)
        rank = jnp.sum(here * before, axis=0, keepdims=True).astype(jnp.int32)
        rank_ref[:, span] = rank
        place = (lax.broadcasted_iota(jnp.int32, (LANES, block), 0) == rank).astype(F32)
        high = (trow >> 5).astype(F32)
        low = (trow & 31).astype(F32)
        told = jnp.concatenate([here, here * high, here * low], axis=0)
        asked = asked + lax.dot_general(
            told.astype(BF), place.astype(BF), NT, preferred_element_type=F32
        )
    there = asked[:cells]
    rows = (asked[cells : 2 * cells] * 32.0 + asked[2 * cells :]).astype(jnp.int32)
    rows = jnp.where(there > 0.5, rows, -1)
    lane = lax.broadcasted_iota(jnp.int32, (cells, LANES), 1)
    over = (jnp.max(carry) > CAP).astype(jnp.int32)
    req_ref[...] = jnp.where(lane == LANES - 1, over, rows)


def send_kernel(
    cells, tok, tg_ref, proj_ref, pcol_ref, cell_ref, rank_ref, wt_ref, out_ref, chosen, place
):
    step = pl.program_id(0)
    per_token = pcol_ref.shape[1]
    back = lax.dot_general(tg_ref[...], proj_ref[0], NT, preferred_element_type=F32)
    back = back.astype(BF)
    for j in range(per_token):
        mine = pcol_ref[:, j : j + 1] == step
        span = pl.ds(j * tok, tok)

        @pl.when(step == 0)
        def _():
            chosen[span, :] = back

        @pl.when(step > 0)
        def _():
            chosen[span, :] = jnp.where(mine, back, chosen[span, :])

    @pl.when(step == pl.num_programs(0) - 1)
    def _():
        count = cell_ref.shape[1]
        at = lax.broadcasted_iota(jnp.int32, (CAP, count), 0) == rank_ref[...]
        place[...] = jnp.where(at, wt_ref[...].astype(F32), 0.0).astype(BF)
        group = 4
        for g in range(cells // group):
            parts = []
            for d in range(g * group, (g + 1) * group):
                here = (cell_ref[...] == d).astype(F32).astype(BF)
                parts.append(place[...] * here)
            pick = jnp.concatenate(parts, axis=0)
            out_ref[pl.ds(g * group * CAP, group * CAP), :] = jnp.dot(
                pick, chosen[...], preferred_element_type=F32
            ).astype(BF)


def look_kernel(ids_ref, table_ref, out_ref):
    rows = ids_ref.shape[0]
    total = table_ref.shape[0]
    pick = lax.broadcasted_iota(jnp.int32, (rows, total), 1) == ids_ref[...]
    out_ref[...] = jnp.dot(
        pick.astype(F32).astype(BF), table_ref[...], preferred_element_type=F32
    ).astype(BF)


def sum_kernel(rows, ids_ref, flags_ref, got_ref, out_ref):
    base = pl.program_id(0) * rows
    slots = ids_ref.shape[1]
    pick = lax.broadcasted_iota(jnp.int32, (rows, slots), 0) + base == ids_ref[...]
    out_ref[:rows, :] = jnp.dot(
        pick.astype(F32).astype(BF), got_ref[...], preferred_element_type=F32
    ).astype(out_ref.dtype)
    over = jnp.max(flags_ref[...]).astype(F32)
    out_ref[rows:, :] = jnp.full((FLAG_ROWS, out_ref.shape[1]), over, F32).astype(out_ref.dtype)


def out_kernel(slot_ref, pcol_ref, wcol_ref, ret_ref, proj_ref, out_ref, picked, total):
    step = pl.program_id(0)
    tok, per_token = slot_ref.shape
    slots = ret_ref.shape[0]

    @pl.when(step == 0)
    def _():
        lane = lax.broadcasted_iota(jnp.int32, (tok, slots), 1)
        for j in range(per_token):
            pick = (lane == slot_ref[:, j : j + 1]).astype(F32).astype(BF)
            row = jnp.dot(pick, ret_ref[...], preferred_element_type=F32)
            picked[j] = row * wcol_ref[:, j : j + 1]

    sums = jnp.zeros(picked.shape[1:], F32)
    for j in range(per_token):
        sums = sums + jnp.where(pcol_ref[:, j : j + 1] == step, picked[j], 0.0)
    part = jnp.dot(sums.astype(BF), proj_ref[0], preferred_element_type=F32)

    @pl.when(step == 0)
    def _():
        total[...] = part

    @pl.when(step > 0)
    def _():
        total[...] += part

    @pl.when(step == pl.num_programs(0) - 1)
    def _():
        out_ref[...] = total[...].astype(BF)


def short_way(picks, pick_weights, token_grads, values, first_moment, second_moment, projectors):
    plane = ("y", "c", "x")
    cells = lax.axis_size(plane)
    depth = lax.axis_size("z")
    parts = lax.axis_size("x")
    rows_dev, width = values.shape
    quarter = rows_dev // parts
    tok, per_token = picks.shape
    proj_count, _, out_width = projectors.shape
    total = tok * per_token
    slots = cells * CAP
    table_rows = depth * quarter
    start = lax.axis_index("x") * quarter
    old_rows = lax.dynamic_slice_in_dim(values, start, quarter, 0)
    table = lax.all_gather(old_rows, "z", axis=0, tiled=True)

    by_pick = picks.T.reshape(1, total)
    owner = by_pick // rows_dev
    row = by_pick % rows_dev
    owner_y = owner // (depth * CORES)
    owner_z = (owner // CORES) % depth
    cell = (owner_y * CORES + owner % CORES) * parts + row // quarter
    trow = owner_z * quarter + row % quarter
    block = 256
    rank, requests = call(
        functools.partial(rank_kernel, cells, block),
        (
            jax.ShapeDtypeStruct((1, total), jnp.int32),
            jax.ShapeDtypeStruct((cells, LANES), jnp.int32),
        ),
        cost=cost(2 * total * cells * 400, 20000),
    )(cell, trow)
    received = lax.all_to_all(requests, plane, split_axis=0, concat_axis=0, tiled=True)

    pcol = picks % proj_count
    wt_row = pick_weights.T.reshape(1, total)
    whole = lambda shape: pl.BlockSpec(shape, lambda i: (0,) * len(shape))
    sent = call(
        functools.partial(send_kernel, cells, tok),
        jax.ShapeDtypeStruct((slots, width), BF),
        grid=(proj_count,),
        in_specs=[
            whole((tok, out_width)),
            pl.BlockSpec((1, width, out_width), lambda i: (i, 0, 0)),
            whole((tok, per_token)),
            whole((1, total)),
            whole((1, total)),
            whole((1, total)),
        ],
        out_specs=whole((slots, width)),
        scratch=[pltpu.VMEM((total, width), BF), pltpu.VMEM((CAP, total), BF)],
        cost=cost(2 * width * (tok * proj_count * out_width + slots * total), 12000000),
    )(token_grads, projectors, pcol, cell, rank, wt_row)
    got = lax.all_to_all(
        sent.reshape(cells, CAP, width), plane, split_axis=0, concat_axis=0, tiled=True
    ).reshape(slots, width)

    asked = received[:, :CAP]
    flags = received[:, LANES - 1 :]
    chunk = slots // 8
    looked = call(
        look_kernel,
        jax.ShapeDtypeStruct((slots, width), BF),
        grid=(8,),
        in_specs=[
            pl.BlockSpec((chunk, 1), lambda i: (i, 0)),
            whole((table_rows, width)),
        ],
        out_specs=pl.BlockSpec((chunk, width), lambda i: (i, 0)),
        cost=cost(2 * width * slots * table_rows, 4000000),
    )(asked.reshape(slots, 1), table)
    returned = lax.all_to_all(
        looked.reshape(cells, CAP, width), plane, split_axis=0, concat_axis=0, tiled=True
    ).reshape(slots, width)

    sums = call(
        functools.partial(sum_kernel, quarter),
        jax.ShapeDtypeStruct((depth * (quarter + FLAG_ROWS), width), BF),
        grid=(depth,),
        in_specs=[whole((1, slots)), whole((cells, 1)), whole((slots, width))],
        out_specs=pl.BlockSpec((quarter + FLAG_ROWS, width), lambda i: (i, 0)),
        cost=cost(2 * width * slots * table_rows, 4000000),
    )(asked.reshape(1, slots), flags, got)
    share = lax.psum_scatter(sums, "z", scatter_dimension=0, tiled=True).astype(F32)
    flag = share[quarter, 0]
    new_first, new_second, new_part = adam_rows(
        old_rows, share[:quarter], first_moment, second_moment
    )
    new_values = lax.all_gather(new_part, "x", axis=0, tiled=True)

    slot_col = (cell * CAP + rank).reshape(per_token, tok).T
    layer_out = call(
        out_kernel,
        jax.ShapeDtypeStruct((tok, out_width), BF),
        grid=(proj_count,),
        in_specs=[
            whole((tok, per_token)),
            whole((tok, per_token)),
            whole((tok, per_token)),
            whole((slots, width)),
            pl.BlockSpec((1, width, out_width), lambda i: (i, 0, 0)),
        ],
        out_specs=whole((tok, out_width)),
        scratch=[
            pltpu.VMEM((per_token, tok, width), F32),
            pltpu.VMEM((tok, out_width), F32),
        ],
        cost=cost(2 * width * (tok * proj_count * out_width + slots * total), 13000000),
    )(slot_col, pcol, pick_weights.astype(F32), returned, projectors)
    return flag, (layer_out, new_values, new_first, new_second)


def on_device(*args):
    flag, outs = short_way(*args)
    return lax.cond(flag > 0.5, lambda given, done: long_way(*given), lambda given, done: done, args, outs)


def solution(mesh):
    mem, dp = mesh.devices.shape
    grid = Mesh(
        mesh.devices.reshape(mem // (Z_CHIPS * CORES), Z_CHIPS, CORES, dp), ("y", "z", "c", "x")
    )
    every = P(("y", "z", "c", "x"), None)
    slab = P(("y", "z", "c"), None)
    return jax.shard_map(
        on_device,
        mesh=grid,
        in_specs=(every, every, every, slab, every, every, P()),
        out_specs=(every, slab, every, every),
        check_vma=False,
    )
```

```python
import functools

import jax
import jax.numpy as jnp
from jax import lax
from jax.experimental import pallas as pl
from jax.experimental.pallas import tpu as pltpu
from jax.sharding import Mesh
from jax.sharding import PartitionSpec as P

beta_one = 0.9
beta_two = 0.999
corr_one = 1.0 - 0.9**50
corr_two = 1.0 - 0.999**50
learn_rate = 0.05
adam_eps = 1e-08

Z_CHIPS = 8
CORES = 2
CAP = 80
LANES = 128
FLAG_ROWS = 16
VMEM = 40 * 1024 * 1024
BF = jnp.bfloat16
F32 = jnp.float32
NT = (((1,), (1,)), ((), ()))


def adam_rows(old_rows, slab_grad, first_moment, second_moment):
    new_first = beta_one * first_moment + (1.0 - beta_one) * slab_grad
    new_second = beta_two * second_moment + (1.0 - beta_two) * slab_grad * slab_grad
    update_step = new_first / corr_one / (jnp.sqrt(new_second / corr_two) + adam_eps)
    updated = (old_rows.astype(jnp.float32) - learn_rate * update_step).astype(jnp.bfloat16)
    return (new_first, new_second, updated)


def long_way(picks, pick_weights, token_grads, values, first_moment, second_moment, projectors):
    mem = ("y", "z", "c")
    owners = lax.axis_size(mem)
    rows_dev = values.shape[0]
    width = values.shape[1]
    tok_count, per_token = picks.shape
    proj_count = projectors.shape[0]
    out_width = projectors.shape[2]
    total_picks = tok_count * per_token
    capacity = 2 * total_picks // owners
    flat_picks = picks.reshape(-1)
    owner_ids = flat_picks // rows_dev
    local_rows = flat_picks - owner_ids * rows_dev
    member = (owner_ids[:, None] == jnp.arange(owners, dtype=jnp.int32)[None, :]).astype(jnp.int32)
    before = jnp.cumsum(member, axis=0) - member
    slot_ids = owner_ids * capacity + jnp.sum(before * member, axis=1)
    proj_ids = picks % proj_count
    flat_proj = projectors.reshape(proj_count * width, out_width)
    requests = jnp.zeros((owners * capacity,), jnp.int32).at[slot_ids].set(local_rows)
    requests = requests.reshape(owners, capacity)
    received = lax.all_to_all(requests, mem, split_axis=0, concat_axis=0, tiled=True)
    looked = values[received]
    returned = lax.all_to_all(looked, mem, split_axis=0, concat_axis=0, tiled=True)
    back_grads = lax.dot_general(token_grads, flat_proj, NT, preferred_element_type=jnp.float32)
    back_grads = back_grads.astype(jnp.bfloat16).reshape(tok_count, proj_count, width)
    chosen = back_grads[jnp.arange(tok_count, dtype=jnp.int32)[:, None], proj_ids].reshape(
        total_picks, width
    )
    grad_rows = jnp.zeros((owners * capacity, width), jnp.bfloat16).at[slot_ids].set(chosen)
    grad_wts = (
        jnp.zeros((owners * capacity,), jnp.bfloat16).at[slot_ids].set(pick_weights.reshape(-1))
    )
    got_rows = lax.all_to_all(
        grad_rows.reshape(owners, capacity, width), mem, split_axis=0, concat_axis=0, tiled=True
    )
    got_wts = lax.all_to_all(
        grad_wts.reshape(owners, capacity), mem, split_axis=0, concat_axis=0, tiled=True
    )
    picked = returned.reshape(owners * capacity, width)[slot_ids].reshape(
        tok_count, per_token, width
    )
    mixing = jnp.where(
        proj_ids[..., None] == jnp.arange(proj_count, dtype=jnp.int32),
        pick_weights[..., None],
        jnp.zeros((), jnp.bfloat16),
    )
    proj_sums = jnp.einsum(
        "tjp,tjd->tpd", mixing, picked, preferred_element_type=jnp.float32
    ).astype(jnp.bfloat16)
    layer_out = jnp.dot(
        proj_sums.reshape(tok_count, proj_count * width),
        flat_proj,
        preferred_element_type=jnp.float32,
    ).astype(jnp.bfloat16)
    weighted = got_wts.astype(jnp.float32)[..., None] * got_rows.astype(jnp.float32)
    slab_grad = (
        jnp.zeros((rows_dev, width), jnp.float32)
        .at[received.reshape(-1)]
        .add(weighted.reshape(-1, width))
    )
    quarter = first_moment.shape[0]
    start = lax.axis_index("x") * quarter
    share = lax.psum_scatter(slab_grad, "x", scatter_dimension=0, tiled=True)
    old_rows = lax.dynamic_slice_in_dim(values, start, quarter, 0)
    new_first, new_second, new_part = adam_rows(old_rows, share, first_moment, second_moment)
    new_values = lax.all_gather(new_part, "x", axis=0, tiled=True)
    return (layer_out, new_values, new_first, new_second)


def call(kernel, out_shape, grid=None, in_specs=None, out_specs=None, scratch=(), cost=None):
    extra = {} if grid is None else {"grid": grid}
    if in_specs is not None:
        extra["in_specs"] = in_specs
    if out_specs is not None:
        extra["out_specs"] = out_specs
    return pl.pallas_call(
        kernel,
        out_shape=out_shape,
        scratch_shapes=list(scratch),
        compiler_params=pltpu.CompilerParams(vmem_limit_bytes=VMEM),
        cost_estimate=cost,
        **extra,
    )


def cost(flops, nbytes):
    return pl.CostEstimate(flops=flops, bytes_accessed=nbytes, transcendentals=0)


def rank_kernel(cells, block, cell_ref, trow_ref, rank_ref, req_ref):
    count = cell_ref.shape[1]
    below = lax.broadcasted_iota(jnp.int32, (block, block), 0) < lax.broadcasted_iota(
        jnp.int32, (block, block), 1
    )
    below = below.astype(F32).astype(BF)
    carry = jnp.zeros((cells, 1), F32)
    asked = jnp.zeros((3 * cells, LANES), F32)
    for b in range(count // block):
        span = pl.ds(b * block, block)
        cell = cell_ref[:, span]
        trow = trow_ref[:, span]
        here = (lax.broadcasted_iota(jnp.int32, (cells, block), 0) == cell).astype(F32)
        before = jnp.dot(here.astype(BF), below, preferred_element_type=F32) + carry
        carry = carry + jnp.sum(here, axis=1, keepdims=True)
        rank = jnp.sum(here * before, axis=0, keepdims=True).astype(jnp.int32)
        rank_ref[:, span] = rank
        place = (lax.broadcasted_iota(jnp.int32, (LANES, block), 0) == rank).astype(F32)
        high = (trow >> 5).astype(F32)
        low = (trow & 31).astype(F32)
        told = jnp.concatenate([here, here * high, here * low], axis=0)
        asked = asked + lax.dot_general(
            told.astype(BF), place.astype(BF), NT, preferred_element_type=F32
        )
    there = asked[:cells]
    rows = (asked[cells : 2 * cells] * 32.0 + asked[2 * cells :]).astype(jnp.int32)
    rows = jnp.where(there > 0.5, rows, -1)
    lane = lax.broadcasted_iota(jnp.int32, (cells, LANES), 1)
    over = (jnp.max(carry) > CAP).astype(jnp.int32)
    req_ref[...] = jnp.where(lane == LANES - 1, over, rows)


def send_kernel(
    cells, tok, tg_ref, proj_ref, pcol_ref, cell_ref, rank_ref, wt_ref, out_ref, chosen, place
):
    step = pl.program_id(0)
    per_token = pcol_ref.shape[1]
    back = lax.dot_general(tg_ref[...], proj_ref[0], NT, preferred_element_type=F32)
    back = back.astype(BF)
    for j in range(per_token):
        mine = pcol_ref[:, j : j + 1] == step
        span = pl.ds(j * tok, tok)

        @pl.when(step == 0)
        def _():
            chosen[span, :] = back

        @pl.when(step > 0)
        def _():
            chosen[span, :] = jnp.where(mine, back, chosen[span, :])

    @pl.when(step == pl.num_programs(0) - 1)
    def _():
        count = cell_ref.shape[1]
        at = lax.broadcasted_iota(jnp.int32, (CAP, count), 0) == rank_ref[...]
        place[...] = jnp.where(at, wt_ref[...].astype(F32), 0.0).astype(BF)
        group = 4
        for g in range(cells // group):
            parts = []
            for d in range(g * group, (g + 1) * group):
                here = (cell_ref[...] == d).astype(F32).astype(BF)
                parts.append(place[...] * here)
            pick = jnp.concatenate(parts, axis=0)
            out_ref[pl.ds(g * group * CAP, group * CAP), :] = jnp.dot(
                pick, chosen[...], preferred_element_type=F32
            ).astype(BF)


def look_kernel(ids_ref, table_ref, out_ref):
    rows = ids_ref.shape[0]
    total = table_ref.shape[0]
    pick = lax.broadcasted_iota(jnp.int32, (rows, total), 1) == ids_ref[...]
    out_ref[...] = jnp.dot(
        pick.astype(F32).astype(BF), table_ref[...], preferred_element_type=F32
    ).astype(BF)


def sum_kernel(ids_ref, flags_ref, z_ref, got_ref, *out_refs):
    depth = len(out_refs)
    rows = out_refs[0].shape[0] - FLAG_ROWS
    slots = ids_ref.shape[1]
    over = jnp.max(flags_ref[...]).astype(F32)
    for k, out_ref in enumerate(out_refs):
        base = lax.rem(z_ref[0] + k, depth) * rows
        pick = lax.broadcasted_iota(jnp.int32, (rows, slots), 0) == ids_ref[...] - base
        out_ref[:rows, :] = jnp.dot(
            pick.astype(F32).astype(BF), got_ref[...], preferred_element_type=F32
        ).astype(out_ref.dtype)
        out_ref[rows:, :] = jnp.full((FLAG_ROWS, out_ref.shape[1]), over, F32).astype(
            out_ref.dtype
        )


def out_kernel(slot_ref, pcol_ref, wcol_ref, ret_ref, proj_ref, out_ref, picked, total):
    step = pl.program_id(0)
    tok, per_token = slot_ref.shape
    slots = ret_ref.shape[0]

    @pl.when(step == 0)
    def _():
        lane = lax.broadcasted_iota(jnp.int32, (tok, slots), 1)
        for j in range(per_token):
            pick = (lane == slot_ref[:, j : j + 1]).astype(F32).astype(BF)
            row = jnp.dot(pick, ret_ref[...], preferred_element_type=F32)
            picked[j] = row * wcol_ref[:, j : j + 1]

    sums = jnp.zeros(picked.shape[1:], F32)
    for j in range(per_token):
        sums = sums + jnp.where(pcol_ref[:, j : j + 1] == step, picked[j], 0.0)
    part = jnp.dot(sums.astype(BF), proj_ref[0], preferred_element_type=F32)

    @pl.when(step == 0)
    def _():
        total[...] = part

    @pl.when(step > 0)
    def _():
        total[...] += part

    @pl.when(step == pl.num_programs(0) - 1)
    def _():
        out_ref[...] = total[...].astype(BF)


def short_way(picks, pick_weights, token_grads, values, first_moment, second_moment, projectors):
    plane = ("y", "c", "x")
    cells = lax.axis_size(plane)
    depth = lax.axis_size("z")
    parts = lax.axis_size("x")
    rows_dev, width = values.shape
    quarter = rows_dev // parts
    tok, per_token = picks.shape
    proj_count, _, out_width = projectors.shape
    total = tok * per_token
    slots = cells * CAP
    table_rows = depth * quarter
    start = lax.axis_index("x") * quarter
    old_rows = lax.dynamic_slice_in_dim(values, start, quarter, 0)
    table = lax.all_gather(old_rows, "z", axis=0, tiled=True)

    by_pick = picks.T.reshape(1, total)
    owner = by_pick // rows_dev
    row = by_pick % rows_dev
    owner_y = owner // (depth * CORES)
    owner_z = (owner // CORES) % depth
    cell = (owner_y * CORES + owner % CORES) * parts + row // quarter
    trow = owner_z * quarter + row % quarter
    block = 256
    rank, requests = call(
        functools.partial(rank_kernel, cells, block),
        (
            jax.ShapeDtypeStruct((1, total), jnp.int32),
            jax.ShapeDtypeStruct((cells, LANES), jnp.int32),
        ),
        cost=cost(2 * total * cells * 400, 20000),
    )(cell, trow)
    received = lax.all_to_all(requests, plane, split_axis=0, concat_axis=0, tiled=True)

    pcol = picks % proj_count
    wt_row = pick_weights.T.reshape(1, total)
    whole = lambda shape: pl.BlockSpec(shape, lambda i: (0,) * len(shape))
    sent = call(
        functools.partial(send_kernel, cells, tok),
        jax.ShapeDtypeStruct((slots, width), BF),
        grid=(proj_count,),
        in_specs=[
            whole((tok, out_width)),
            pl.BlockSpec((1, width, out_width), lambda i: (i, 0, 0)),
            whole((tok, per_token)),
            whole((1, total)),
            whole((1, total)),
            whole((1, total)),
        ],
        out_specs=whole((slots, width)),
        scratch=[pltpu.VMEM((total, width), BF), pltpu.VMEM((CAP, total), BF)],
        cost=cost(2 * width * (tok * proj_count * out_width + slots * total), 12000000),
    )(token_grads, projectors, pcol, cell, rank, wt_row)
    got = lax.all_to_all(
        sent.reshape(cells, CAP, width), plane, split_axis=0, concat_axis=0, tiled=True
    ).reshape(slots, width)

    asked = received[:, :CAP]
    flags = received[:, LANES - 1 :]
    vmem = pl.BlockSpec(memory_space=pltpu.VMEM)
    chunk = slots // 8
    looked = call(
        look_kernel,
        jax.ShapeDtypeStruct((slots, width), BF),
        grid=(8,),
        in_specs=[
            pl.BlockSpec((chunk, 1), lambda i: (i, 0)),
            whole((table_rows, width)),
        ],
        out_specs=pl.BlockSpec((chunk, width), lambda i: (i, 0)),
        cost=cost(2 * width * slots * table_rows, 4000000),
    )(asked.reshape(slots, 1), table)
    got, looked = lax.optimization_barrier((got, looked))
    returned = lax.all_to_all(
        looked.reshape(cells, CAP, width), plane, split_axis=0, concat_axis=0, tiled=True
    ).reshape(slots, width)

    z_here = lax.axis_index("z").reshape(1)
    sums = call(
        sum_kernel,
        (jax.ShapeDtypeStruct((quarter + FLAG_ROWS, width), BF),) * depth,
        in_specs=[vmem, vmem, pl.BlockSpec(memory_space=pltpu.SMEM), vmem],
        out_specs=(vmem,) * depth,
        cost=cost(2 * width * slots * table_rows, 4000000),
    )(asked.reshape(1, slots), flags, z_here, got)
    shares = [sums[0]] + [
        lax.ppermute(sums[k], "z", [(i, (i + k) % depth) for i in range(depth)])
        for k in range(1, depth)
    ]
    share = functools.reduce(lambda p, q: p + q, [s.astype(F32) for s in shares])
    flag = share[quarter, 0]
    new_first, new_second, new_part = adam_rows(
        old_rows, share[:quarter], first_moment, second_moment
    )
    x_here = lax.axis_index("x")
    new_values = jnp.zeros((parts, quarter, width), BF)
    for k in range(parts):
        piece = new_part
        if k:
            piece = lax.ppermute(new_part, "x", [(i, (i + k) % parts) for i in range(parts)])
        mine = jnp.arange(parts) == (x_here - k) % parts
        new_values = jnp.where(mine[:, None, None], piece[None], new_values)
    new_values = new_values.reshape(rows_dev, width)

    slot_col = (cell * CAP + rank).reshape(per_token, tok).T
    layer_out = call(
        out_kernel,
        jax.ShapeDtypeStruct((tok, out_width), BF),
        grid=(proj_count,),
        in_specs=[
            whole((tok, per_token)),
            whole((tok, per_token)),
            whole((tok, per_token)),
            whole((slots, width)),
            pl.BlockSpec((1, width, out_width), lambda i: (i, 0, 0)),
        ],
        out_specs=whole((tok, out_width)),
        scratch=[
            pltpu.VMEM((per_token, tok, width), F32),
            pltpu.VMEM((tok, out_width), F32),
        ],
        cost=cost(2 * width * (tok * proj_count * out_width + slots * total), 13000000),
    )(slot_col, pcol, pick_weights.astype(F32), returned, projectors)
    return flag, (layer_out, new_values, new_first, new_second)


def on_device(*args):
    flag, outs = short_way(*args)
    return lax.cond(flag > 0.5, lambda given, done: long_way(*given), lambda given, done: done, args, outs)


def solution(mesh):
    mem, dp = mesh.devices.shape
    grid = Mesh(
        mesh.devices.reshape(mem // (Z_CHIPS * CORES), Z_CHIPS, CORES, dp), ("y", "z", "c", "x")
    )
    every = P(("y", "z", "c", "x"), None)
    slab = P(("y", "z", "c"), None)
    return jax.shard_map(
        on_device,
        mesh=grid,
        in_specs=(every, every, every, slab, every, every, P()),
        out_specs=(every, slab, every, every),
        check_vma=False,
    )
```

```python
import functools

import jax
import jax.numpy as jnp
from jax import lax
from jax.experimental import pallas as pl
from jax.experimental.pallas import tpu as pltpu
from jax.sharding import Mesh
from jax.sharding import PartitionSpec as P

beta_one = 0.9
beta_two = 0.999
corr_one = 1.0 - 0.9**50
corr_two = 1.0 - 0.999**50
learn_rate = 0.05
adam_eps = 1e-08

Z_CHIPS = 8
CORES = 2
CAP = 80
LANES = 128
OVER = 1e30
BF = jnp.bfloat16
F32 = jnp.float32
NT = (((1,), (1,)), ((), ()))


def adam_rows(old_rows, slab_grad, first_moment, second_moment):
    new_first = beta_one * first_moment + (1.0 - beta_one) * slab_grad
    new_second = beta_two * second_moment + (1.0 - beta_two) * slab_grad * slab_grad
    update_step = new_first / corr_one / (jnp.sqrt(new_second / corr_two) + adam_eps)
    updated = (old_rows.astype(jnp.float32) - learn_rate * update_step).astype(jnp.bfloat16)
    return (new_first, new_second, updated)


def long_way(picks, pick_weights, token_grads, values, first_moment, second_moment, projectors):
    mem = ("y", "z", "c")
    owners = lax.axis_size(mem)
    rows_dev = values.shape[0]
    width = values.shape[1]
    tok_count, per_token = picks.shape
    proj_count = projectors.shape[0]
    out_width = projectors.shape[2]
    total_picks = tok_count * per_token
    capacity = 2 * total_picks // owners
    flat_picks = picks.reshape(-1)
    owner_ids = flat_picks // rows_dev
    local_rows = flat_picks - owner_ids * rows_dev
    member = (owner_ids[:, None] == jnp.arange(owners, dtype=jnp.int32)[None, :]).astype(jnp.int32)
    before = jnp.cumsum(member, axis=0) - member
    slot_ids = owner_ids * capacity + jnp.sum(before * member, axis=1)
    proj_ids = picks % proj_count
    flat_proj = projectors.reshape(proj_count * width, out_width)
    requests = jnp.zeros((owners * capacity,), jnp.int32).at[slot_ids].set(local_rows)
    requests = requests.reshape(owners, capacity)
    received = lax.all_to_all(requests, mem, split_axis=0, concat_axis=0, tiled=True)
    looked = values[received]
    returned = lax.all_to_all(looked, mem, split_axis=0, concat_axis=0, tiled=True)
    back_grads = lax.dot_general(token_grads, flat_proj, NT, preferred_element_type=jnp.float32)
    back_grads = back_grads.astype(jnp.bfloat16).reshape(tok_count, proj_count, width)
    chosen = back_grads[jnp.arange(tok_count, dtype=jnp.int32)[:, None], proj_ids].reshape(
        total_picks, width
    )
    grad_rows = jnp.zeros((owners * capacity, width), jnp.bfloat16).at[slot_ids].set(chosen)
    grad_wts = (
        jnp.zeros((owners * capacity,), jnp.bfloat16).at[slot_ids].set(pick_weights.reshape(-1))
    )
    got_rows = lax.all_to_all(
        grad_rows.reshape(owners, capacity, width), mem, split_axis=0, concat_axis=0, tiled=True
    )
    got_wts = lax.all_to_all(
        grad_wts.reshape(owners, capacity), mem, split_axis=0, concat_axis=0, tiled=True
    )
    picked = returned.reshape(owners * capacity, width)[slot_ids].reshape(
        tok_count, per_token, width
    )
    mixing = jnp.where(
        proj_ids[..., None] == jnp.arange(proj_count, dtype=jnp.int32),
        pick_weights[..., None],
        jnp.zeros((), jnp.bfloat16),
    )
    proj_sums = jnp.einsum(
        "tjp,tjd->tpd", mixing, picked, preferred_element_type=jnp.float32
    ).astype(jnp.bfloat16)
    layer_out = jnp.dot(
        proj_sums.reshape(tok_count, proj_count * width),
        flat_proj,
        preferred_element_type=jnp.float32,
    ).astype(jnp.bfloat16)
    weighted = got_wts.astype(jnp.float32)[..., None] * got_rows.astype(jnp.float32)
    slab_grad = (
        jnp.zeros((rows_dev, width), jnp.float32)
        .at[received.reshape(-1)]
        .add(weighted.reshape(-1, width))
    )
    quarter = first_moment.shape[0]
    start = lax.axis_index("x") * quarter
    share = jnp.sum(
        lax.all_to_all(
            slab_grad.reshape(-1, quarter, width), "x", split_axis=0, concat_axis=0, tiled=True
        ),
        axis=0,
    )
    old_rows = lax.dynamic_slice_in_dim(values, start, quarter, 0)
    new_first, new_second, new_part = adam_rows(old_rows, share, first_moment, second_moment)
    new_values = lax.all_gather(new_part, "x", axis=0, tiled=True)
    return (layer_out, new_values, new_first, new_second)


def call(kernel, out_shape, vmem, grid=None, in_specs=None, out_specs=None, scratch=(), cost=None):
    extra = {} if grid is None else {"grid": grid}
    if in_specs is not None:
        extra["in_specs"] = in_specs
    if out_specs is not None:
        extra["out_specs"] = out_specs
    return pl.pallas_call(
        kernel,
        out_shape=out_shape,
        scratch_shapes=list(scratch),
        compiler_params=pltpu.CompilerParams(vmem_limit_bytes=vmem * 1024 * 1024),
        cost_estimate=cost,
        **extra,
    )


def cost(flops, nbytes):
    return pl.CostEstimate(flops=flops, bytes_accessed=nbytes, transcendentals=0)


def rank_kernel(cells, block, cell_ref, trow_ref, rank_ref, req_ref):
    count = cell_ref.shape[1]
    below = lax.broadcasted_iota(jnp.int32, (block, block), 0) < lax.broadcasted_iota(
        jnp.int32, (block, block), 1
    )
    below = below.astype(F32).astype(BF)
    carry = jnp.zeros((cells, 1), F32)
    asked = jnp.zeros((3 * cells, LANES), F32)
    for b in range(count // block):
        span = pl.ds(b * block, block)
        cell = cell_ref[:, span]
        trow = trow_ref[:, span]
        here = (lax.broadcasted_iota(jnp.int32, (cells, block), 0) == cell).astype(F32)
        before = jnp.dot(here.astype(BF), below, preferred_element_type=F32) + carry
        carry = carry + jnp.sum(here, axis=1, keepdims=True)
        rank = jnp.sum(here * before, axis=0, keepdims=True).astype(jnp.int32)
        rank_ref[:, span] = rank
        place = (lax.broadcasted_iota(jnp.int32, (LANES, block), 0) == rank).astype(F32)
        high = (trow >> 5).astype(F32)
        low = (trow & 31).astype(F32)
        told = jnp.concatenate([here, here * high, here * low], axis=0)
        asked = asked + lax.dot_general(
            told.astype(BF), place.astype(BF), NT, preferred_element_type=F32
        )
    there = asked[:cells]
    rows = (asked[cells : 2 * cells] * 32.0 + asked[2 * cells :]).astype(jnp.int32)
    rows = jnp.where(there > 0.5, rows, -1)
    lane = lax.broadcasted_iota(jnp.int32, (cells, LANES), 1)
    over = (jnp.max(carry) > CAP).astype(jnp.int32)
    req_ref[...] = jnp.where(lane == LANES - 1, over, rows)


def send_kernel(
    group, projs, tg_ref, proj_ref, pcol_ref, cell_ref, rank_ref, wt_ref, out_ref, chosen, place
):
    step = pl.program_id(0)
    tok, per_token = pcol_ref.shape

    @pl.when(step == 0)
    def _():
        count = cell_ref.shape[1]
        at = lax.broadcasted_iota(jnp.int32, (CAP, count), 0) == rank_ref[...]
        place[...] = jnp.where(at, wt_ref[...].astype(F32), 0.0).astype(BF)

    @pl.when(step < projs)
    def _():
        back = lax.dot_general(tg_ref[...], proj_ref[0], NT, preferred_element_type=F32)
        back = back.astype(BF)
        for j in range(per_token):
            mine = (pcol_ref[:, j : j + 1] == step) | (step == 0)
            span = pl.ds(j * tok, tok)
            chosen[span, :] = jnp.where(mine, back, chosen[span, :])

    @pl.when(step >= projs)
    def _():
        first = (step - projs) * group
        parts = []
        for d in range(group):
            here = (cell_ref[...] == first + d).astype(F32).astype(BF)
            parts.append(place[...] * here)
        pick = jnp.concatenate(parts, axis=0)
        out_ref[...] = jnp.dot(pick, chosen[...], preferred_element_type=F32).astype(BF)


def look_kernel(ids_ref, *refs):
    *pieces, out_ref, table = refs
    rows = pieces[0].shape[0]

    @pl.when(pl.program_id(0) == 0)
    def _():
        for k, piece in enumerate(pieces):
            table[pl.ds(k * rows, rows), :] = piece[...]

    pick = lax.broadcasted_iota(jnp.int32, (ids_ref.shape[0], table.shape[0]), 1) == ids_ref[...]
    out_ref[...] = jnp.dot(
        pick.astype(F32).astype(BF), table[...], preferred_element_type=F32
    ).astype(BF)


def sum_kernel(ids_ref, flags_ref, got_ref, *out_refs):
    rows = out_refs[0].shape[0]
    slots = ids_ref.shape[1]
    over = jnp.where(jnp.max(flags_ref[...]) > 0, OVER, 0.0)
    for k, out_ref in enumerate(out_refs):
        pick = lax.broadcasted_iota(jnp.int32, (rows, slots), 0) == ids_ref[...] - k * rows
        part = jnp.dot(pick.astype(F32).astype(BF), got_ref[...], preferred_element_type=F32)
        out_ref[...] = (part + over).astype(out_ref.dtype)


def out_kernel(slot_ref, pcol_ref, wcol_ref, ret_ref, proj_ref, out_ref, picked, total):
    step = pl.program_id(0)
    tok, per_token = slot_ref.shape
    slots = ret_ref.shape[0]

    @pl.when(step == 0)
    def _():
        lane = lax.broadcasted_iota(jnp.int32, (tok, slots), 1)
        for j in range(per_token):
            pick = (lane == slot_ref[:, j : j + 1]).astype(F32).astype(BF)
            row = jnp.dot(pick, ret_ref[...], preferred_element_type=F32)
            picked[j] = row * wcol_ref[:, j : j + 1]

    sums = jnp.zeros(picked.shape[1:], F32)
    for j in range(per_token):
        sums = sums + jnp.where(pcol_ref[:, j : j + 1] == step, picked[j], 0.0)
    part = jnp.dot(sums.astype(BF), proj_ref[0], preferred_element_type=F32)

    @pl.when(step == 0)
    def _():
        total[...] = part

    @pl.when(step > 0)
    def _():
        total[...] += part

    @pl.when(step == pl.num_programs(0) - 1)
    def _():
        out_ref[...] = total[...].astype(BF)


def short_way(picks, pick_weights, token_grads, values, first_moment, second_moment, projectors):
    plane = ("y", "c", "x")
    cells = lax.axis_size(plane)
    depth = lax.axis_size("z")
    parts = lax.axis_size("x")
    rows_dev, width = values.shape
    quarter = rows_dev // parts
    tok, per_token = picks.shape
    proj_count, _, out_width = projectors.shape
    total = tok * per_token
    slots = cells * CAP
    table_rows = depth * quarter
    start = lax.axis_index("x") * quarter
    old_rows = lax.dynamic_slice_in_dim(values, start, quarter, 0)

    by_pick = picks.T.reshape(1, total)
    owner = lax.div(by_pick, rows_dev)
    row = lax.rem(by_pick, rows_dev)
    owner_y = lax.div(owner, depth * CORES)
    owner_z = lax.rem(lax.div(owner, CORES), depth)
    cell = (owner_y * CORES + lax.rem(owner, CORES)) * parts + lax.div(row, quarter)
    trow = owner_z * quarter + lax.rem(row, quarter)
    block = 256
    rank, requests = call(
        functools.partial(rank_kernel, cells, block),
        (
            jax.ShapeDtypeStruct((1, total), jnp.int32),
            jax.ShapeDtypeStruct((cells, LANES), jnp.int32),
        ),
        8,
        cost=cost(2 * total * cells * 400, 20000),
    )(cell, trow)
    received = lax.all_to_all(requests, plane, split_axis=0, concat_axis=0, tiled=True)

    pcol = lax.rem(picks, proj_count)
    wt_row = pick_weights.T.reshape(1, total)
    whole = lambda shape: pl.BlockSpec(shape, lambda i: (0,) * len(shape))
    group = 4
    sent = call(
        functools.partial(send_kernel, group, proj_count),
        jax.ShapeDtypeStruct((slots, width), BF),
        24,
        grid=(proj_count + cells // group,),
        in_specs=[
            whole((tok, out_width)),
            pl.BlockSpec(
                (1, width, out_width), lambda i: (jnp.minimum(i, proj_count - 1), 0, 0)
            ),
            whole((tok, per_token)),
            whole((1, total)),
            whole((1, total)),
            whole((1, total)),
        ],
        out_specs=pl.BlockSpec(
            (group * CAP, width), lambda i: (jnp.maximum(i - proj_count, 0), 0)
        ),
        scratch=[pltpu.VMEM((total, width), BF), pltpu.VMEM((CAP, total), BF)],
        cost=cost(2 * width * (tok * proj_count * out_width + slots * total), 12000000),
    )(token_grads, projectors, pcol, cell, rank, wt_row)
    got = lax.all_to_all(
        sent.reshape(cells, CAP, width), plane, split_axis=0, concat_axis=0, tiled=True
    ).reshape(slots, width)

    pieces = [old_rows] + [
        lax.ppermute(old_rows, "z", [(i, (i - k) % depth) for i in range(depth)])
        for k in range(1, depth)
    ]
    z_here = lax.axis_index("z")
    told = received[:, :CAP]
    from_z = lax.rem(lax.div(told, quarter) + depth - z_here, depth)
    asked = jnp.where(told < 0, -1, from_z * quarter + lax.rem(told, quarter))
    flags = received[:, LANES - 1 :]
    vmem = pl.BlockSpec(memory_space=pltpu.VMEM)
    chunk = slots // 8
    looked = call(
        look_kernel,
        jax.ShapeDtypeStruct((slots, width), BF),
        16,
        grid=(8,),
        in_specs=[pl.BlockSpec((chunk, 1), lambda i: (i, 0))] + [whole((quarter, width))] * depth,
        out_specs=pl.BlockSpec((chunk, width), lambda i: (i, 0)),
        scratch=[pltpu.VMEM((table_rows, width), BF)],
        cost=cost(2 * width * slots * table_rows, 4000000),
    )(asked.reshape(slots, 1), *pieces)
    got, looked = lax.optimization_barrier((got, looked))
    returned = lax.all_to_all(
        looked.reshape(cells, CAP, width), plane, split_axis=0, concat_axis=0, tiled=True
    ).reshape(slots, width)

    sums = call(
        sum_kernel,
        (jax.ShapeDtypeStruct((quarter, width), BF),) * depth,
        16,
        in_specs=[vmem] * 3,
        out_specs=(vmem,) * depth,
        cost=cost(2 * width * slots * table_rows, 4000000),
    )(asked.reshape(1, slots), flags, got)
    shares = [sums[0]] + [
        lax.ppermute(sums[k], "z", [(i, (i + k) % depth) for i in range(depth)])
        for k in range(1, depth)
    ]
    share = functools.reduce(lambda p, q: p + q, [s.astype(F32) for s in shares])
    flag = share[0, 0] > 0.5 * OVER
    new_first, new_second, new_part = adam_rows(old_rows, share, first_moment, second_moment)
    x_here = lax.axis_index("x")
    new_values = jnp.zeros((parts, quarter, width), BF)
    for k in range(parts):
        piece = new_part
        if k:
            piece = lax.ppermute(new_part, "x", [(i, (i + k) % parts) for i in range(parts)])
        mine = jnp.arange(parts) == (x_here - k) % parts
        new_values = jnp.where(mine[:, None, None], piece[None], new_values)
    new_values = new_values.reshape(rows_dev, width)

    slot_col = (cell * CAP + rank).reshape(per_token, tok).T
    layer_out = call(
        out_kernel,
        jax.ShapeDtypeStruct((tok, out_width), BF),
        32,
        grid=(proj_count,),
        in_specs=[
            whole((tok, per_token)),
            whole((tok, per_token)),
            whole((tok, per_token)),
            whole((slots, width)),
            pl.BlockSpec((1, width, out_width), lambda i: (i, 0, 0)),
        ],
        out_specs=whole((tok, out_width)),
        scratch=[
            pltpu.VMEM((per_token, tok, width), F32),
            pltpu.VMEM((tok, out_width), F32),
        ],
        cost=cost(2 * width * (tok * proj_count * out_width + slots * total), 13000000),
    )(slot_col, pcol, pick_weights.astype(F32), returned, projectors)
    return flag, (layer_out, new_values, new_first, new_second)


def on_device(*args):
    flag, outs = short_way(*args)
    return lax.cond(flag, lambda given, done: long_way(*given), lambda given, done: done, args, outs)


def solution(mesh):
    mem, dp = mesh.devices.shape
    grid = Mesh(
        mesh.devices.reshape(mem // (Z_CHIPS * CORES), Z_CHIPS, CORES, dp), ("y", "z", "c", "x")
    )
    every = P(("y", "z", "c", "x"), None)
    slab = P(("y", "z", "c"), None)
    return jax.shard_map(
        on_device,
        mesh=grid,
        in_specs=(every, every, every, slab, every, every, P()),
        out_specs=(every, slab, every, every),
        check_vma=False,
    )
```

```python
import functools

import jax
import jax.numpy as jnp
from jax import lax
from jax.experimental import pallas as pl
from jax.experimental.pallas import tpu as pltpu
from jax.sharding import Mesh
from jax.sharding import PartitionSpec as P

beta_one = 0.9
beta_two = 0.999
corr_one = 1.0 - 0.9**50
corr_two = 1.0 - 0.999**50
learn_rate = 0.05
adam_eps = 1e-08

Z_CHIPS = 8
CORES = 2
CAP = 72
LANES = 128
OVER = 1e30
BF = jnp.bfloat16
F32 = jnp.float32
NT = (((1,), (1,)), ((), ()))


def adam_rows(old_rows, slab_grad, first_moment, second_moment):
    new_first = beta_one * first_moment + (1.0 - beta_one) * slab_grad
    new_second = beta_two * second_moment + (1.0 - beta_two) * slab_grad * slab_grad
    update_step = new_first / corr_one / (jnp.sqrt(new_second / corr_two) + adam_eps)
    updated = (old_rows.astype(jnp.float32) - learn_rate * update_step).astype(jnp.bfloat16)
    return (new_first, new_second, updated)


def long_way(picks, pick_weights, token_grads, values, first_moment, second_moment, projectors):
    mem = ("y", "z", "c")
    owners = lax.axis_size(mem)
    rows_dev = values.shape[0]
    width = values.shape[1]
    tok_count, per_token = picks.shape
    proj_count = projectors.shape[0]
    out_width = projectors.shape[2]
    total_picks = tok_count * per_token
    capacity = 2 * total_picks // owners
    flat_picks = picks.reshape(-1)
    owner_ids = flat_picks // rows_dev
    local_rows = flat_picks - owner_ids * rows_dev
    member = (owner_ids[:, None] == jnp.arange(owners, dtype=jnp.int32)[None, :]).astype(jnp.int32)
    before = jnp.cumsum(member, axis=0) - member
    slot_ids = owner_ids * capacity + jnp.sum(before * member, axis=1)
    proj_ids = picks % proj_count
    flat_proj = projectors.reshape(proj_count * width, out_width)
    requests = jnp.zeros((owners * capacity,), jnp.int32).at[slot_ids].set(local_rows)
    requests = requests.reshape(owners, capacity)
    received = lax.all_to_all(requests, mem, split_axis=0, concat_axis=0, tiled=True)
    looked = values[received]
    returned = lax.all_to_all(looked, mem, split_axis=0, concat_axis=0, tiled=True)
    back_grads = lax.dot_general(token_grads, flat_proj, NT, preferred_element_type=jnp.float32)
    back_grads = back_grads.astype(jnp.bfloat16).reshape(tok_count, proj_count, width)
    chosen = back_grads[jnp.arange(tok_count, dtype=jnp.int32)[:, None], proj_ids].reshape(
        total_picks, width
    )
    grad_rows = jnp.zeros((owners * capacity, width), jnp.bfloat16).at[slot_ids].set(chosen)
    grad_wts = (
        jnp.zeros((owners * capacity,), jnp.bfloat16).at[slot_ids].set(pick_weights.reshape(-1))
    )
    got_rows = lax.all_to_all(
        grad_rows.reshape(owners, capacity, width), mem, split_axis=0, concat_axis=0, tiled=True
    )
    got_wts = lax.all_to_all(
        grad_wts.reshape(owners, capacity), mem, split_axis=0, concat_axis=0, tiled=True
    )
    picked = returned.reshape(owners * capacity, width)[slot_ids].reshape(
        tok_count, per_token, width
    )
    mixing = jnp.where(
        proj_ids[..., None] == jnp.arange(proj_count, dtype=jnp.int32),
        pick_weights[..., None],
        jnp.zeros((), jnp.bfloat16),
    )
    proj_sums = jnp.einsum(
        "tjp,tjd->tpd", mixing, picked, preferred_element_type=jnp.float32
    ).astype(jnp.bfloat16)
    layer_out = jnp.dot(
        proj_sums.reshape(tok_count, proj_count * width),
        flat_proj,
        preferred_element_type=jnp.float32,
    ).astype(jnp.bfloat16)
    weighted = got_wts.astype(jnp.float32)[..., None] * got_rows.astype(jnp.float32)
    slab_grad = (
        jnp.zeros((rows_dev, width), jnp.float32)
        .at[received.reshape(-1)]
        .add(weighted.reshape(-1, width))
    )
    quarter = first_moment.shape[0]
    start = lax.axis_index("x") * quarter
    share = jnp.sum(
        lax.all_to_all(
            slab_grad.reshape(-1, quarter, width), "x", split_axis=0, concat_axis=0, tiled=True
        ),
        axis=0,
    )
    old_rows = lax.dynamic_slice_in_dim(values, start, quarter, 0)
    new_first, new_second, new_part = adam_rows(old_rows, share, first_moment, second_moment)
    new_values = lax.all_gather(new_part, "x", axis=0, tiled=True)
    return (layer_out, new_values, new_first, new_second)


def call(kernel, out_shape, vmem, grid=None, in_specs=None, out_specs=None, scratch=(), cost=None):
    extra = {} if grid is None else {"grid": grid}
    if in_specs is not None:
        extra["in_specs"] = in_specs
    if out_specs is not None:
        extra["out_specs"] = out_specs
    return pl.pallas_call(
        kernel,
        out_shape=out_shape,
        scratch_shapes=list(scratch),
        compiler_params=pltpu.CompilerParams(vmem_limit_bytes=vmem * 1024 * 1024),
        cost_estimate=cost,
        **extra,
    )


def cost(flops, nbytes):
    return pl.CostEstimate(flops=flops, bytes_accessed=nbytes, transcendentals=0)


def rank_kernel(cells, block, cell_ref, trow_ref, rank_ref, req_ref):
    count = cell_ref.shape[1]
    below = lax.broadcasted_iota(jnp.int32, (block, block), 0) < lax.broadcasted_iota(
        jnp.int32, (block, block), 1
    )
    below = below.astype(F32).astype(BF)
    carry = jnp.zeros((cells, 1), F32)
    asked = jnp.zeros((3 * cells, LANES), F32)
    for b in range(count // block):
        span = pl.ds(b * block, block)
        cell = cell_ref[:, span]
        trow = trow_ref[:, span]
        here = (lax.broadcasted_iota(jnp.int32, (cells, block), 0) == cell).astype(F32)
        before = jnp.dot(here.astype(BF), below, preferred_element_type=F32) + carry
        carry = carry + jnp.sum(here, axis=1, keepdims=True)
        rank = jnp.sum(here * before, axis=0, keepdims=True).astype(jnp.int32)
        rank_ref[:, span] = rank
        place = (lax.broadcasted_iota(jnp.int32, (LANES, block), 0) == rank).astype(F32)
        high = (trow >> 5).astype(F32)
        low = (trow & 31).astype(F32)
        told = jnp.concatenate([here, here * high, here * low], axis=0)
        asked = asked + lax.dot_general(
            told.astype(BF), place.astype(BF), NT, preferred_element_type=F32
        )
    there = asked[:cells]
    rows = (asked[cells : 2 * cells] * 32.0 + asked[2 * cells :]).astype(jnp.int32)
    rows = jnp.where(there > 0.5, rows, -1)
    lane = lax.broadcasted_iota(jnp.int32, (cells, LANES), 1)
    over = (jnp.max(carry) > CAP).astype(jnp.int32)
    req_ref[...] = jnp.where(lane == LANES - 1, over, rows)


def send_kernel(
    group, tg_ref, proj_ref, pcol_ref, cell_ref, rank_ref, wt_ref, out_ref, chosen, made, sems
):
    tok, per_token = pcol_ref.shape
    count = cell_ref.shape[1]
    for p in range(proj_ref.shape[0]):
        back = lax.dot_general(tg_ref[...], proj_ref[p], NT, preferred_element_type=F32)
        back = back.astype(BF)
        for j in range(per_token):
            span = pl.ds(j * tok, tok)
            if p == 0:
                chosen[span, :] = back
            else:
                chosen[span, :] = jnp.where(pcol_ref[:, j : j + 1] == p, back, chosen[span, :])
    at = lax.broadcasted_iota(jnp.int32, (CAP, count), 0) == rank_ref[...]
    place = jnp.where(at, wt_ref[...].astype(F32), 0.0).astype(BF)
    copies = []
    for g in range(made.shape[0] // (group * CAP)):
        parts = []
        for d in range(group):
            here = (cell_ref[...] == g * group + d).astype(F32).astype(BF)
            parts.append(place * here)
        pick = jnp.concatenate(parts, axis=0)
        span = pl.ds(g * group * CAP, group * CAP)
        made[span, :] = jnp.dot(pick, chosen[...], preferred_element_type=F32).astype(BF)
        copies.append(pltpu.make_async_copy(made.at[span, :], out_ref.at[span, :], sems.at[g]))
        copies[-1].start()
    for copy in copies:
        copy.wait()


def look_kernel(ids_ref, *refs):
    *pieces, out_ref, table = refs
    rows = pieces[0].shape[0]

    @pl.when(pl.program_id(0) == 0)
    def _():
        for k, piece in enumerate(pieces):
            table[pl.ds(k * rows, rows), :] = piece[...]

    pick = lax.broadcasted_iota(jnp.int32, (ids_ref.shape[0], table.shape[0]), 1) == ids_ref[...]
    out_ref[...] = jnp.dot(
        pick.astype(F32).astype(BF), table[...], preferred_element_type=F32
    ).astype(BF)


def sum_kernel(ids_ref, flags_ref, got_ref, *out_refs):
    rows = out_refs[0].shape[0]
    slots = ids_ref.shape[1]
    over = jnp.where(jnp.max(flags_ref[...]) > 0, OVER, 0.0)
    for k, out_ref in enumerate(out_refs):
        pick = lax.broadcasted_iota(jnp.int32, (rows, slots), 0) == ids_ref[...] - k * rows
        part = jnp.dot(pick.astype(F32).astype(BF), got_ref[...], preferred_element_type=F32)
        out_ref[...] = (part + over).astype(out_ref.dtype)


def out_kernel(slot_ref, pcol_ref, wcol_ref, ret_ref, proj_ref, out_ref, sums):
    tok, per_token = slot_ref.shape
    slots = ret_ref.shape[0]
    projs, width, out_width = proj_ref.shape
    lane = lax.broadcasted_iota(jnp.int32, (tok, slots), 1)
    for j in range(per_token):
        pick = (lane == slot_ref[:, j : j + 1]).astype(F32).astype(BF)
        row = jnp.dot(pick, ret_ref[...], preferred_element_type=F32) * wcol_ref[:, j : j + 1]
        for p in range(projs):
            part = jnp.where(pcol_ref[:, j : j + 1] == p, row, 0.0)
            if j == 0:
                sums[p] = part
            else:
                sums[p] += part
    mixed = jnp.concatenate([sums[p].astype(BF) for p in range(projs)], axis=1)
    chunk = 512
    for n in range(out_width // chunk):
        span = pl.ds(n * chunk, chunk)
        out_ref[:, span] = jnp.dot(
            mixed, proj_ref[:, :, span].reshape(projs * width, chunk), preferred_element_type=F32
        ).astype(BF)


def short_way(picks, pick_weights, token_grads, values, first_moment, second_moment, projectors):
    plane = ("y", "c", "x")
    cells = lax.axis_size(plane)
    depth = lax.axis_size("z")
    parts = lax.axis_size("x")
    rows_dev, width = values.shape
    quarter = rows_dev // parts
    tok, per_token = picks.shape
    proj_count, _, out_width = projectors.shape
    total = tok * per_token
    slots = cells * CAP
    table_rows = depth * quarter
    start = lax.axis_index("x") * quarter
    old_rows = lax.dynamic_slice_in_dim(values, start, quarter, 0)

    by_pick = picks.T.reshape(1, total)
    owner = lax.div(by_pick, rows_dev)
    row = lax.rem(by_pick, rows_dev)
    owner_y = lax.div(owner, depth * CORES)
    owner_z = lax.rem(lax.div(owner, CORES), depth)
    cell = (owner_y * CORES + lax.rem(owner, CORES)) * parts + lax.div(row, quarter)
    trow = owner_z * quarter + lax.rem(row, quarter)
    block = 256
    rank, requests = call(
        functools.partial(rank_kernel, cells, block),
        (
            jax.ShapeDtypeStruct((1, total), jnp.int32),
            jax.ShapeDtypeStruct((cells, LANES), jnp.int32),
        ),
        8,
        cost=cost(2 * total * cells * 400, 20000),
    )(cell, trow)
    received = lax.all_to_all(requests, plane, split_axis=0, concat_axis=0, tiled=True)

    pcol = lax.rem(picks, proj_count)
    wt_row = pick_weights.T.reshape(1, total)
    whole = lambda shape: pl.BlockSpec(shape, lambda i: (0,) * len(shape))
    vmem = pl.BlockSpec(memory_space=pltpu.VMEM)
    group = 8
    sent = call(
        functools.partial(send_kernel, group),
        jax.ShapeDtypeStruct((slots, width), BF),
        20,
        in_specs=[vmem] * 6,
        out_specs=pl.BlockSpec(memory_space=pltpu.HBM),
        scratch=[
            pltpu.VMEM((total, width), BF),
            pltpu.VMEM((slots, width), BF),
            pltpu.SemaphoreType.DMA((cells // group,)),
        ],
        cost=cost(2 * width * (tok * proj_count * out_width + slots * total), 12000000),
    )(token_grads, projectors, pcol, cell, rank, wt_row)
    pieces = [old_rows] + [
        lax.ppermute(old_rows, "z", [(i, (i - k) % depth) for i in range(depth)])
        for k in range(1, depth)
    ]
    near = depth // 2 - 1
    sent, *pieces[near : depth - near + 1] = lax.optimization_barrier(
        (sent, *pieces[near : depth - near + 1])
    )
    got = lax.all_to_all(
        sent.reshape(cells, CAP, width), plane, split_axis=0, concat_axis=0, tiled=True
    ).reshape(slots, width)

    z_here = lax.axis_index("z")
    told = received[:, :CAP]
    from_z = lax.rem(lax.div(told, quarter) + depth - z_here, depth)
    asked = jnp.where(told < 0, -1, from_z * quarter + lax.rem(told, quarter))
    flags = received[:, LANES - 1 :]
    chunk = slots // 8
    looked = call(
        look_kernel,
        jax.ShapeDtypeStruct((slots, width), BF),
        16,
        grid=(8,),
        in_specs=[pl.BlockSpec((chunk, 1), lambda i: (i, 0))] + [whole((quarter, width))] * depth,
        out_specs=pl.BlockSpec((chunk, width), lambda i: (i, 0)),
        scratch=[pltpu.VMEM((table_rows, width), BF)],
        cost=cost(2 * width * slots * table_rows, 4000000),
    )(asked.reshape(slots, 1), *pieces)
    got, looked = lax.optimization_barrier((got, looked))
    returned = lax.all_to_all(
        looked.reshape(cells, CAP, width), plane, split_axis=0, concat_axis=0, tiled=True
    ).reshape(slots, width)

    sums = call(
        sum_kernel,
        (jax.ShapeDtypeStruct((quarter, width), BF),) * depth,
        16,
        in_specs=[vmem] * 3,
        out_specs=(vmem,) * depth,
        cost=cost(2 * width * slots * table_rows, 4000000),
    )(asked.reshape(1, slots), flags, got)
    shares = [sums[0]] + [
        lax.ppermute(sums[k], "z", [(i, (i + k) % depth) for i in range(depth)])
        for k in range(1, depth)
    ]
    share = functools.reduce(lambda p, q: p + q, [s.astype(F32) for s in shares])
    flag = share[0, 0] > 0.5 * OVER
    new_first, new_second, new_part = adam_rows(old_rows, share, first_moment, second_moment)
    x_here = lax.axis_index("x")
    new_values = jnp.zeros((parts, quarter, width), BF)
    for k in range(parts):
        piece = new_part
        if k:
            piece = lax.ppermute(new_part, "x", [(i, (i + k) % parts) for i in range(parts)])
        mine = jnp.arange(parts) == (x_here - k) % parts
        new_values = jnp.where(mine[:, None, None], piece[None], new_values)
    new_values = new_values.reshape(rows_dev, width)

    slot_col = (cell * CAP + rank).reshape(per_token, tok).T
    layer_out = call(
        out_kernel,
        jax.ShapeDtypeStruct((tok, out_width), BF),
        24,
        in_specs=[vmem] * 5,
        out_specs=vmem,
        scratch=[pltpu.VMEM((proj_count, tok, width), F32)],
        cost=cost(2 * width * (tok * proj_count * out_width + slots * total), 13000000),
    )(slot_col, pcol, pick_weights.astype(F32), returned, projectors)
    return flag, (layer_out, new_values, new_first, new_second)


def on_device(*args):
    flag, outs = lax.optimization_barrier(short_way(*args))
    return lax.cond(flag, lambda given, done: long_way(*given), lambda given, done: done, args, outs)


def solution(mesh):
    mem, dp = mesh.devices.shape
    grid = Mesh(
        mesh.devices.reshape(mem // (Z_CHIPS * CORES), Z_CHIPS, CORES, dp), ("y", "z", "c", "x")
    )
    every = P(("y", "z", "c", "x"), None)
    slab = P(("y", "z", "c"), None)
    return jax.shard_map(
        on_device,
        mesh=grid,
        in_specs=(every, every, every, slab, every, every, P()),
        out_specs=(every, slab, every, every),
        check_vma=False,
    )
```

```python
import functools

import jax
import jax.numpy as jnp
from jax import lax
from jax.experimental import pallas as pl
from jax.experimental.pallas import tpu as pltpu
from jax.sharding import Mesh
from jax.sharding import PartitionSpec as P

beta_one = 0.9
beta_two = 0.999
corr_one = 1.0 - 0.9**50
corr_two = 1.0 - 0.999**50
learn_rate = 0.05
adam_eps = 1e-08

Z_CHIPS = 8
CORES = 2
CAP = 72
LANES = 128
OVER = 1e30
BF = jnp.bfloat16
F32 = jnp.float32
NT = (((1,), (1,)), ((), ()))


def adam_rows(old_rows, slab_grad, first_moment, second_moment):
    new_first = beta_one * first_moment + (1.0 - beta_one) * slab_grad
    new_second = beta_two * second_moment + (1.0 - beta_two) * slab_grad * slab_grad
    update_step = new_first / corr_one / (jnp.sqrt(new_second / corr_two) + adam_eps)
    updated = (old_rows.astype(jnp.float32) - learn_rate * update_step).astype(jnp.bfloat16)
    return (new_first, new_second, updated)


def long_way(picks, pick_weights, token_grads, values, first_moment, second_moment, projectors):
    mem = ("y", "z", "c")
    owners = lax.axis_size(mem)
    rows_dev = values.shape[0]
    width = values.shape[1]
    tok_count, per_token = picks.shape
    proj_count = projectors.shape[0]
    out_width = projectors.shape[2]
    total_picks = tok_count * per_token
    capacity = 2 * total_picks // owners
    flat_picks = picks.reshape(-1)
    owner_ids = flat_picks // rows_dev
    local_rows = flat_picks - owner_ids * rows_dev
    member = (owner_ids[:, None] == jnp.arange(owners, dtype=jnp.int32)[None, :]).astype(jnp.int32)
    before = jnp.cumsum(member, axis=0) - member
    slot_ids = owner_ids * capacity + jnp.sum(before * member, axis=1)
    proj_ids = picks % proj_count
    flat_proj = projectors.reshape(proj_count * width, out_width)
    requests = jnp.zeros((owners * capacity,), jnp.int32).at[slot_ids].set(local_rows)
    requests = requests.reshape(owners, capacity)
    received = lax.all_to_all(requests, mem, split_axis=0, concat_axis=0, tiled=True)
    looked = values[received]
    returned = lax.all_to_all(looked, mem, split_axis=0, concat_axis=0, tiled=True)
    back_grads = lax.dot_general(token_grads, flat_proj, NT, preferred_element_type=jnp.float32)
    back_grads = back_grads.astype(jnp.bfloat16).reshape(tok_count, proj_count, width)
    chosen = back_grads[jnp.arange(tok_count, dtype=jnp.int32)[:, None], proj_ids].reshape(
        total_picks, width
    )
    grad_rows = jnp.zeros((owners * capacity, width), jnp.bfloat16).at[slot_ids].set(chosen)
    grad_wts = (
        jnp.zeros((owners * capacity,), jnp.bfloat16).at[slot_ids].set(pick_weights.reshape(-1))
    )
    got_rows = lax.all_to_all(
        grad_rows.reshape(owners, capacity, width), mem, split_axis=0, concat_axis=0, tiled=True
    )
    got_wts = lax.all_to_all(
        grad_wts.reshape(owners, capacity), mem, split_axis=0, concat_axis=0, tiled=True
    )
    picked = returned.reshape(owners * capacity, width)[slot_ids].reshape(
        tok_count, per_token, width
    )
    mixing = jnp.where(
        proj_ids[..., None] == jnp.arange(proj_count, dtype=jnp.int32),
        pick_weights[..., None],
        jnp.zeros((), jnp.bfloat16),
    )
    proj_sums = jnp.einsum(
        "tjp,tjd->tpd", mixing, picked, preferred_element_type=jnp.float32
    ).astype(jnp.bfloat16)
    layer_out = jnp.dot(
        proj_sums.reshape(tok_count, proj_count * width),
        flat_proj,
        preferred_element_type=jnp.float32,
    ).astype(jnp.bfloat16)
    weighted = got_wts.astype(jnp.float32)[..., None] * got_rows.astype(jnp.float32)
    slab_grad = (
        jnp.zeros((rows_dev, width), jnp.float32)
        .at[received.reshape(-1)]
        .add(weighted.reshape(-1, width))
    )
    quarter = first_moment.shape[0]
    start = lax.axis_index("x") * quarter
    share = jnp.sum(
        lax.all_to_all(
            slab_grad.reshape(-1, quarter, width), "x", split_axis=0, concat_axis=0, tiled=True
        ),
        axis=0,
    )
    old_rows = lax.dynamic_slice_in_dim(values, start, quarter, 0)
    new_first, new_second, new_part = adam_rows(old_rows, share, first_moment, second_moment)
    new_values = lax.all_gather(new_part, "x", axis=0, tiled=True)
    return (layer_out, new_values, new_first, new_second)


def call(kernel, out_shape, vmem, grid=None, in_specs=None, out_specs=None, scratch=(), cost=None):
    extra = {} if grid is None else {"grid": grid}
    if in_specs is not None:
        extra["in_specs"] = in_specs
    if out_specs is not None:
        extra["out_specs"] = out_specs
    return pl.pallas_call(
        kernel,
        out_shape=out_shape,
        scratch_shapes=list(scratch),
        compiler_params=pltpu.CompilerParams(vmem_limit_bytes=vmem * 1024 * 1024),
        cost_estimate=cost,
        **extra,
    )


def cost(flops, nbytes):
    return pl.CostEstimate(flops=flops, bytes_accessed=nbytes, transcendentals=0)


def rank_kernel(
    sizes, pick_ref, wt_ref, cell_ref, rank_ref, wrow_ref, req_ref, pcol_ref, slot_ref, wcol_ref
):
    cells, depth, parts, rows_dev, proj_count = sizes
    per_token, tok = pick_ref.shape
    count = per_token * tok
    quarter = rows_dev // parts
    block = 256
    by_token = pick_ref[...]
    flat = jnp.concatenate([by_token[j : j + 1] for j in range(per_token)], axis=1)
    weights = wt_ref[...].astype(F32)
    wrow_ref[...] = jnp.concatenate([weights[j : j + 1] for j in range(per_token)], axis=1)
    owner = lax.div(flat, rows_dev)
    row = lax.rem(flat, rows_dev)
    owner_z = lax.rem(lax.div(owner, CORES), depth)
    cells_row = (
        lax.div(owner, depth * CORES) * CORES + lax.rem(owner, CORES)
    ) * parts + lax.div(row, quarter)
    trows = owner_z * quarter + lax.rem(row, quarter)
    cell_ref[...] = cells_row
    below = lax.broadcasted_iota(jnp.int32, (block, block), 0) < lax.broadcasted_iota(
        jnp.int32, (block, block), 1
    )
    below = below.astype(F32).astype(BF)
    carry = jnp.zeros((cells, 1), F32)
    asked = jnp.zeros((3 * cells, LANES), F32)
    ranks = []
    for b in range(count // block):
        cell = cells_row[:, b * block : (b + 1) * block]
        trow = trows[:, b * block : (b + 1) * block]
        here = (lax.broadcasted_iota(jnp.int32, (cells, block), 0) == cell).astype(F32)
        before = jnp.dot(here.astype(BF), below, preferred_element_type=F32) + carry
        carry = carry + jnp.sum(here, axis=1, keepdims=True)
        rank = jnp.sum(here * before, axis=0, keepdims=True).astype(jnp.int32)
        ranks.append(rank)
        place = (lax.broadcasted_iota(jnp.int32, (LANES, block), 0) == rank).astype(F32)
        high = (trow >> 5).astype(F32)
        low = (trow & 31).astype(F32)
        told = jnp.concatenate([here, here * high, here * low], axis=0)
        asked = asked + lax.dot_general(
            told.astype(BF), place.astype(BF), NT, preferred_element_type=F32
        )
    there = asked[:cells]
    rows = (asked[cells : 2 * cells] * 32.0 + asked[2 * cells :]).astype(jnp.int32)
    rows = jnp.where(there > 0.5, rows, -1)
    lane = lax.broadcasted_iota(jnp.int32, (cells, LANES), 1)
    over = (jnp.max(carry) > CAP).astype(jnp.int32)
    req_ref[...] = jnp.where(lane == LANES - 1, over, rows)
    rank_row = jnp.concatenate(ranks, axis=1)
    rank_ref[...] = rank_row
    slots = cells_row * CAP + rank_row
    by_row = jnp.concatenate([slots[:, j * tok : (j + 1) * tok] for j in range(per_token)], axis=0)
    slot_ref[...] = by_row.T
    pcol_ref[...] = lax.rem(by_token, proj_count).T
    wcol_ref[...] = weights.T


def send_kernel(
    group,
    tg_ref,
    proj_ref,
    pcol_ref,
    cell_ref,
    rank_ref,
    wt_ref,
    out_ref,
    grads,
    projs,
    chosen,
    made,
    in_sems,
    out_sems,
):
    tok, per_token = pcol_ref.shape
    count = cell_ref.shape[1]
    proj_count = proj_ref.shape[0]
    come = [pltpu.make_async_copy(tg_ref, grads, in_sems.at[proj_count])]
    for p in range(proj_count):
        come.append(pltpu.make_async_copy(proj_ref.at[p], projs.at[p], in_sems.at[p]))
    for copy in come:
        copy.start()
    at = lax.broadcasted_iota(jnp.int32, (CAP, count), 0) == rank_ref[...]
    place = jnp.where(at, wt_ref[...], 0.0).astype(BF)
    come[0].wait()
    for p in range(proj_count):
        come[p + 1].wait()
        back = lax.dot_general(grads[...], projs[p], NT, preferred_element_type=F32).astype(BF)
        for j in range(per_token):
            span = pl.ds(j * tok, tok)
            if p == 0:
                chosen[span, :] = back
            else:
                chosen[span, :] = jnp.where(pcol_ref[:, j : j + 1] == p, back, chosen[span, :])
    copies = []
    for g in range(made.shape[0] // (group * CAP)):
        parts = []
        for d in range(group):
            here = (cell_ref[...] == g * group + d).astype(F32).astype(BF)
            parts.append(place * here)
        pick = jnp.concatenate(parts, axis=0)
        span = pl.ds(g * group * CAP, group * CAP)
        made[span, :] = jnp.dot(pick, chosen[...], preferred_element_type=F32).astype(BF)
        copies.append(pltpu.make_async_copy(made.at[span, :], out_ref.at[span, :], out_sems.at[g]))
        copies[-1].start()
    for copy in copies:
        copy.wait()


def look_kernel(ids_ref, *refs):
    *pieces, out_ref, table, sems = refs
    rows = pieces[0].shape[0]

    @pl.when(pl.program_id(0) == 0)
    def _():
        copies = [
            pltpu.make_async_copy(piece, table.at[pl.ds(k * rows, rows), :], sems.at[k])
            for k, piece in enumerate(pieces)
        ]
        for copy in copies:
            copy.start()
        for copy in copies:
            copy.wait()

    pick = lax.broadcasted_iota(jnp.int32, (ids_ref.shape[0], table.shape[0]), 1) == ids_ref[...]
    out_ref[...] = jnp.dot(
        pick.astype(F32).astype(BF), table[...], preferred_element_type=F32
    ).astype(BF)


def sum_kernel(ids_ref, flags_ref, got_ref, *out_refs):
    rows = out_refs[0].shape[0]
    slots = ids_ref.shape[1]
    over = jnp.where(jnp.max(flags_ref[...]) > 0, OVER, 0.0)
    for k, out_ref in enumerate(out_refs):
        pick = lax.broadcasted_iota(jnp.int32, (rows, slots), 0) == ids_ref[...] - k * rows
        part = jnp.dot(pick.astype(F32).astype(BF), got_ref[...], preferred_element_type=F32)
        out_ref[...] = (part + over).astype(out_ref.dtype)


def out_kernel(
    slot_ref, pcol_ref, wcol_ref, ret_ref, proj_ref, out_ref, projs, sums, made, in_sems, out_sems
):
    tok, per_token = slot_ref.shape
    slots = ret_ref.shape[0]
    proj_count, width, out_width = proj_ref.shape
    come = [
        pltpu.make_async_copy(proj_ref.at[p], projs.at[p], in_sems.at[p])
        for p in range(proj_count)
    ]
    for copy in come:
        copy.start()
    lane = lax.broadcasted_iota(jnp.int32, (tok, slots), 1)
    for j in range(per_token):
        pick = (lane == slot_ref[:, j : j + 1]).astype(F32).astype(BF)
        row = jnp.dot(pick, ret_ref[...], preferred_element_type=F32) * wcol_ref[:, j : j + 1]
        for p in range(proj_count):
            part = jnp.where(pcol_ref[:, j : j + 1] == p, row, 0.0)
            if j == 0:
                sums[p] = part
            else:
                sums[p] += part
    mixed = jnp.concatenate([sums[p].astype(BF) for p in range(proj_count)], axis=1)
    for copy in come:
        copy.wait()
    chunk = out_width // made.shape[0]
    copies = []
    for n in range(made.shape[0]):
        span = pl.ds(n * chunk, chunk)
        made[n] = jnp.dot(
            mixed,
            projs[:, :, span].reshape(proj_count * width, chunk),
            preferred_element_type=F32,
        ).astype(BF)
        copies.append(pltpu.make_async_copy(made.at[n], out_ref.at[:, span], out_sems.at[n]))
        copies[-1].start()
    for copy in copies:
        copy.wait()


def short_way(picks, pick_weights, token_grads, values, first_moment, second_moment, projectors):
    plane = ("y", "c", "x")
    cells = lax.axis_size(plane)
    depth = lax.axis_size("z")
    parts = lax.axis_size("x")
    rows_dev, width = values.shape
    quarter = rows_dev // parts
    tok, per_token = picks.shape
    proj_count, _, out_width = projectors.shape
    total = tok * per_token
    slots = cells * CAP
    table_rows = depth * quarter
    start = lax.axis_index("x") * quarter
    old_rows = lax.dynamic_slice_in_dim(values, start, quarter, 0)

    hbm = pl.BlockSpec(memory_space=pl.ANY)
    vmem = pl.BlockSpec(memory_space=pltpu.VMEM)
    i32 = lambda *shape: jax.ShapeDtypeStruct(shape, jnp.int32)
    f32 = lambda *shape: jax.ShapeDtypeStruct(shape, F32)
    cell, rank, wt_row, requests, pcol, slot_col, wcol = call(
        functools.partial(rank_kernel, (cells, depth, parts, rows_dev, proj_count)),
        (
            i32(1, total),
            i32(1, total),
            f32(1, total),
            i32(cells, LANES),
            i32(tok, per_token),
            i32(tok, per_token),
            f32(tok, per_token),
        ),
        60,
        in_specs=[vmem] * 2,
        out_specs=(vmem,) * 7,
        cost=cost(2 * total * cells * 400, 20000),
    )(picks.T, pick_weights.T)
    received = lax.all_to_all(requests, plane, split_axis=0, concat_axis=0, tiled=True)

    group = 8
    sent = call(
        functools.partial(send_kernel, group),
        jax.ShapeDtypeStruct((slots, width), BF),
        60,
        in_specs=[hbm] * 2 + [vmem] * 4,
        out_specs=hbm,
        scratch=[
            pltpu.VMEM((tok, out_width), BF),
            pltpu.VMEM(projectors.shape, BF),
            pltpu.VMEM((total, width), BF),
            pltpu.VMEM((slots, width), BF),
            pltpu.SemaphoreType.DMA((proj_count + 1,)),
            pltpu.SemaphoreType.DMA((cells // group,)),
        ],
        cost=cost(2 * width * (tok * proj_count * out_width + slots * total), 12000000),
    )(token_grads, projectors, pcol, cell, rank, wt_row)
    got = lax.all_to_all(
        sent.reshape(cells, CAP, width), plane, split_axis=0, concat_axis=0, tiled=True
    ).reshape(slots, width)

    onward = [(i, (i + 1) % depth) for i in range(depth)]
    backward = [(i, (i - 1) % depth) for i in range(depth)]
    pieces = [old_rows] + [None] * (depth - 1)
    for k in range(1, depth // 2 + 1):
        pieces[k] = lax.ppermute(pieces[k - 1], "z", backward)
        if k < depth // 2:
            pieces[depth - k] = lax.ppermute(pieces[(depth - k + 1) % depth], "z", onward)
    z_here = lax.axis_index("z")
    told = received[:, :CAP]
    from_z = lax.rem(lax.div(told, quarter) + depth - z_here, depth)
    asked = jnp.where(told < 0, -1, from_z * quarter + lax.rem(told, quarter))
    flags = received[:, LANES - 1 :]
    chunk = slots // 8
    looked = call(
        look_kernel,
        jax.ShapeDtypeStruct((slots, width), BF),
        60,
        grid=(8,),
        in_specs=[pl.BlockSpec((chunk, 1), lambda i: (i, 0))] + [hbm] * depth,
        out_specs=pl.BlockSpec((chunk, width), lambda i: (i, 0)),
        scratch=[pltpu.VMEM((table_rows, width), BF), pltpu.SemaphoreType.DMA((depth,))],
        cost=cost(2 * width * slots * table_rows, 4000000),
    )(asked.reshape(slots, 1), *pieces)
    sums = call(
        sum_kernel,
        (jax.ShapeDtypeStruct((quarter, width), BF),) * depth,
        16,
        in_specs=[vmem] * 3,
        out_specs=(vmem,) * depth,
        cost=cost(2 * width * slots * table_rows, 4000000),
    )(asked.reshape(1, slots), flags, got)
    looked, *sums = lax.optimization_barrier((looked, *sums))
    returned = lax.all_to_all(
        looked.reshape(cells, CAP, width), plane, split_axis=0, concat_axis=0, tiled=True
    ).reshape(slots, width)

    ahead = sums[depth // 2]
    behind = sums[depth // 2 + 1]
    for k in range(depth // 2 - 1, 0, -1):
        ahead = (lax.ppermute(ahead, "z", onward).astype(F32) + sums[k].astype(F32)).astype(BF)
        if k > 1:
            behind = (
                lax.ppermute(behind, "z", backward).astype(F32) + sums[depth - k + 1].astype(F32)
            ).astype(BF)
    share = (
        sums[0].astype(F32)
        + lax.ppermute(ahead, "z", onward).astype(F32)
        + lax.ppermute(behind, "z", backward).astype(F32)
    )
    flag = share[0, 0] > 0.5 * OVER
    new_first, new_second, new_part = adam_rows(old_rows, share, first_moment, second_moment)
    new_parts = [new_part] + [
        lax.ppermute(new_part, "x", [(i, (i + k) % parts) for i in range(parts)])
        for k in range(1, parts)
    ]

    chunks = 4
    layer_out = call(
        out_kernel,
        jax.ShapeDtypeStruct((tok, out_width), BF),
        48,
        in_specs=[vmem] * 4 + [hbm],
        out_specs=hbm,
        scratch=[
            pltpu.VMEM(projectors.shape, BF),
            pltpu.VMEM((proj_count, tok, width), F32),
            pltpu.VMEM((chunks, tok, out_width // chunks), BF),
            pltpu.SemaphoreType.DMA((proj_count,)),
            pltpu.SemaphoreType.DMA((chunks,)),
        ],
        cost=cost(2 * width * (tok * proj_count * out_width + slots * total), 13000000),
    )(slot_col, pcol, wcol, returned, projectors)
    return flag, (layer_out, new_parts, new_first, new_second)


def joined(outs):
    layer_out, new_parts, new_first, new_second = outs
    parts = len(new_parts)
    x_here = lax.axis_index("x")
    new_values = jnp.zeros((parts, *new_parts[0].shape), BF)
    for k, piece in enumerate(new_parts):
        mine = jnp.arange(parts) == lax.rem(x_here + parts - k, parts)
        new_values = jnp.where(mine[:, None, None], piece[None], new_values)
    return layer_out, new_values.reshape(-1, new_values.shape[2]), new_first, new_second


def on_device(*args):
    flag, outs = short_way(*args)
    return lax.cond(
        flag, lambda given, done: long_way(*given), lambda given, done: joined(done), args, outs
    )


def solution(mesh):
    mem, dp = mesh.devices.shape
    grid = Mesh(
        mesh.devices.reshape(mem // (Z_CHIPS * CORES), Z_CHIPS, CORES, dp), ("y", "z", "c", "x")
    )
    every = P(("y", "z", "c", "x"), None)
    slab = P(("y", "z", "c"), None)
    return jax.shard_map(
        on_device,
        mesh=grid,
        in_specs=(every, every, every, slab, every, every, P()),
        out_specs=(every, slab, every, every),
        check_vma=False,
    )
```

```python
import functools

import jax
import jax.numpy as jnp
from jax import lax
from jax.experimental import pallas as pl
from jax.experimental.pallas import tpu as pltpu
from jax.sharding import Mesh
from jax.sharding import PartitionSpec as P

beta_one = 0.9
beta_two = 0.999
corr_one = 1.0 - 0.9**50
corr_two = 1.0 - 0.999**50
learn_rate = 0.05
adam_eps = 1e-08

Z_CHIPS = 8
CORES = 2
CAP = 72
LANES = 128
OVER = 1e30
BF = jnp.bfloat16
F32 = jnp.float32
NT = (((1,), (1,)), ((), ()))


def adam_rows(old_rows, slab_grad, first_moment, second_moment):
    new_first = beta_one * first_moment + (1.0 - beta_one) * slab_grad
    new_second = beta_two * second_moment + (1.0 - beta_two) * slab_grad * slab_grad
    update_step = new_first / corr_one / (jnp.sqrt(new_second / corr_two) + adam_eps)
    updated = (old_rows.astype(jnp.float32) - learn_rate * update_step).astype(jnp.bfloat16)
    return (new_first, new_second, updated)


def spread(new_part):
    parts = lax.axis_size("x")
    return [new_part] + [
        lax.ppermute(new_part, "x", [(i, (i + k) % parts) for i in range(parts)])
        for k in range(1, parts)
    ]


def joined(outs):
    layer_out, new_parts, new_first, new_second = outs
    parts = len(new_parts)
    x_here = lax.axis_index("x")
    new_values = jnp.zeros((parts, *new_parts[0].shape), BF)
    for k, piece in enumerate(new_parts):
        mine = jnp.arange(parts) == lax.rem(x_here + parts - k, parts)
        new_values = jnp.where(mine[:, None, None], piece[None], new_values)
    return layer_out, new_values.reshape(-1, new_values.shape[2]), new_first, new_second


def long_way(picks, pick_weights, token_grads, values, first_moment, second_moment, projectors):
    mem = ("y", "z", "c")
    owners = lax.axis_size(mem)
    rows_dev = values.shape[0]
    width = values.shape[1]
    tok_count, per_token = picks.shape
    proj_count = projectors.shape[0]
    out_width = projectors.shape[2]
    total_picks = tok_count * per_token
    capacity = 2 * total_picks // owners
    flat_picks = picks.reshape(-1)
    owner_ids = flat_picks // rows_dev
    local_rows = flat_picks - owner_ids * rows_dev
    member = (owner_ids[:, None] == jnp.arange(owners, dtype=jnp.int32)[None, :]).astype(jnp.int32)
    before = jnp.cumsum(member, axis=0) - member
    slot_ids = owner_ids * capacity + jnp.sum(before * member, axis=1)
    proj_ids = picks % proj_count
    flat_proj = projectors.reshape(proj_count * width, out_width)
    requests = jnp.zeros((owners * capacity,), jnp.int32).at[slot_ids].set(local_rows)
    requests = requests.reshape(owners, capacity)
    received = lax.all_to_all(requests, mem, split_axis=0, concat_axis=0, tiled=True)
    looked = values[received]
    returned = lax.all_to_all(looked, mem, split_axis=0, concat_axis=0, tiled=True)
    back_grads = lax.dot_general(token_grads, flat_proj, NT, preferred_element_type=jnp.float32)
    back_grads = back_grads.astype(jnp.bfloat16).reshape(tok_count, proj_count, width)
    chosen = back_grads[jnp.arange(tok_count, dtype=jnp.int32)[:, None], proj_ids].reshape(
        total_picks, width
    )
    grad_rows = jnp.zeros((owners * capacity, width), jnp.bfloat16).at[slot_ids].set(chosen)
    grad_wts = (
        jnp.zeros((owners * capacity,), jnp.bfloat16).at[slot_ids].set(pick_weights.reshape(-1))
    )
    got_rows = lax.all_to_all(
        grad_rows.reshape(owners, capacity, width), mem, split_axis=0, concat_axis=0, tiled=True
    )
    got_wts = lax.all_to_all(
        grad_wts.reshape(owners, capacity), mem, split_axis=0, concat_axis=0, tiled=True
    )
    picked = returned.reshape(owners * capacity, width)[slot_ids].reshape(
        tok_count, per_token, width
    )
    mixing = jnp.where(
        proj_ids[..., None] == jnp.arange(proj_count, dtype=jnp.int32),
        pick_weights[..., None],
        jnp.zeros((), jnp.bfloat16),
    )
    proj_sums = jnp.einsum(
        "tjp,tjd->tpd", mixing, picked, preferred_element_type=jnp.float32
    ).astype(jnp.bfloat16)
    layer_out = jnp.dot(
        proj_sums.reshape(tok_count, proj_count * width),
        flat_proj,
        preferred_element_type=jnp.float32,
    ).astype(jnp.bfloat16)
    weighted = got_wts.astype(jnp.float32)[..., None] * got_rows.astype(jnp.float32)
    slab_grad = (
        jnp.zeros((rows_dev, width), jnp.float32)
        .at[received.reshape(-1)]
        .add(weighted.reshape(-1, width))
    )
    quarter = first_moment.shape[0]
    start = lax.axis_index("x") * quarter
    share = jnp.sum(
        lax.all_to_all(
            slab_grad.reshape(-1, quarter, width), "x", split_axis=0, concat_axis=0, tiled=True
        ),
        axis=0,
    )
    old_rows = lax.dynamic_slice_in_dim(values, start, quarter, 0)
    new_first, new_second, new_part = adam_rows(old_rows, share, first_moment, second_moment)
    return joined((layer_out, spread(new_part), new_first, new_second))


def call(kernel, out_shape, vmem, grid=None, in_specs=None, out_specs=None, scratch=(), cost=None):
    extra = {} if grid is None else {"grid": grid}
    if in_specs is not None:
        extra["in_specs"] = in_specs
    if out_specs is not None:
        extra["out_specs"] = out_specs
    return pl.pallas_call(
        kernel,
        out_shape=out_shape,
        scratch_shapes=list(scratch),
        compiler_params=pltpu.CompilerParams(vmem_limit_bytes=vmem * 1024 * 1024),
        cost_estimate=cost,
        **extra,
    )


def cost(flops, nbytes):
    return pl.CostEstimate(flops=flops, bytes_accessed=nbytes, transcendentals=0)


def rank_kernel(
    sizes, pick_ref, wt_ref, cell_ref, rank_ref, wrow_ref, req_ref, pcol_ref, slot_ref, wcol_ref
):
    cells, depth, parts, rows_dev, proj_count = sizes
    per_token, tok = pick_ref.shape
    count = per_token * tok
    quarter = rows_dev // parts
    block = 256
    by_token = pick_ref[...]
    flat = jnp.concatenate([by_token[j : j + 1] for j in range(per_token)], axis=1)
    weights = wt_ref[...].astype(F32)
    wrow_ref[...] = jnp.concatenate([weights[j : j + 1] for j in range(per_token)], axis=1)
    owner = lax.div(flat, rows_dev)
    row = lax.rem(flat, rows_dev)
    owner_z = lax.rem(lax.div(owner, CORES), depth)
    cells_row = (
        lax.div(owner, depth * CORES) * CORES + lax.rem(owner, CORES)
    ) * parts + lax.div(row, quarter)
    trows = owner_z * quarter + lax.rem(row, quarter)
    cell_ref[...] = cells_row
    below = lax.broadcasted_iota(jnp.int32, (block, block), 0) < lax.broadcasted_iota(
        jnp.int32, (block, block), 1
    )
    below = below.astype(F32).astype(BF)
    carry = jnp.zeros((cells, 1), F32)
    asked = jnp.zeros((3 * cells, LANES), F32)
    ranks = []
    for b in range(count // block):
        cell = cells_row[:, b * block : (b + 1) * block]
        trow = trows[:, b * block : (b + 1) * block]
        here = (lax.broadcasted_iota(jnp.int32, (cells, block), 0) == cell).astype(F32)
        before = jnp.dot(here.astype(BF), below, preferred_element_type=F32) + carry
        carry = carry + jnp.sum(here, axis=1, keepdims=True)
        rank = jnp.sum(here * before, axis=0, keepdims=True).astype(jnp.int32)
        ranks.append(rank)
        place = (lax.broadcasted_iota(jnp.int32, (LANES, block), 0) == rank).astype(F32)
        high = (trow >> 5).astype(F32)
        low = (trow & 31).astype(F32)
        told = jnp.concatenate([here, here * high, here * low], axis=0)
        asked = asked + lax.dot_general(
            told.astype(BF), place.astype(BF), NT, preferred_element_type=F32
        )
    there = asked[:cells]
    rows = (asked[cells : 2 * cells] * 32.0 + asked[2 * cells :]).astype(jnp.int32)
    rows = jnp.where(there > 0.5, rows, -1)
    lane = lax.broadcasted_iota(jnp.int32, (cells, LANES), 1)
    over = (jnp.max(carry) > CAP).astype(jnp.int32)
    req_ref[...] = jnp.where(lane == LANES - 1, over, rows)
    rank_row = jnp.concatenate(ranks, axis=1)
    rank_ref[...] = rank_row
    slots = cells_row * CAP + rank_row
    by_row = jnp.concatenate([slots[:, j * tok : (j + 1) * tok] for j in range(per_token)], axis=0)
    slot_ref[...] = by_row.T
    pcol_ref[...] = lax.rem(by_token, proj_count).T
    wcol_ref[...] = weights.T


def send_kernel(
    group,
    tg_ref,
    proj_ref,
    pcol_ref,
    cell_ref,
    rank_ref,
    wt_ref,
    out_ref,
    grads,
    projs,
    chosen,
    made,
    in_sems,
    out_sems,
):
    tok, per_token = pcol_ref.shape
    count = cell_ref.shape[1]
    proj_count = proj_ref.shape[0]
    come = [pltpu.make_async_copy(tg_ref, grads, in_sems.at[proj_count])]
    for p in range(proj_count):
        come.append(pltpu.make_async_copy(proj_ref.at[p], projs.at[p], in_sems.at[p]))
    for copy in come:
        copy.start()
    at = lax.broadcasted_iota(jnp.int32, (CAP, count), 0) == rank_ref[...]
    place = jnp.where(at, wt_ref[...], 0.0).astype(BF)
    come[0].wait()
    for p in range(proj_count):
        come[p + 1].wait()
        back = lax.dot_general(grads[...], projs[p], NT, preferred_element_type=F32).astype(BF)
        for j in range(per_token):
            span = pl.ds(j * tok, tok)
            if p == 0:
                chosen[span, :] = back
            else:
                chosen[span, :] = jnp.where(pcol_ref[:, j : j + 1] == p, back, chosen[span, :])
    copies = []
    for g in range(made.shape[0] // (group * CAP)):
        parts = []
        for d in range(group):
            here = (cell_ref[...] == g * group + d).astype(F32).astype(BF)
            parts.append(place * here)
        pick = jnp.concatenate(parts, axis=0)
        span = pl.ds(g * group * CAP, group * CAP)
        made[span, :] = jnp.dot(pick, chosen[...], preferred_element_type=F32).astype(BF)
        copies.append(pltpu.make_async_copy(made.at[span, :], out_ref.at[span, :], out_sems.at[g]))
        copies[-1].start()
    for copy in copies:
        copy.wait()


def look_kernel(group, got_ref, z_ref, *refs):
    *pieces, out_ref, table, made, in_sems, out_sems = refs
    rows = pieces[0].shape[0]
    cells = got_ref.shape[0]
    depth = len(pieces)
    come = [
        pltpu.make_async_copy(piece, table.at[pl.ds(k * rows, rows), :], in_sems.at[k])
        for k, piece in enumerate(pieces)
    ]
    for copy in come:
        copy.start()
    told = got_ref[...]
    from_z = lax.rem(lax.div(told, rows) + depth - z_ref[0], depth)
    asked = jnp.where(told < 0, -1, from_z * rows + lax.rem(told, rows)).T
    lane = lax.broadcasted_iota(jnp.int32, (CAP, depth * rows), 1)
    for copy in come:
        copy.wait()
    copies = []
    for g in range(cells // group):
        parts = []
        for d in range(g * group, (g + 1) * group):
            parts.append((lane == asked[:CAP, d : d + 1]).astype(F32).astype(BF))
        pick = jnp.concatenate(parts, axis=0)
        span = pl.ds(g * group * CAP, group * CAP)
        made[span, :] = jnp.dot(pick, table[...], preferred_element_type=F32).astype(BF)
        copies.append(pltpu.make_async_copy(made.at[span, :], out_ref.at[span, :], out_sems.at[g]))
        copies[-1].start()
    for copy in copies:
        copy.wait()


def sum_kernel(ids_ref, flags_ref, got_ref, *out_refs):
    rows = out_refs[0].shape[0]
    slots = ids_ref.shape[1]
    over = jnp.where(jnp.max(flags_ref[...]) > 0, OVER, 0.0)
    for k, out_ref in enumerate(out_refs):
        pick = lax.broadcasted_iota(jnp.int32, (rows, slots), 0) == ids_ref[...] - k * rows
        part = jnp.dot(pick.astype(F32).astype(BF), got_ref[...], preferred_element_type=F32)
        out_ref[...] = (part + over).astype(out_ref.dtype)


def out_kernel(
    slot_ref, pcol_ref, wcol_ref, ret_ref, proj_ref, out_ref, projs, sums, made, in_sems, out_sems
):
    tok, per_token = slot_ref.shape
    slots = ret_ref.shape[0]
    proj_count, width, out_width = proj_ref.shape
    come = [
        pltpu.make_async_copy(proj_ref.at[p], projs.at[p], in_sems.at[p])
        for p in range(proj_count)
    ]
    for copy in come:
        copy.start()
    lane = lax.broadcasted_iota(jnp.int32, (tok, slots), 1)
    for j in range(per_token):
        pick = (lane == slot_ref[:, j : j + 1]).astype(F32).astype(BF)
        row = jnp.dot(pick, ret_ref[...], preferred_element_type=F32) * wcol_ref[:, j : j + 1]
        for p in range(proj_count):
            part = jnp.where(pcol_ref[:, j : j + 1] == p, row, 0.0)
            if j == 0:
                sums[p] = part
            else:
                sums[p] += part
    mixed = jnp.concatenate([sums[p].astype(BF) for p in range(proj_count)], axis=1)
    for copy in come:
        copy.wait()
    chunk = out_width // made.shape[0]
    copies = []
    for n in range(made.shape[0]):
        span = pl.ds(n * chunk, chunk)
        made[n] = jnp.dot(
            mixed,
            projs[:, :, span].reshape(proj_count * width, chunk),
            preferred_element_type=F32,
        ).astype(BF)
        copies.append(pltpu.make_async_copy(made.at[n], out_ref.at[:, span], out_sems.at[n]))
        copies[-1].start()
    for copy in copies:
        copy.wait()


def short_way(picks, pick_weights, token_grads, values, first_moment, second_moment, projectors):
    plane = ("y", "c", "x")
    cells = lax.axis_size(plane)
    depth = lax.axis_size("z")
    parts = lax.axis_size("x")
    rows_dev, width = values.shape
    quarter = rows_dev // parts
    tok, per_token = picks.shape
    proj_count, _, out_width = projectors.shape
    total = tok * per_token
    slots = cells * CAP
    table_rows = depth * quarter
    start = lax.axis_index("x") * quarter
    old_rows = lax.dynamic_slice_in_dim(values, start, quarter, 0)

    hbm = pl.BlockSpec(memory_space=pl.ANY)
    vmem = pl.BlockSpec(memory_space=pltpu.VMEM)
    i32 = lambda *shape: jax.ShapeDtypeStruct(shape, jnp.int32)
    f32 = lambda *shape: jax.ShapeDtypeStruct(shape, F32)
    cell, rank, wt_row, requests, pcol, slot_col, wcol = call(
        functools.partial(rank_kernel, (cells, depth, parts, rows_dev, proj_count)),
        (
            i32(1, total),
            i32(1, total),
            f32(1, total),
            i32(cells, LANES),
            i32(tok, per_token),
            i32(tok, per_token),
            f32(tok, per_token),
        ),
        60,
        in_specs=[vmem] * 2,
        out_specs=(vmem,) * 7,
        cost=cost(2 * total * cells * 400, 20000),
    )(picks.T, pick_weights.T)
    received = lax.all_to_all(requests, plane, split_axis=0, concat_axis=0, tiled=True)

    group = 8
    sent = call(
        functools.partial(send_kernel, group),
        jax.ShapeDtypeStruct((slots, width), BF),
        60,
        in_specs=[hbm] * 2 + [vmem] * 4,
        out_specs=hbm,
        scratch=[
            pltpu.VMEM((tok, out_width), BF),
            pltpu.VMEM(projectors.shape, BF),
            pltpu.VMEM((total, width), BF),
            pltpu.VMEM((slots, width), BF),
            pltpu.SemaphoreType.DMA((proj_count + 1,)),
            pltpu.SemaphoreType.DMA((cells // group,)),
        ],
        cost=cost(2 * width * (tok * proj_count * out_width + slots * total), 12000000),
    )(token_grads, projectors, pcol, cell, rank, wt_row)
    got = lax.all_to_all(
        sent.reshape(cells, CAP, width), plane, split_axis=0, concat_axis=0, tiled=True
    ).reshape(slots, width)

    onward = [(i, (i + 1) % depth) for i in range(depth)]
    backward = [(i, (i - 1) % depth) for i in range(depth)]
    pieces = [old_rows] + [None] * (depth - 1)
    for k in range(1, depth // 2 + 1):
        pieces[k] = lax.ppermute(pieces[k - 1], "z", backward)
        if k < depth // 2:
            pieces[depth - k] = lax.ppermute(pieces[(depth - k + 1) % depth], "z", onward)
    z_here = lax.axis_index("z")
    told = received[:, :CAP]
    from_z = lax.rem(lax.div(told, quarter) + depth - z_here, depth)
    asked = jnp.where(told < 0, -1, from_z * quarter + lax.rem(told, quarter))
    flags = received[:, LANES - 1 :]
    looked = call(
        functools.partial(look_kernel, group),
        jax.ShapeDtypeStruct((slots, width), BF),
        60,
        in_specs=[vmem, pl.BlockSpec(memory_space=pltpu.SMEM)] + [hbm] * depth,
        out_specs=hbm,
        scratch=[
            pltpu.VMEM((table_rows, width), BF),
            pltpu.VMEM((slots, width), BF),
            pltpu.SemaphoreType.DMA((depth,)),
            pltpu.SemaphoreType.DMA((cells // group,)),
        ],
        cost=cost(2 * width * slots * table_rows, 4000000),
    )(received, z_here.reshape(1), *pieces)
    sums = call(
        sum_kernel,
        (jax.ShapeDtypeStruct((quarter, width), BF),) * depth,
        16,
        in_specs=[vmem] * 3,
        out_specs=(vmem,) * depth,
        cost=cost(2 * width * slots * table_rows, 4000000),
    )(asked.reshape(1, slots), flags, got)
    looked, *sums = lax.optimization_barrier((looked, *sums))
    returned = lax.all_to_all(
        looked.reshape(cells, CAP, width), plane, split_axis=0, concat_axis=0, tiled=True
    ).reshape(slots, width)

    ahead = sums[depth // 2]
    behind = sums[depth // 2 + 1]
    for k in range(depth // 2 - 1, 0, -1):
        ahead = (lax.ppermute(ahead, "z", onward).astype(F32) + sums[k].astype(F32)).astype(BF)
        if k > 1:
            behind = (
                lax.ppermute(behind, "z", backward).astype(F32) + sums[depth - k + 1].astype(F32)
            ).astype(BF)
    share = (
        sums[0].astype(F32)
        + lax.ppermute(ahead, "z", onward).astype(F32)
        + lax.ppermute(behind, "z", backward).astype(F32)
    )
    flag = share[0, 0] > 0.5 * OVER
    new_first, new_second, new_part = adam_rows(old_rows, share, first_moment, second_moment)
    new_parts = spread(new_part)

    chunks = 4
    layer_out = call(
        out_kernel,
        jax.ShapeDtypeStruct((tok, out_width), BF),
        48,
        in_specs=[vmem] * 4 + [hbm],
        out_specs=hbm,
        scratch=[
            pltpu.VMEM(projectors.shape, BF),
            pltpu.VMEM((proj_count, tok, width), F32),
            pltpu.VMEM((chunks, tok, out_width // chunks), BF),
            pltpu.SemaphoreType.DMA((proj_count,)),
            pltpu.SemaphoreType.DMA((chunks,)),
        ],
        cost=cost(2 * width * (tok * proj_count * out_width + slots * total), 13000000),
    )(slot_col, pcol, wcol, returned, projectors)
    return flag, (layer_out, new_parts, new_first, new_second)


def on_device(*args):
    flag, outs = short_way(*args)
    return lax.cond(
        flag, lambda given, done: long_way(*given), lambda given, done: joined(done), args, outs
    )


def solution(mesh):
    mem, dp = mesh.devices.shape
    grid = Mesh(
        mesh.devices.reshape(mem // (Z_CHIPS * CORES), Z_CHIPS, CORES, dp), ("y", "z", "c", "x")
    )
    every = P(("y", "z", "c", "x"), None)
    slab = P(("y", "z", "c"), None)
    return jax.shard_map(
        on_device,
        mesh=grid,
        in_specs=(every, every, every, slab, every, every, P()),
        out_specs=(every, slab, every, every),
        check_vma=False,
    )
```

```python
import functools

import jax
import jax.numpy as jnp
from jax import lax
from jax.experimental import pallas as pl
from jax.experimental.pallas import tpu as pltpu
from jax.sharding import Mesh
from jax.sharding import PartitionSpec as P

beta_one = 0.9
beta_two = 0.999
corr_one = 1.0 - 0.9**50
corr_two = 1.0 - 0.999**50
learn_rate = 0.05
adam_eps = 1e-08

Z_CHIPS = 8
CORES = 2
CAP = 72
LANES = 128
OVER = 1e30
BF = jnp.bfloat16
F32 = jnp.float32
NT = (((1,), (1,)), ((), ()))


def adam_rows(old_rows, slab_grad, first_moment, second_moment):
    new_first = beta_one * first_moment + (1.0 - beta_one) * slab_grad
    new_second = beta_two * second_moment + (1.0 - beta_two) * slab_grad * slab_grad
    update_step = new_first / corr_one / (jnp.sqrt(new_second / corr_two) + adam_eps)
    updated = (old_rows.astype(jnp.float32) - learn_rate * update_step).astype(jnp.bfloat16)
    return (new_first, new_second, updated)


def spread(new_part):
    parts = lax.axis_size("x")
    return [new_part] + [
        lax.ppermute(new_part, "x", [(i, (i + k) % parts) for i in range(parts)])
        for k in range(1, parts)
    ]


def joined(outs):
    layer_out, new_parts, new_first, new_second = outs
    parts = len(new_parts)
    x_here = lax.axis_index("x")
    new_values = jnp.zeros((parts, *new_parts[0].shape), BF)
    for k, piece in enumerate(new_parts):
        mine = jnp.arange(parts) == lax.rem(x_here + parts - k, parts)
        new_values = jnp.where(mine[:, None, None], piece[None], new_values)
    return layer_out, new_values.reshape(-1, new_values.shape[2]), new_first, new_second


def long_way(picks, pick_weights, token_grads, values, first_moment, second_moment, projectors):
    mem = ("y", "z", "c")
    owners = lax.axis_size(mem)
    rows_dev, width = values.shape
    tok_count, per_token = picks.shape
    proj_count, _, out_width = projectors.shape
    total_picks = tok_count * per_token
    capacity = 2 * total_picks // owners
    slots = owners * capacity
    swap = lambda rows: lax.all_to_all(rows, mem, split_axis=0, concat_axis=0, tiled=True)
    flat_picks = picks.reshape(-1)
    owner_ids = flat_picks // rows_dev
    local_rows = flat_picks - owner_ids * rows_dev
    member = (owner_ids[:, None] == jnp.arange(owners, dtype=jnp.int32)[None, :]).astype(jnp.int32)
    before = jnp.cumsum(member, axis=0) - member
    slot_ids = owner_ids * capacity + jnp.sum(before * member, axis=1)
    number = jnp.arange(total_picks, dtype=jnp.int32)
    pick_in = jnp.full((slots,), total_picks, jnp.int32).at[slot_ids].set(number)
    in_slots = lambda per_pick: jnp.concatenate([per_pick, jnp.zeros((1,), per_pick.dtype)])[pick_in]
    proj_ids = picks % proj_count
    requests = in_slots(local_rows).reshape(owners, capacity)
    received = swap(requests)
    returned = swap(values[received])
    _, back_grads = lax.scan(
        lambda none, proj: (
            none,
            lax.dot_general(token_grads, proj, NT, preferred_element_type=F32).astype(BF),
        ),
        0,
        projectors,
    )
    back_rows = in_slots(proj_ids.reshape(-1) * tok_count + number // per_token)
    send_rows = back_grads.reshape(proj_count * tok_count, width)[back_rows]
    got_rows = swap(send_rows.reshape(owners, capacity, width)).reshape(slots, width)
    got_wts = swap(in_slots(pick_weights.reshape(-1)).reshape(owners, capacity)).reshape(slots)
    picked = returned.reshape(slots, width)[slot_ids].reshape(tok_count, per_token, width)
    mixing = jnp.where(
        proj_ids[..., None] == jnp.arange(proj_count, dtype=jnp.int32),
        pick_weights[..., None],
        jnp.zeros((), BF),
    )
    proj_sums = jnp.einsum("tjp,tjd->ptd", mixing, picked, preferred_element_type=F32).astype(BF)
    layer_out, _ = lax.scan(
        lambda acc, part: (acc + jnp.dot(*part, preferred_element_type=F32), None),
        jnp.zeros((tok_count, out_width), F32),
        (proj_sums, projectors),
    )
    chunk = slots // 20

    def add_chunk(acc, part):
        ids, wts, rows = part
        place = jnp.arange(rows_dev, dtype=jnp.int32)[:, None] == ids[None, :]
        place = jnp.where(place, wts[None, :], jnp.zeros((), BF))
        return acc + jnp.dot(place, rows, preferred_element_type=F32), None

    slab_grad, _ = lax.scan(
        add_chunk,
        jnp.zeros((rows_dev, width), F32),
        (
            received.reshape(-1, chunk),
            got_wts.reshape(-1, chunk),
            got_rows.reshape(-1, chunk, width),
        ),
    )
    quarter = first_moment.shape[0]
    share = jnp.sum(
        lax.all_to_all(
            slab_grad.reshape(-1, quarter, width), "x", split_axis=0, concat_axis=0, tiled=True
        ),
        axis=0,
    )
    old_rows = lax.dynamic_slice_in_dim(values, lax.axis_index("x") * quarter, quarter, 0)
    new_first, new_second, new_part = adam_rows(old_rows, share, first_moment, second_moment)
    return joined((layer_out.astype(BF), spread(new_part), new_first, new_second))


def call(kernel, out_shape, vmem, grid=None, in_specs=None, out_specs=None, scratch=(), cost=None):
    extra = {} if grid is None else {"grid": grid}
    if in_specs is not None:
        extra["in_specs"] = in_specs
    if out_specs is not None:
        extra["out_specs"] = out_specs
    return pl.pallas_call(
        kernel,
        out_shape=out_shape,
        scratch_shapes=list(scratch),
        compiler_params=pltpu.CompilerParams(vmem_limit_bytes=vmem * 1024 * 1024),
        cost_estimate=cost,
        **extra,
    )


def cost(flops, nbytes):
    return pl.CostEstimate(flops=flops, bytes_accessed=nbytes, transcendentals=0)


def rank_kernel(
    sizes, pick_ref, wt_ref, cell_ref, rank_ref, wrow_ref, req_ref, pcol_ref, slot_ref, wcol_ref
):
    cells, depth, parts, rows_dev, proj_count = sizes
    per_token, tok = pick_ref.shape
    count = per_token * tok
    quarter = rows_dev // parts
    block = 256
    by_token = pick_ref[...]
    flat = jnp.concatenate([by_token[j : j + 1] for j in range(per_token)], axis=1)
    weights = wt_ref[...].astype(F32)
    wrow_ref[...] = jnp.concatenate([weights[j : j + 1] for j in range(per_token)], axis=1)
    owner = lax.div(flat, rows_dev)
    row = lax.rem(flat, rows_dev)
    owner_z = lax.rem(lax.div(owner, CORES), depth)
    cells_row = (
        lax.div(owner, depth * CORES) * CORES + lax.rem(owner, CORES)
    ) * parts + lax.div(row, quarter)
    trows = owner_z * quarter + lax.rem(row, quarter)
    cell_ref[...] = cells_row
    below = lax.broadcasted_iota(jnp.int32, (block, block), 0) < lax.broadcasted_iota(
        jnp.int32, (block, block), 1
    )
    below = below.astype(F32).astype(BF)
    carry = jnp.zeros((cells, 1), F32)
    asked = jnp.zeros((3 * cells, LANES), F32)
    ranks = []
    for b in range(count // block):
        cell = cells_row[:, b * block : (b + 1) * block]
        trow = trows[:, b * block : (b + 1) * block]
        here = (lax.broadcasted_iota(jnp.int32, (cells, block), 0) == cell).astype(F32)
        before = jnp.dot(here.astype(BF), below, preferred_element_type=F32) + carry
        carry = carry + jnp.sum(here, axis=1, keepdims=True)
        rank = jnp.sum(here * before, axis=0, keepdims=True).astype(jnp.int32)
        ranks.append(rank)
        place = (lax.broadcasted_iota(jnp.int32, (LANES, block), 0) == rank).astype(F32)
        high = (trow >> 5).astype(F32)
        low = (trow & 31).astype(F32)
        told = jnp.concatenate([here, here * high, here * low], axis=0)
        asked = asked + lax.dot_general(
            told.astype(BF), place.astype(BF), NT, preferred_element_type=F32
        )
    there = asked[:cells]
    rows = (asked[cells : 2 * cells] * 32.0 + asked[2 * cells :]).astype(jnp.int32)
    rows = jnp.where(there > 0.5, rows, -1)
    lane = lax.broadcasted_iota(jnp.int32, (cells, LANES), 1)
    over = (jnp.max(carry) > CAP).astype(jnp.int32)
    req_ref[...] = jnp.where(lane == LANES - 1, over, rows)
    rank_row = jnp.concatenate(ranks, axis=1)
    rank_ref[...] = rank_row
    slots = cells_row * CAP + rank_row
    by_row = jnp.concatenate([slots[:, j * tok : (j + 1) * tok] for j in range(per_token)], axis=0)
    slot_ref[...] = by_row.T
    pcol_ref[...] = lax.rem(by_token, proj_count).T
    wcol_ref[...] = weights.T


def send_kernel(
    group,
    tg_ref,
    proj_ref,
    pcol_ref,
    cell_ref,
    rank_ref,
    wt_ref,
    out_ref,
    grads,
    projs,
    chosen,
    made,
    in_sems,
    out_sems,
):
    tok, per_token = pcol_ref.shape
    count = cell_ref.shape[1]
    proj_count = proj_ref.shape[0]
    come = [pltpu.make_async_copy(tg_ref, grads, in_sems.at[proj_count])]
    for p in range(proj_count):
        come.append(pltpu.make_async_copy(proj_ref.at[p], projs.at[p], in_sems.at[p]))
    for copy in come:
        copy.start()
    at = lax.broadcasted_iota(jnp.int32, (CAP, count), 0) == rank_ref[...]
    place = jnp.where(at, wt_ref[...], 0.0).astype(BF)
    come[0].wait()
    for p in range(proj_count):
        come[p + 1].wait()
        back = lax.dot_general(grads[...], projs[p], NT, preferred_element_type=F32).astype(BF)
        for j in range(per_token):
            span = pl.ds(j * tok, tok)
            if p == 0:
                chosen[span, :] = back
            else:
                chosen[span, :] = jnp.where(pcol_ref[:, j : j + 1] == p, back, chosen[span, :])
    copies = []
    for g in range(made.shape[0] // (group * CAP)):
        parts = []
        for d in range(group):
            here = (cell_ref[...] == g * group + d).astype(F32).astype(BF)
            parts.append(place * here)
        pick = jnp.concatenate(parts, axis=0)
        span = pl.ds(g * group * CAP, group * CAP)
        made[span, :] = jnp.dot(pick, chosen[...], preferred_element_type=F32).astype(BF)
        copies.append(pltpu.make_async_copy(made.at[span, :], out_ref.at[span, :], out_sems.at[g]))
        copies[-1].start()
    for copy in copies:
        copy.wait()


def look_kernel(group, got_ref, z_ref, *refs):
    *pieces, out_ref, table, made, in_sems, out_sems = refs
    rows = pieces[0].shape[0]
    cells = got_ref.shape[0]
    depth = len(pieces)
    come = [
        pltpu.make_async_copy(piece, table.at[pl.ds(k * rows, rows), :], in_sems.at[k])
        for k, piece in enumerate(pieces)
    ]
    for copy in come:
        copy.start()
    told = got_ref[...]
    from_z = lax.rem(lax.div(told, rows) + depth - z_ref[0], depth)
    asked = jnp.where(told < 0, -1, from_z * rows + lax.rem(told, rows)).T
    lane = lax.broadcasted_iota(jnp.int32, (CAP, depth * rows), 1)
    for copy in come:
        copy.wait()
    copies = []
    for g in range(cells // group):
        parts = []
        for d in range(g * group, (g + 1) * group):
            parts.append((lane == asked[:CAP, d : d + 1]).astype(F32).astype(BF))
        pick = jnp.concatenate(parts, axis=0)
        span = pl.ds(g * group * CAP, group * CAP)
        made[span, :] = jnp.dot(pick, table[...], preferred_element_type=F32).astype(BF)
        copies.append(pltpu.make_async_copy(made.at[span, :], out_ref.at[span, :], out_sems.at[g]))
        copies[-1].start()
    for copy in copies:
        copy.wait()


def sum_kernel(ids_ref, flags_ref, got_ref, *out_refs):
    rows = out_refs[0].shape[0]
    slots = ids_ref.shape[1]
    over = jnp.where(jnp.max(flags_ref[...]) > 0, OVER, 0.0)
    for k, out_ref in enumerate(out_refs):
        pick = lax.broadcasted_iota(jnp.int32, (rows, slots), 0) == ids_ref[...] - k * rows
        part = jnp.dot(pick.astype(F32).astype(BF), got_ref[...], preferred_element_type=F32)
        out_ref[...] = (part + over).astype(out_ref.dtype)


def out_kernel(
    slot_ref, pcol_ref, wcol_ref, ret_ref, proj_ref, out_ref, projs, made, in_sems, out_sems
):
    tok, per_token = slot_ref.shape
    slots = ret_ref.shape[0]
    proj_count, width, out_width = proj_ref.shape
    chunks = made.shape[0]
    chunk = out_width // chunks
    spans = [pl.ds(n * chunk, chunk) for n in range(chunks)]
    come = [
        pltpu.make_async_copy(proj_ref.at[:, :, span], projs.at[:, :, span], in_sems.at[n])
        for n, span in enumerate(spans)
    ]
    for copy in come:
        copy.start()
    lane = lax.broadcasted_iota(jnp.int32, (tok, slots), 1)
    pick = [(lane == slot_ref[:, j : j + 1]).astype(F32).astype(BF) for j in range(per_token)]
    rows = jnp.dot(jnp.concatenate(pick, axis=0), ret_ref[...], preferred_element_type=F32)
    sums = []
    for p in range(proj_count):
        weight = [
            jnp.where(pcol_ref[:, j : j + 1] == p, wcol_ref[:, j : j + 1], 0.0)
            for j in range(per_token)
        ]
        parts = [rows[j * tok : (j + 1) * tok] * weight[j] for j in range(per_token)]
        sums.append(functools.reduce(lambda a, b: a + b, parts).astype(BF))
    mixed = jnp.concatenate(sums, axis=1)
    copies = []
    for n, span in enumerate(spans):
        come[n].wait()
        made[n] = jnp.dot(
            mixed,
            projs[:, :, span].reshape(proj_count * width, chunk),
            preferred_element_type=F32,
        ).astype(BF)
        copies.append(pltpu.make_async_copy(made.at[n], out_ref.at[:, span], out_sems.at[n]))
        copies[-1].start()
    for copy in copies:
        copy.wait()


def short_way(picks, pick_weights, token_grads, values, first_moment, second_moment, projectors):
    plane = ("y", "c", "x")
    cells = lax.axis_size(plane)
    depth = lax.axis_size("z")
    parts = lax.axis_size("x")
    rows_dev, width = values.shape
    quarter = rows_dev // parts
    tok, per_token = picks.shape
    proj_count, _, out_width = projectors.shape
    total = tok * per_token
    slots = cells * CAP
    table_rows = depth * quarter
    start = lax.axis_index("x") * quarter
    old_rows = lax.dynamic_slice_in_dim(values, start, quarter, 0)

    hbm = pl.BlockSpec(memory_space=pl.ANY)
    vmem = pl.BlockSpec(memory_space=pltpu.VMEM)
    i32 = lambda *shape: jax.ShapeDtypeStruct(shape, jnp.int32)
    f32 = lambda *shape: jax.ShapeDtypeStruct(shape, F32)
    cell, rank, wt_row, requests, pcol, slot_col, wcol = call(
        functools.partial(rank_kernel, (cells, depth, parts, rows_dev, proj_count)),
        (
            i32(1, total),
            i32(1, total),
            f32(1, total),
            i32(cells, LANES),
            i32(tok, per_token),
            i32(tok, per_token),
            f32(tok, per_token),
        ),
        60,
        in_specs=[vmem] * 2,
        out_specs=(vmem,) * 7,
        cost=cost(2 * total * cells * 400, 20000),
    )(picks.T, pick_weights.T)
    received = lax.all_to_all(requests, plane, split_axis=0, concat_axis=0, tiled=True)

    onward = [(i, (i + 1) % depth) for i in range(depth)]
    backward = [(i, (i - 1) % depth) for i in range(depth)]
    pieces = [old_rows] + [None] * (depth - 1)
    for k in range(1, depth // 2 + 1):
        pieces[k] = lax.ppermute(pieces[k - 1], "z", backward)
        if k < depth // 2:
            pieces[depth - k] = lax.ppermute(pieces[(depth - k + 1) % depth], "z", onward)
        if k == 1:
            rank, pieces[1], pieces[depth - 1] = lax.optimization_barrier(
                (rank, pieces[1], pieces[depth - 1])
            )

    group = 8
    sent = call(
        functools.partial(send_kernel, group),
        jax.ShapeDtypeStruct((slots, width), BF),
        60,
        in_specs=[hbm] * 2 + [vmem] * 4,
        out_specs=hbm,
        scratch=[
            pltpu.VMEM((tok, out_width), BF),
            pltpu.VMEM(projectors.shape, BF),
            pltpu.VMEM((total, width), BF),
            pltpu.VMEM((slots, width), BF),
            pltpu.SemaphoreType.DMA((proj_count + 1,)),
            pltpu.SemaphoreType.DMA((cells // group,)),
        ],
        cost=cost(2 * width * (tok * proj_count * out_width + slots * total), 12000000),
    )(token_grads, projectors, pcol, cell, rank, wt_row)
    got = lax.all_to_all(
        sent.reshape(cells, CAP, width), plane, split_axis=0, concat_axis=0, tiled=True
    ).reshape(slots, width)

    z_here = lax.axis_index("z")
    told = received[:, :CAP]
    from_z = lax.rem(lax.div(told, quarter) + depth - z_here, depth)
    asked = jnp.where(told < 0, -1, from_z * quarter + lax.rem(told, quarter))
    flags = received[:, LANES - 1 :]
    looked = call(
        functools.partial(look_kernel, group),
        jax.ShapeDtypeStruct((slots, width), BF),
        60,
        in_specs=[vmem, pl.BlockSpec(memory_space=pltpu.SMEM)] + [hbm] * depth,
        out_specs=hbm,
        scratch=[
            pltpu.VMEM((table_rows, width), BF),
            pltpu.VMEM((slots, width), BF),
            pltpu.SemaphoreType.DMA((depth,)),
            pltpu.SemaphoreType.DMA((cells // group,)),
        ],
        cost=cost(2 * width * slots * table_rows, 4000000),
    )(received, z_here.reshape(1), *pieces)
    sums = call(
        sum_kernel,
        (jax.ShapeDtypeStruct((quarter, width), BF),) * depth,
        16,
        in_specs=[vmem] * 3,
        out_specs=(vmem,) * depth,
        cost=cost(2 * width * slots * table_rows, 4000000),
    )(asked.reshape(1, slots), flags, got)
    looked, *sums = lax.optimization_barrier((looked, *sums))
    returned = lax.all_to_all(
        looked.reshape(cells, CAP, width), plane, split_axis=0, concat_axis=0, tiled=True
    ).reshape(slots, width)

    ahead = sums[depth // 2]
    behind = sums[depth // 2 + 1]
    for k in range(depth // 2 - 1, 0, -1):
        ahead = (lax.ppermute(ahead, "z", onward).astype(F32) + sums[k].astype(F32)).astype(BF)
        if k > 1:
            behind = (
                lax.ppermute(behind, "z", backward).astype(F32) + sums[depth - k + 1].astype(F32)
            ).astype(BF)
    share = (
        sums[0].astype(F32)
        + lax.ppermute(ahead, "z", onward).astype(F32)
        + lax.ppermute(behind, "z", backward).astype(F32)
    )
    flag = share[0, 0] > 0.5 * OVER
    new_first, new_second, new_part = adam_rows(old_rows, share, first_moment, second_moment)
    new_parts = spread(new_part)

    chunks = 4
    layer_out = call(
        out_kernel,
        jax.ShapeDtypeStruct((tok, out_width), BF),
        48,
        in_specs=[vmem] * 4 + [hbm],
        out_specs=hbm,
        scratch=[
            pltpu.VMEM(projectors.shape, BF),
            pltpu.VMEM((chunks, tok, out_width // chunks), BF),
            pltpu.SemaphoreType.DMA((chunks,)),
            pltpu.SemaphoreType.DMA((chunks,)),
        ],
        cost=cost(2 * width * (tok * proj_count * out_width + slots * total), 13000000),
    )(slot_col, pcol, wcol, returned, projectors)
    return flag, (layer_out, new_parts, new_first, new_second)


def on_device(*args):
    flag, outs = short_way(*args)
    return lax.cond(
        flag, lambda given, done: long_way(*given), lambda given, done: joined(done), args, outs
    )


def solution(mesh):
    mem, dp = mesh.devices.shape
    grid = Mesh(
        mesh.devices.reshape(mem // (Z_CHIPS * CORES), Z_CHIPS, CORES, dp), ("y", "z", "c", "x")
    )
    every = P(("y", "z", "c", "x"), None)
    slab = P(("y", "z", "c"), None)
    return jax.shard_map(
        on_device,
        mesh=grid,
        in_specs=(every, every, every, slab, every, every, P()),
        out_specs=(every, slab, every, every),
        check_vma=False,
    )
```

```python
import functools

import jax
import jax.numpy as jnp
from jax import lax
from jax.experimental import pallas as pl
from jax.experimental.pallas import tpu as pltpu
from jax.sharding import Mesh
from jax.sharding import PartitionSpec as P

beta_one = 0.9
beta_two = 0.999
corr_one = 1.0 - 0.9**50
corr_two = 1.0 - 0.999**50
learn_rate = 0.05
adam_eps = 1e-08

Z_CHIPS = 8
CORES = 2
CAP = 72
LANES = 128
OVER = 1e30
BF = jnp.bfloat16
F32 = jnp.float32
NT = (((1,), (1,)), ((), ()))


def adam_rows(old_rows, slab_grad, first_moment, second_moment):
    new_first = beta_one * first_moment + (1.0 - beta_one) * slab_grad
    new_second = beta_two * second_moment + (1.0 - beta_two) * slab_grad * slab_grad
    update_step = new_first / corr_one / (jnp.sqrt(new_second / corr_two) + adam_eps)
    updated = (old_rows.astype(jnp.float32) - learn_rate * update_step).astype(jnp.bfloat16)
    return (new_first, new_second, updated)


def spread(new_part):
    parts = lax.axis_size("x")
    return [new_part] + [
        lax.ppermute(new_part, "x", [(i, (i + k) % parts) for i in range(parts)])
        for k in range(1, parts)
    ]


def joined(outs):
    layer_out, new_parts, new_first, new_second = outs
    parts = len(new_parts)
    x_here = lax.axis_index("x")
    new_values = jnp.zeros((parts, *new_parts[0].shape), BF)
    for k, piece in enumerate(new_parts):
        mine = jnp.arange(parts) == lax.rem(x_here + parts - k, parts)
        new_values = jnp.where(mine[:, None, None], piece[None], new_values)
    return layer_out, new_values.reshape(-1, new_values.shape[2]), new_first, new_second


def long_way(picks, pick_weights, token_grads, values, first_moment, second_moment, projectors):
    mem = ("y", "z", "c")
    owners = lax.axis_size(mem)
    rows_dev, width = values.shape
    tok_count, per_token = picks.shape
    proj_count, _, out_width = projectors.shape
    total_picks = tok_count * per_token
    capacity = 2 * total_picks // owners
    slots = owners * capacity
    swap = lambda rows: lax.all_to_all(rows, mem, split_axis=0, concat_axis=0, tiled=True)
    flat_picks = picks.reshape(-1)
    owner_ids = flat_picks // rows_dev
    local_rows = flat_picks - owner_ids * rows_dev
    member = (owner_ids[:, None] == jnp.arange(owners, dtype=jnp.int32)[None, :]).astype(jnp.int32)
    before = jnp.cumsum(member, axis=0) - member
    slot_ids = owner_ids * capacity + jnp.sum(before * member, axis=1)
    number = jnp.arange(total_picks, dtype=jnp.int32)
    pick_in = jnp.full((slots,), total_picks, jnp.int32).at[slot_ids].set(number)
    in_slots = lambda per_pick: jnp.concatenate([per_pick, jnp.zeros((1,), per_pick.dtype)])[pick_in]
    proj_ids = picks % proj_count
    requests = in_slots(local_rows).reshape(owners, capacity)
    received = swap(requests)
    returned = swap(values[received])
    _, back_grads = lax.scan(
        lambda none, proj: (
            none,
            lax.dot_general(token_grads, proj, NT, preferred_element_type=F32).astype(BF),
        ),
        0,
        projectors,
    )
    back_rows = in_slots(proj_ids.reshape(-1) * tok_count + number // per_token)
    send_rows = back_grads.reshape(proj_count * tok_count, width)[back_rows]
    got_rows = swap(send_rows.reshape(owners, capacity, width)).reshape(slots, width)
    got_wts = swap(in_slots(pick_weights.reshape(-1)).reshape(owners, capacity)).reshape(slots)
    picked = returned.reshape(slots, width)[slot_ids].reshape(tok_count, per_token, width)
    mixing = jnp.where(
        proj_ids[..., None] == jnp.arange(proj_count, dtype=jnp.int32),
        pick_weights[..., None],
        jnp.zeros((), BF),
    )
    proj_sums = jnp.einsum("tjp,tjd->ptd", mixing, picked, preferred_element_type=F32).astype(BF)
    layer_out, _ = lax.scan(
        lambda acc, part: (acc + jnp.dot(*part, preferred_element_type=F32), None),
        jnp.zeros((tok_count, out_width), F32),
        (proj_sums, projectors),
    )
    chunk = slots // 20

    def add_chunk(acc, part):
        ids, wts, rows = part
        place = jnp.arange(rows_dev, dtype=jnp.int32)[:, None] == ids[None, :]
        place = jnp.where(place, wts[None, :], jnp.zeros((), BF))
        return acc + jnp.dot(place, rows, preferred_element_type=F32), None

    slab_grad, _ = lax.scan(
        add_chunk,
        jnp.zeros((rows_dev, width), F32),
        (
            received.reshape(-1, chunk),
            got_wts.reshape(-1, chunk),
            got_rows.reshape(-1, chunk, width),
        ),
    )
    quarter = first_moment.shape[0]
    share = jnp.sum(
        lax.all_to_all(
            slab_grad.reshape(-1, quarter, width), "x", split_axis=0, concat_axis=0, tiled=True
        ),
        axis=0,
    )
    old_rows = lax.dynamic_slice_in_dim(values, lax.axis_index("x") * quarter, quarter, 0)
    new_first, new_second, new_part = adam_rows(old_rows, share, first_moment, second_moment)
    return joined((layer_out.astype(BF), spread(new_part), new_first, new_second))


def call(kernel, out_shape, vmem, grid=None, in_specs=None, out_specs=None, scratch=(), cost=None):
    extra = {} if grid is None else {"grid": grid}
    if in_specs is not None:
        extra["in_specs"] = in_specs
    if out_specs is not None:
        extra["out_specs"] = out_specs
    return pl.pallas_call(
        kernel,
        out_shape=out_shape,
        scratch_shapes=list(scratch),
        compiler_params=pltpu.CompilerParams(vmem_limit_bytes=vmem * 1024 * 1024),
        cost_estimate=cost,
        **extra,
    )


def cost(flops, nbytes):
    return pl.CostEstimate(flops=flops, bytes_accessed=nbytes, transcendentals=0)


def rank_kernel(
    sizes, pick_ref, wt_ref, cell_ref, rank_ref, wrow_ref, req_ref, pcol_ref, slot_ref, wcol_ref
):
    cells, depth, parts, rows_dev, proj_count = sizes
    per_token, tok = pick_ref.shape
    count = per_token * tok
    quarter = rows_dev // parts
    block = 256
    by_token = pick_ref[...]
    flat = jnp.concatenate([by_token[j : j + 1] for j in range(per_token)], axis=1)
    weights = wt_ref[...].astype(F32)
    wrow_ref[...] = jnp.concatenate([weights[j : j + 1] for j in range(per_token)], axis=1)
    owner = lax.div(flat, rows_dev)
    row = lax.rem(flat, rows_dev)
    owner_z = lax.rem(lax.div(owner, CORES), depth)
    cells_row = (
        lax.div(owner, depth * CORES) * CORES + lax.rem(owner, CORES)
    ) * parts + lax.div(row, quarter)
    trows = owner_z * quarter + lax.rem(row, quarter)
    cell_ref[...] = cells_row
    below = lax.broadcasted_iota(jnp.int32, (block, block), 0) < lax.broadcasted_iota(
        jnp.int32, (block, block), 1
    )
    below = below.astype(F32).astype(BF)
    carry = jnp.zeros((cells, 1), F32)
    asked = jnp.zeros((3 * cells, LANES), F32)
    ranks = []
    for b in range(count // block):
        cell = cells_row[:, b * block : (b + 1) * block]
        trow = trows[:, b * block : (b + 1) * block]
        here = (lax.broadcasted_iota(jnp.int32, (cells, block), 0) == cell).astype(F32)
        before = jnp.dot(here.astype(BF), below, preferred_element_type=F32) + carry
        carry = carry + jnp.sum(here, axis=1, keepdims=True)
        rank = jnp.sum(here * before, axis=0, keepdims=True).astype(jnp.int32)
        ranks.append(rank)
        place = (lax.broadcasted_iota(jnp.int32, (LANES, block), 0) == rank).astype(F32)
        high = (trow >> 5).astype(F32)
        low = (trow & 31).astype(F32)
        told = jnp.concatenate([here, here * high, here * low], axis=0)
        asked = asked + lax.dot_general(
            told.astype(BF), place.astype(BF), NT, preferred_element_type=F32
        )
    there = asked[:cells]
    rows = (asked[cells : 2 * cells] * 32.0 + asked[2 * cells :]).astype(jnp.int32)
    rows = jnp.where(there > 0.5, rows, -1)
    lane = lax.broadcasted_iota(jnp.int32, (cells, LANES), 1)
    over = (jnp.max(carry) > CAP).astype(jnp.int32)
    req_ref[...] = jnp.where(lane == LANES - 1, over, rows)
    rank_row = jnp.concatenate(ranks, axis=1)
    rank_ref[...] = rank_row
    slots = cells_row * CAP + rank_row
    by_row = jnp.concatenate([slots[:, j * tok : (j + 1) * tok] for j in range(per_token)], axis=0)
    slot_ref[...] = by_row.T
    pcol_ref[...] = lax.rem(by_token, proj_count).T
    wcol_ref[...] = weights.T


def send_kernel(
    group, projs, tg_ref, proj_ref, pcol_ref, cell_ref, rank_ref, wt_ref, out_ref, chosen, place
):
    step = pl.program_id(0)
    tok, per_token = pcol_ref.shape

    @pl.when(step == 0)
    def _():
        count = cell_ref.shape[1]
        at = lax.broadcasted_iota(jnp.int32, (CAP, count), 0) == rank_ref[...]
        place[...] = jnp.where(at, wt_ref[...], 0.0).astype(BF)

    @pl.when(step < projs)
    def _():
        back = lax.dot_general(tg_ref[...], proj_ref[0], NT, preferred_element_type=F32)
        back = back.astype(BF)
        for j in range(per_token):
            mine = (pcol_ref[:, j : j + 1] == step) | (step == 0)
            span = pl.ds(j * tok, tok)
            chosen[span, :] = jnp.where(mine, back, chosen[span, :])

    @pl.when(step >= projs)
    def _():
        first = (step - projs) * group
        parts = []
        for d in range(group):
            here = (cell_ref[...] == first + d).astype(F32).astype(BF)
            parts.append(place[...] * here)
        pick = jnp.concatenate(parts, axis=0)
        out_ref[...] = jnp.dot(pick, chosen[...], preferred_element_type=F32).astype(BF)


def look_kernel(group, got_ref, z_ref, *refs):
    *pieces, out_ref, table, ids = refs
    step = pl.program_id(0)
    rows = pieces[0].shape[0]
    depth = len(pieces)

    @pl.when(step == 0)
    def _():
        for k, piece in enumerate(pieces):
            table[pl.ds(k * rows, rows), :] = piece[...]
        told = got_ref[...]
        from_z = lax.rem(lax.div(told, rows) + depth - z_ref[0], depth)
        asked = jnp.where(told < 0, -1, from_z * rows + lax.rem(told, rows)).T
        for g in range(ids.shape[0]):
            ids[g] = asked[:, g * group : (g + 1) * group]

    lane = lax.broadcasted_iota(jnp.int32, (CAP, depth * rows), 1)
    mine = ids[step]
    parts = [(lane == mine[:CAP, d : d + 1]).astype(F32).astype(BF) for d in range(group)]
    pick = jnp.concatenate(parts, axis=0)
    out_ref[...] = jnp.dot(pick, table[...], preferred_element_type=F32).astype(BF)


def sum_kernel(ids_ref, flags_ref, got_ref, *out_refs):
    rows = out_refs[0].shape[0]
    slots = ids_ref.shape[1]
    over = jnp.where(jnp.max(flags_ref[...]) > 0, OVER, 0.0)
    for k, out_ref in enumerate(out_refs):
        pick = lax.broadcasted_iota(jnp.int32, (rows, slots), 0) == ids_ref[...] - k * rows
        part = jnp.dot(pick.astype(F32).astype(BF), got_ref[...], preferred_element_type=F32)
        out_ref[...] = (part + over).astype(out_ref.dtype)


def out_kernel(slot_ref, pcol_ref, wcol_ref, ret_ref, proj_ref, out_ref, mixed):
    tok, per_token = slot_ref.shape
    slots, width = ret_ref.shape
    proj_count = proj_ref.shape[0]

    @pl.when(pl.program_id(0) == 0)
    def _():
        lane = lax.broadcasted_iota(jnp.int32, (tok, slots), 1)
        pick = [(lane == slot_ref[:, j : j + 1]).astype(F32).astype(BF) for j in range(per_token)]
        rows = jnp.dot(jnp.concatenate(pick, axis=0), ret_ref[...], preferred_element_type=F32)
        for p in range(proj_count):
            weight = [
                jnp.where(pcol_ref[:, j : j + 1] == p, wcol_ref[:, j : j + 1], 0.0)
                for j in range(per_token)
            ]
            parts = [rows[j * tok : (j + 1) * tok] * weight[j] for j in range(per_token)]
            sums = functools.reduce(lambda a, b: a + b, parts)
            mixed[:, p * width : (p + 1) * width] = sums.astype(BF)

    out_ref[...] = jnp.dot(
        mixed[...],
        proj_ref[...].reshape(proj_count * width, proj_ref.shape[2]),
        preferred_element_type=F32,
    ).astype(BF)


def short_way(picks, pick_weights, token_grads, values, first_moment, second_moment, projectors):
    plane = ("y", "c", "x")
    cells = lax.axis_size(plane)
    depth = lax.axis_size("z")
    parts = lax.axis_size("x")
    rows_dev, width = values.shape
    quarter = rows_dev // parts
    tok, per_token = picks.shape
    proj_count, _, out_width = projectors.shape
    total = tok * per_token
    slots = cells * CAP
    table_rows = depth * quarter
    start = lax.axis_index("x") * quarter
    old_rows = lax.dynamic_slice_in_dim(values, start, quarter, 0)

    vmem = pl.BlockSpec(memory_space=pltpu.VMEM)
    i32 = lambda *shape: jax.ShapeDtypeStruct(shape, jnp.int32)
    f32 = lambda *shape: jax.ShapeDtypeStruct(shape, F32)
    cell, rank, wt_row, requests, pcol, slot_col, wcol = call(
        functools.partial(rank_kernel, (cells, depth, parts, rows_dev, proj_count)),
        (
            i32(1, total),
            i32(1, total),
            f32(1, total),
            i32(cells, LANES),
            i32(tok, per_token),
            i32(tok, per_token),
            f32(tok, per_token),
        ),
        60,
        in_specs=[vmem] * 2,
        out_specs=(vmem,) * 7,
        cost=cost(2 * total * cells * 400, 20000),
    )(picks.T, pick_weights.T)
    received = lax.all_to_all(requests, plane, split_axis=0, concat_axis=0, tiled=True)

    onward = [(i, (i + 1) % depth) for i in range(depth)]
    backward = [(i, (i - 1) % depth) for i in range(depth)]
    pieces = [old_rows] + [None] * (depth - 1)
    for k in range(1, depth // 2 + 1):
        pieces[k] = lax.ppermute(pieces[k - 1], "z", backward)
        if k < depth // 2:
            pieces[depth - k] = lax.ppermute(pieces[(depth - k + 1) % depth], "z", onward)

    group = 8
    whole = lambda *shape: pl.BlockSpec(shape, lambda i: (0,) * len(shape))
    sent = call(
        functools.partial(send_kernel, group, proj_count),
        jax.ShapeDtypeStruct((slots, width), BF),
        60,
        grid=(proj_count + cells // group,),
        in_specs=[
            whole(tok, out_width),
            pl.BlockSpec(
                (1, width, out_width), lambda i: (jnp.minimum(i, proj_count - 1), 0, 0)
            ),
            whole(tok, per_token),
            whole(1, total),
            whole(1, total),
            whole(1, total),
        ],
        out_specs=pl.BlockSpec(
            (group * CAP, width), lambda i: (jnp.maximum(i - proj_count, 0), 0)
        ),
        scratch=[pltpu.VMEM((total, width), BF), pltpu.VMEM((CAP, total), BF)],
        cost=cost(2 * width * (tok * proj_count * out_width + slots * total), 12000000),
    )(token_grads, projectors, pcol, cell, rank, wt_row)
    got = lax.all_to_all(
        sent.reshape(cells, CAP, width), plane, split_axis=0, concat_axis=0, tiled=True
    ).reshape(slots, width)

    z_here = lax.axis_index("z")
    told = received[:, :CAP]
    from_z = lax.rem(lax.div(told, quarter) + depth - z_here, depth)
    asked = jnp.where(told < 0, -1, from_z * quarter + lax.rem(told, quarter))
    flags = received[:, LANES - 1 :]
    looked = call(
        functools.partial(look_kernel, group),
        jax.ShapeDtypeStruct((slots, width), BF),
        60,
        grid=(cells // group,),
        in_specs=[whole(cells, LANES), pl.BlockSpec(memory_space=pltpu.SMEM)]
        + [whole(quarter, width)] * depth,
        out_specs=pl.BlockSpec((group * CAP, width), lambda i: (i, 0)),
        scratch=[
            pltpu.VMEM((table_rows, width), BF),
            pltpu.VMEM((cells // group, LANES, group), jnp.int32),
        ],
        cost=cost(2 * width * slots * table_rows, 4000000),
    )(received, z_here.reshape(1), *pieces)
    sums = call(
        sum_kernel,
        (jax.ShapeDtypeStruct((quarter, width), BF),) * depth,
        16,
        in_specs=[vmem] * 3,
        out_specs=(vmem,) * depth,
        cost=cost(2 * width * slots * table_rows, 4000000),
    )(asked.reshape(1, slots), flags, got)
    looked, *sums = lax.optimization_barrier((looked, *sums))
    returned = lax.all_to_all(
        looked.reshape(cells, CAP, width), plane, split_axis=0, concat_axis=0, tiled=True
    ).reshape(slots, width)

    ahead = sums[depth // 2]
    behind = sums[depth // 2 + 1]
    for k in range(depth // 2 - 1, 0, -1):
        ahead = (lax.ppermute(ahead, "z", onward).astype(F32) + sums[k].astype(F32)).astype(BF)
        if k > 1:
            behind = (
                lax.ppermute(behind, "z", backward).astype(F32) + sums[depth - k + 1].astype(F32)
            ).astype(BF)
    share = (
        sums[0].astype(F32)
        + lax.ppermute(ahead, "z", onward).astype(F32)
        + lax.ppermute(behind, "z", backward).astype(F32)
    )
    flag = share[0, 0] > 0.5 * OVER
    new_first, new_second, new_part = adam_rows(old_rows, share, first_moment, second_moment)
    new_parts = spread(new_part)

    chunk = out_width // 2
    layer_out = call(
        out_kernel,
        jax.ShapeDtypeStruct((tok, out_width), BF),
        48,
        grid=(out_width // chunk,),
        in_specs=[
            whole(tok, per_token),
            whole(tok, per_token),
            whole(tok, per_token),
            whole(slots, width),
            pl.BlockSpec((proj_count, width, chunk), lambda i: (0, 0, i)),
        ],
        out_specs=pl.BlockSpec((tok, chunk), lambda i: (0, i)),
        scratch=[pltpu.VMEM((tok, proj_count * width), BF)],
        cost=cost(2 * width * (tok * proj_count * out_width + slots * total), 13000000),
    )(slot_col, pcol, wcol, returned, projectors)
    return flag, (layer_out, new_parts, new_first, new_second)


def on_device(*args):
    flag, outs = short_way(*args)
    return lax.cond(
        flag, lambda given, done: long_way(*given), lambda given, done: joined(done), args, outs
    )


def solution(mesh):
    mem, dp = mesh.devices.shape
    grid = Mesh(
        mesh.devices.reshape(mem // (Z_CHIPS * CORES), Z_CHIPS, CORES, dp), ("y", "z", "c", "x")
    )
    every = P(("y", "z", "c", "x"), None)
    slab = P(("y", "z", "c"), None)
    return jax.shard_map(
        on_device,
        mesh=grid,
        in_specs=(every, every, every, slab, every, every, P()),
        out_specs=(every, slab, every, every),
        check_vma=False,
    )
```

```python
import functools

import jax
import jax.numpy as jnp
from jax import lax
from jax.experimental import pallas as pl
from jax.experimental.pallas import tpu as pltpu
from jax.sharding import Mesh
from jax.sharding import PartitionSpec as P

beta_one = 0.9
beta_two = 0.999
corr_one = 1.0 - 0.9**50
corr_two = 1.0 - 0.999**50
learn_rate = 0.05
adam_eps = 1e-08

Z_CHIPS = 8
CORES = 2
CAP = 80
LANES = 128
OVER = 1e30
BF = jnp.bfloat16
F32 = jnp.float32
NT = (((1,), (1,)), ((), ()))


def adam_rows(old_rows, slab_grad, first_moment, second_moment):
    new_first = beta_one * first_moment + (1.0 - beta_one) * slab_grad
    new_second = beta_two * second_moment + (1.0 - beta_two) * slab_grad * slab_grad
    update_step = new_first / corr_one / (jnp.sqrt(new_second / corr_two) + adam_eps)
    updated = (old_rows.astype(jnp.float32) - learn_rate * update_step).astype(jnp.bfloat16)
    return (new_first, new_second, updated)


def spread(new_part):
    parts = lax.axis_size("x")
    return [new_part] + [
        lax.ppermute(new_part, "x", [(i, (i + k) % parts) for i in range(parts)])
        for k in range(1, parts)
    ]


def joined(outs):
    layer_out, new_parts, new_first, new_second = outs
    parts = len(new_parts)
    x_here = lax.axis_index("x")
    new_values = jnp.zeros((parts, *new_parts[0].shape), BF)
    for k, piece in enumerate(new_parts):
        mine = jnp.arange(parts) == lax.rem(x_here + parts - k, parts)
        new_values = jnp.where(mine[:, None, None], piece[None], new_values)
    return layer_out, new_values.reshape(-1, new_values.shape[2]), new_first, new_second


def long_way(picks, pick_weights, token_grads, values, first_moment, second_moment, projectors):
    mem = ("y", "z", "c")
    owners = lax.axis_size(mem)
    rows_dev, width = values.shape
    tok_count, per_token = picks.shape
    proj_count, _, out_width = projectors.shape
    total_picks = tok_count * per_token
    capacity = 2 * total_picks // owners
    slots = owners * capacity
    swap = lambda rows: lax.all_to_all(rows, mem, split_axis=0, concat_axis=0, tiled=True)
    flat_picks = picks.reshape(-1)
    owner_ids = flat_picks // rows_dev
    local_rows = flat_picks - owner_ids * rows_dev
    member = (owner_ids[:, None] == jnp.arange(owners, dtype=jnp.int32)[None, :]).astype(jnp.int32)
    before = jnp.cumsum(member, axis=0) - member
    slot_ids = owner_ids * capacity + jnp.sum(before * member, axis=1)
    number = jnp.arange(total_picks, dtype=jnp.int32)
    pick_in = jnp.full((slots,), total_picks, jnp.int32).at[slot_ids].set(number)
    in_slots = lambda per_pick: jnp.concatenate([per_pick, jnp.zeros((1,), per_pick.dtype)])[pick_in]
    proj_ids = picks % proj_count
    requests = in_slots(local_rows).reshape(owners, capacity)
    received = swap(requests)
    returned = swap(values[received])
    _, back_grads = lax.scan(
        lambda none, proj: (
            none,
            lax.dot_general(token_grads, proj, NT, preferred_element_type=F32).astype(BF),
        ),
        0,
        projectors,
    )
    back_rows = in_slots(proj_ids.reshape(-1) * tok_count + number // per_token)
    send_rows = back_grads.reshape(proj_count * tok_count, width)[back_rows]
    got_rows = swap(send_rows.reshape(owners, capacity, width)).reshape(slots, width)
    got_wts = swap(in_slots(pick_weights.reshape(-1)).reshape(owners, capacity)).reshape(slots)
    picked = returned.reshape(slots, width)[slot_ids].reshape(tok_count, per_token, width)
    mixing = jnp.where(
        proj_ids[..., None] == jnp.arange(proj_count, dtype=jnp.int32),
        pick_weights[..., None],
        jnp.zeros((), BF),
    )
    proj_sums = jnp.einsum("tjp,tjd->ptd", mixing, picked, preferred_element_type=F32).astype(BF)
    layer_out, _ = lax.scan(
        lambda acc, part: (acc + jnp.dot(*part, preferred_element_type=F32), None),
        jnp.zeros((tok_count, out_width), F32),
        (proj_sums, projectors),
    )
    chunk = slots // 20

    def add_chunk(acc, part):
        ids, wts, rows = part
        place = jnp.arange(rows_dev, dtype=jnp.int32)[:, None] == ids[None, :]
        place = jnp.where(place, wts[None, :], jnp.zeros((), BF))
        return acc + jnp.dot(place, rows, preferred_element_type=F32), None

    slab_grad, _ = lax.scan(
        add_chunk,
        jnp.zeros((rows_dev, width), F32),
        (
            received.reshape(-1, chunk),
            got_wts.reshape(-1, chunk),
            got_rows.reshape(-1, chunk, width),
        ),
    )
    quarter = first_moment.shape[0]
    share = jnp.sum(
        lax.all_to_all(
            slab_grad.reshape(-1, quarter, width), "x", split_axis=0, concat_axis=0, tiled=True
        ),
        axis=0,
    )
    old_rows = lax.dynamic_slice_in_dim(values, lax.axis_index("x") * quarter, quarter, 0)
    new_first, new_second, new_part = adam_rows(old_rows, share, first_moment, second_moment)
    return joined((layer_out.astype(BF), spread(new_part), new_first, new_second))


def call(kernel, out_shape, vmem, grid=None, in_specs=None, out_specs=None, scratch=(), cost=None):
    extra = {} if grid is None else {"grid": grid}
    if in_specs is not None:
        extra["in_specs"] = in_specs
    if out_specs is not None:
        extra["out_specs"] = out_specs
    return pl.pallas_call(
        kernel,
        out_shape=out_shape,
        scratch_shapes=list(scratch),
        compiler_params=pltpu.CompilerParams(vmem_limit_bytes=vmem * 1024 * 1024),
        cost_estimate=cost,
        **extra,
    )


def cost(flops, nbytes):
    return pl.CostEstimate(flops=flops, bytes_accessed=nbytes, transcendentals=0)


def rank_kernel(
    sizes, pick_ref, wt_ref, cell_ref, rank_ref, wrow_ref, req_ref, pcol_ref, slot_ref, wcol_ref
):
    cells, depth, parts, rows_dev, proj_count = sizes
    per_token, tok = pick_ref.shape
    count = per_token * tok
    quarter = rows_dev // parts
    block = 256
    by_token = pick_ref[...]
    flat = jnp.concatenate([by_token[j : j + 1] for j in range(per_token)], axis=1)
    weights = wt_ref[...].astype(F32)
    wrow_ref[...] = jnp.concatenate([weights[j : j + 1] for j in range(per_token)], axis=1)
    owner = lax.div(flat, rows_dev)
    row = lax.rem(flat, rows_dev)
    owner_z = lax.rem(lax.div(owner, CORES), depth)
    cells_row = (
        lax.div(owner, depth * CORES) * CORES + lax.rem(owner, CORES)
    ) * parts + lax.div(row, quarter)
    trows = owner_z * quarter + lax.rem(row, quarter)
    cell_ref[...] = cells_row
    below = lax.broadcasted_iota(jnp.int32, (block, block), 0) < lax.broadcasted_iota(
        jnp.int32, (block, block), 1
    )
    below = below.astype(F32).astype(BF)
    carry = jnp.zeros((cells, 1), F32)
    asked = jnp.zeros((3 * cells, LANES), F32)
    ranks = []
    for b in range(count // block):
        cell = cells_row[:, b * block : (b + 1) * block]
        trow = trows[:, b * block : (b + 1) * block]
        here = (lax.broadcasted_iota(jnp.int32, (cells, block), 0) == cell).astype(F32)
        before = jnp.dot(here.astype(BF), below, preferred_element_type=F32) + carry
        carry = carry + jnp.sum(here, axis=1, keepdims=True)
        rank = jnp.sum(here * before, axis=0, keepdims=True).astype(jnp.int32)
        ranks.append(rank)
        place = (lax.broadcasted_iota(jnp.int32, (LANES, block), 0) == rank).astype(F32)
        high = (trow >> 5).astype(F32)
        low = (trow & 31).astype(F32)
        told = jnp.concatenate([here, here * high, here * low], axis=0)
        asked = asked + lax.dot_general(
            told.astype(BF), place.astype(BF), NT, preferred_element_type=F32
        )
    there = asked[:cells]
    rows = (asked[cells : 2 * cells] * 32.0 + asked[2 * cells :]).astype(jnp.int32)
    rows = jnp.where(there > 0.5, rows, -1)
    lane = lax.broadcasted_iota(jnp.int32, (cells, LANES), 1)
    over = (jnp.max(carry) > CAP).astype(jnp.int32)
    req_ref[...] = jnp.where(lane == LANES - 1, over, rows)
    rank_row = jnp.concatenate(ranks, axis=1)
    rank_ref[...] = rank_row
    slots = cells_row * CAP + rank_row
    by_row = jnp.concatenate([slots[:, j * tok : (j + 1) * tok] for j in range(per_token)], axis=0)
    slot_ref[...] = by_row.T
    pcol_ref[...] = lax.rem(by_token, proj_count).T
    wcol_ref[...] = weights.T


def send_kernel(
    group,
    tg_ref,
    proj_ref,
    pcol_ref,
    cell_ref,
    rank_ref,
    wt_ref,
    out_ref,
    grads,
    projs,
    chosen,
    made,
    in_sems,
    out_sems,
):
    tok, per_token = pcol_ref.shape
    count = cell_ref.shape[1]
    proj_count = proj_ref.shape[0]
    come = [pltpu.make_async_copy(tg_ref, grads, in_sems.at[proj_count])]
    for p in range(proj_count):
        come.append(pltpu.make_async_copy(proj_ref.at[p], projs.at[p], in_sems.at[p]))
    for copy in come:
        copy.start()
    at = lax.broadcasted_iota(jnp.int32, (CAP, count), 0) == rank_ref[...]
    place = jnp.where(at, wt_ref[...], 0.0).astype(BF)
    come[0].wait()
    for p in range(proj_count):
        come[p + 1].wait()
        back = lax.dot_general(grads[...], projs[p], NT, preferred_element_type=F32).astype(BF)
        for j in range(per_token):
            span = pl.ds(j * tok, tok)
            if p == 0:
                chosen[span, :] = back
            else:
                chosen[span, :] = jnp.where(pcol_ref[:, j : j + 1] == p, back, chosen[span, :])
    copies = []
    for g in range(made.shape[0] // (group * CAP)):
        parts = []
        for d in range(group):
            here = (cell_ref[...] == g * group + d).astype(F32).astype(BF)
            parts.append(place * here)
        pick = jnp.concatenate(parts, axis=0)
        span = pl.ds(g * group * CAP, group * CAP)
        made[span, :] = jnp.dot(pick, chosen[...], preferred_element_type=F32).astype(BF)
        copies.append(pltpu.make_async_copy(made.at[span, :], out_ref.at[span, :], out_sems.at[g]))
        copies[-1].start()
    for copy in copies:
        copy.wait()


def look_kernel(group, got_ref, z_ref, *refs):
    *pieces, out_ref, table, made, in_sems, out_sems = refs
    rows = pieces[0].shape[0]
    cells = got_ref.shape[0]
    depth = len(pieces)
    come = [
        pltpu.make_async_copy(piece, table.at[pl.ds(k * rows, rows), :], in_sems.at[k])
        for k, piece in enumerate(pieces)
    ]
    for copy in come:
        copy.start()
    told = got_ref[...]
    from_z = lax.rem(lax.div(told, rows) + depth - z_ref[0], depth)
    asked = jnp.where(told < 0, -1, from_z * rows + lax.rem(told, rows)).T
    lane = lax.broadcasted_iota(jnp.int32, (CAP, depth * rows), 1)
    for copy in come:
        copy.wait()
    copies = []
    for g in range(cells // group):
        parts = []
        for d in range(g * group, (g + 1) * group):
            parts.append((lane == asked[:CAP, d : d + 1]).astype(F32).astype(BF))
        pick = jnp.concatenate(parts, axis=0)
        span = pl.ds(g * group * CAP, group * CAP)
        made[span, :] = jnp.dot(pick, table[...], preferred_element_type=F32).astype(BF)
        copies.append(pltpu.make_async_copy(made.at[span, :], out_ref.at[span, :], out_sems.at[g]))
        copies[-1].start()
    for copy in copies:
        copy.wait()


def sum_kernel(ids_ref, flags_ref, got_ref, *out_refs):
    rows = out_refs[0].shape[0]
    slots = ids_ref.shape[1]
    over = jnp.where(jnp.max(flags_ref[...]) > 0, OVER, 0.0)
    for k, out_ref in enumerate(out_refs):
        pick = lax.broadcasted_iota(jnp.int32, (rows, slots), 0) == ids_ref[...] - k * rows
        part = jnp.dot(pick.astype(F32).astype(BF), got_ref[...], preferred_element_type=F32)
        out_ref[...] = (part + over).astype(out_ref.dtype)


def out_kernel(
    slot_ref, pcol_ref, wcol_ref, ret_ref, proj_ref, out_ref, projs, made, in_sems, out_sems
):
    tok, per_token = slot_ref.shape
    slots = ret_ref.shape[0]
    proj_count, width, out_width = proj_ref.shape
    chunks = made.shape[0]
    chunk = out_width // chunks
    spans = [pl.ds(n * chunk, chunk) for n in range(chunks)]
    come = [
        pltpu.make_async_copy(proj_ref.at[:, :, span], projs.at[:, :, span], in_sems.at[n])
        for n, span in enumerate(spans)
    ]
    for copy in come:
        copy.start()
    lane = lax.broadcasted_iota(jnp.int32, (tok, slots), 1)
    pick = [(lane == slot_ref[:, j : j + 1]).astype(F32).astype(BF) for j in range(per_token)]
    rows = jnp.dot(jnp.concatenate(pick, axis=0), ret_ref[...], preferred_element_type=F32)
    sums = []
    for p in range(proj_count):
        weight = [
            jnp.where(pcol_ref[:, j : j + 1] == p, wcol_ref[:, j : j + 1], 0.0)
            for j in range(per_token)
        ]
        parts = [rows[j * tok : (j + 1) * tok] * weight[j] for j in range(per_token)]
        sums.append(functools.reduce(lambda a, b: a + b, parts).astype(BF))
    mixed = jnp.concatenate(sums, axis=1)
    copies = []
    for n, span in enumerate(spans):
        come[n].wait()
        made[n] = jnp.dot(
            mixed,
            projs[:, :, span].reshape(proj_count * width, chunk),
            preferred_element_type=F32,
        ).astype(BF)
        copies.append(pltpu.make_async_copy(made.at[n], out_ref.at[:, span], out_sems.at[n]))
        copies[-1].start()
    for copy in copies:
        copy.wait()


def short_way(picks, pick_weights, token_grads, values, first_moment, second_moment, projectors):
    plane = ("y", "c", "x")
    cells = lax.axis_size(plane)
    depth = lax.axis_size("z")
    parts = lax.axis_size("x")
    rows_dev, width = values.shape
    quarter = rows_dev // parts
    tok, per_token = picks.shape
    proj_count, _, out_width = projectors.shape
    total = tok * per_token
    slots = cells * CAP
    table_rows = depth * quarter
    start = lax.axis_index("x") * quarter
    old_rows = lax.dynamic_slice_in_dim(values, start, quarter, 0)

    hbm = pl.BlockSpec(memory_space=pl.ANY)
    vmem = pl.BlockSpec(memory_space=pltpu.VMEM)
    i32 = lambda *shape: jax.ShapeDtypeStruct(shape, jnp.int32)
    f32 = lambda *shape: jax.ShapeDtypeStruct(shape, F32)
    cell, rank, wt_row, requests, pcol, slot_col, wcol = call(
        functools.partial(rank_kernel, (cells, depth, parts, rows_dev, proj_count)),
        (
            i32(1, total),
            i32(1, total),
            f32(1, total),
            i32(cells, LANES),
            i32(tok, per_token),
            i32(tok, per_token),
            f32(tok, per_token),
        ),
        60,
        in_specs=[vmem] * 2,
        out_specs=(vmem,) * 7,
        cost=cost(2 * total * cells * 400, 20000),
    )(picks.T, pick_weights.T)
    received = lax.all_to_all(requests, plane, split_axis=0, concat_axis=0, tiled=True)

    onward = [(i, (i + 1) % depth) for i in range(depth)]
    backward = [(i, (i - 1) % depth) for i in range(depth)]
    pieces = [old_rows] + [None] * (depth - 1)
    for k in range(1, depth // 2 + 1):
        pieces[k] = lax.ppermute(pieces[k - 1], "z", backward)
        if k < depth // 2:
            pieces[depth - k] = lax.ppermute(pieces[(depth - k + 1) % depth], "z", onward)

    group = 8
    sent = call(
        functools.partial(send_kernel, group),
        jax.ShapeDtypeStruct((slots, width), BF),
        60,
        in_specs=[hbm] * 2 + [vmem] * 4,
        out_specs=hbm,
        scratch=[
            pltpu.VMEM((tok, out_width), BF),
            pltpu.VMEM(projectors.shape, BF),
            pltpu.VMEM((total, width), BF),
            pltpu.VMEM((slots, width), BF),
            pltpu.SemaphoreType.DMA((proj_count + 1,)),
            pltpu.SemaphoreType.DMA((cells // group,)),
        ],
        cost=cost(2 * width * (tok * proj_count * out_width + slots * total), 12000000),
    )(token_grads, projectors, pcol, cell, rank, wt_row)
    got = lax.all_to_all(
        sent.reshape(cells, CAP, width), plane, split_axis=0, concat_axis=0, tiled=True
    ).reshape(slots, width)

    z_here = lax.axis_index("z")
    told = received[:, :CAP]
    from_z = lax.rem(lax.div(told, quarter) + depth - z_here, depth)
    asked = jnp.where(told < 0, -1, from_z * quarter + lax.rem(told, quarter))
    flags = received[:, LANES - 1 :]
    looked = call(
        functools.partial(look_kernel, group),
        jax.ShapeDtypeStruct((slots, width), BF),
        60,
        in_specs=[vmem, pl.BlockSpec(memory_space=pltpu.SMEM)] + [hbm] * depth,
        out_specs=hbm,
        scratch=[
            pltpu.VMEM((table_rows, width), BF),
            pltpu.VMEM((slots, width), BF),
            pltpu.SemaphoreType.DMA((depth,)),
            pltpu.SemaphoreType.DMA((cells // group,)),
        ],
        cost=cost(2 * width * slots * table_rows, 4000000),
    )(received, z_here.reshape(1), *pieces)
    sums = call(
        sum_kernel,
        (jax.ShapeDtypeStruct((quarter, width), BF),) * depth,
        16,
        in_specs=[vmem] * 3,
        out_specs=(vmem,) * depth,
        cost=cost(2 * width * slots * table_rows, 4000000),
    )(asked.reshape(1, slots), flags, got)
    looked, *sums = lax.optimization_barrier((looked, *sums))
    returned = lax.all_to_all(
        looked.reshape(cells, CAP, width), plane, split_axis=0, concat_axis=0, tiled=True
    ).reshape(slots, width)

    ahead = sums[depth // 2]
    behind = sums[depth // 2 + 1]
    for k in range(depth // 2 - 1, 0, -1):
        ahead = (lax.ppermute(ahead, "z", onward).astype(F32) + sums[k].astype(F32)).astype(BF)
        if k > 1:
            behind = (
                lax.ppermute(behind, "z", backward).astype(F32) + sums[depth - k + 1].astype(F32)
            ).astype(BF)
    share = (
        sums[0].astype(F32)
        + lax.ppermute(ahead, "z", onward).astype(F32)
        + lax.ppermute(behind, "z", backward).astype(F32)
    )
    flag = share[0, 0] > 0.5 * OVER
    new_first, new_second, new_part = adam_rows(old_rows, share, first_moment, second_moment)
    new_parts = spread(new_part)

    chunks = 4
    layer_out = call(
        out_kernel,
        jax.ShapeDtypeStruct((tok, out_width), BF),
        48,
        in_specs=[vmem] * 4 + [hbm],
        out_specs=hbm,
        scratch=[
            pltpu.VMEM(projectors.shape, BF),
            pltpu.VMEM((chunks, tok, out_width // chunks), BF),
            pltpu.SemaphoreType.DMA((chunks,)),
            pltpu.SemaphoreType.DMA((chunks,)),
        ],
        cost=cost(2 * width * (tok * proj_count * out_width + slots * total), 13000000),
    )(slot_col, pcol, wcol, returned, projectors)
    return flag, (layer_out, new_parts, new_first, new_second)


def on_device(*args):
    flag, outs = short_way(*args)
    return lax.cond(
        flag, lambda given, done: long_way(*given), lambda given, done: joined(done), args, outs
    )


def solution(mesh):
    mem, dp = mesh.devices.shape
    grid = Mesh(
        mesh.devices.reshape(mem // (Z_CHIPS * CORES), Z_CHIPS, CORES, dp), ("y", "z", "c", "x")
    )
    every = P(("y", "z", "c", "x"), None)
    slab = P(("y", "z", "c"), None)
    return jax.shard_map(
        on_device,
        mesh=grid,
        in_specs=(every, every, every, slab, every, every, P()),
        out_specs=(every, slab, every, every),
        check_vma=False,
    )
```

```python
import functools

import jax
import jax.numpy as jnp
from jax import lax
from jax.experimental import pallas as pl
from jax.experimental.pallas import tpu as pltpu
from jax.sharding import Mesh
from jax.sharding import PartitionSpec as P

beta_one = 0.9
beta_two = 0.999
corr_one = 1.0 - 0.9**50
corr_two = 1.0 - 0.999**50
learn_rate = 0.05
adam_eps = 1e-08

Z_CHIPS = 8
CORES = 2
CAP = 72
LANES = 128
OVER = 1e30
BF = jnp.bfloat16
F32 = jnp.float32
NT = (((1,), (1,)), ((), ()))


def adam_rows(old_rows, slab_grad, first_moment, second_moment):
    new_first = beta_one * first_moment + (1.0 - beta_one) * slab_grad
    new_second = beta_two * second_moment + (1.0 - beta_two) * slab_grad * slab_grad
    update_step = new_first / corr_one / (jnp.sqrt(new_second / corr_two) + adam_eps)
    updated = (old_rows.astype(jnp.float32) - learn_rate * update_step).astype(jnp.bfloat16)
    return (new_first, new_second, updated)


def spread(new_part):
    parts = lax.axis_size("x")
    return [new_part] + [
        lax.ppermute(new_part, "x", [(i, (i + k) % parts) for i in range(parts)])
        for k in range(1, parts)
    ]


def long_way(picks, pick_weights, token_grads, values, first_moment, second_moment, projectors):
    mem = ("y", "z", "c")
    owners = lax.axis_size(mem)
    rows_dev, width = values.shape
    tok_count, per_token = picks.shape
    proj_count, _, out_width = projectors.shape
    total_picks = tok_count * per_token
    capacity = 2 * total_picks // owners
    slots = owners * capacity
    swap = lambda rows: lax.all_to_all(rows, mem, split_axis=0, concat_axis=0, tiled=True)
    flat_picks = picks.reshape(-1)
    owner_ids = flat_picks // rows_dev
    local_rows = flat_picks - owner_ids * rows_dev
    member = (owner_ids[:, None] == jnp.arange(owners, dtype=jnp.int32)[None, :]).astype(jnp.int32)
    before = jnp.cumsum(member, axis=0) - member
    slot_ids = owner_ids * capacity + jnp.sum(before * member, axis=1)
    number = jnp.arange(total_picks, dtype=jnp.int32)
    pick_in = jnp.full((slots,), total_picks, jnp.int32).at[slot_ids].set(number)
    in_slots = lambda per_pick: jnp.concatenate([per_pick, jnp.zeros((1,), per_pick.dtype)])[pick_in]
    proj_ids = picks % proj_count
    requests = in_slots(local_rows).reshape(owners, capacity)
    received = swap(requests)
    returned = swap(values[received])
    _, back_grads = lax.scan(
        lambda none, proj: (
            none,
            lax.dot_general(token_grads, proj, NT, preferred_element_type=F32).astype(BF),
        ),
        0,
        projectors,
    )
    back_rows = in_slots(proj_ids.reshape(-1) * tok_count + number // per_token)
    send_rows = back_grads.reshape(proj_count * tok_count, width)[back_rows]
    got_rows = swap(send_rows.reshape(owners, capacity, width)).reshape(slots, width)
    got_wts = swap(in_slots(pick_weights.reshape(-1)).reshape(owners, capacity)).reshape(slots)
    picked = returned.reshape(slots, width)[slot_ids].reshape(tok_count, per_token, width)
    mixing = jnp.where(
        proj_ids[..., None] == jnp.arange(proj_count, dtype=jnp.int32),
        pick_weights[..., None],
        jnp.zeros((), BF),
    )
    proj_sums = jnp.einsum("tjp,tjd->ptd", mixing, picked, preferred_element_type=F32).astype(BF)
    layer_out, _ = lax.scan(
        lambda acc, part: (acc + jnp.dot(*part, preferred_element_type=F32), None),
        jnp.zeros((tok_count, out_width), F32),
        (proj_sums, projectors),
    )
    chunk = slots // 20

    def add_chunk(acc, part):
        ids, wts, rows = part
        place = jnp.arange(rows_dev, dtype=jnp.int32)[:, None] == ids[None, :]
        place = jnp.where(place, wts[None, :], jnp.zeros((), BF))
        return acc + jnp.dot(place, rows, preferred_element_type=F32), None

    slab_grad, _ = lax.scan(
        add_chunk,
        jnp.zeros((rows_dev, width), F32),
        (
            received.reshape(-1, chunk),
            got_wts.reshape(-1, chunk),
            got_rows.reshape(-1, chunk, width),
        ),
    )
    quarter = first_moment.shape[0]
    share = jnp.sum(
        lax.all_to_all(
            slab_grad.reshape(-1, quarter, width), "x", split_axis=0, concat_axis=0, tiled=True
        ),
        axis=0,
    )
    old_rows = lax.dynamic_slice_in_dim(values, lax.axis_index("x") * quarter, quarter, 0)
    new_first, new_second, new_part = adam_rows(old_rows, share, first_moment, second_moment)
    return layer_out.astype(BF), spread(new_part), new_first, new_second


def call(kernel, out_shape, vmem, grid=None, in_specs=None, out_specs=None, scratch=(), cost=None):
    extra = {} if grid is None else {"grid": grid}
    if in_specs is not None:
        extra["in_specs"] = in_specs
    if out_specs is not None:
        extra["out_specs"] = out_specs
    return pl.pallas_call(
        kernel,
        out_shape=out_shape,
        scratch_shapes=list(scratch),
        compiler_params=pltpu.CompilerParams(vmem_limit_bytes=vmem * 1024 * 1024),
        cost_estimate=cost,
        **extra,
    )


def cost(flops, nbytes):
    return pl.CostEstimate(flops=flops, bytes_accessed=nbytes, transcendentals=0)


def rank_kernel(
    sizes, pick_ref, wt_ref, cell_ref, rank_ref, wrow_ref, req_ref, pcol_ref, slot_ref, wcol_ref
):
    cells, depth, parts, rows_dev, proj_count = sizes
    per_token, tok = pick_ref.shape
    count = per_token * tok
    quarter = rows_dev // parts
    block = 256
    by_token = pick_ref[...]
    flat = jnp.concatenate([by_token[j : j + 1] for j in range(per_token)], axis=1)
    weights = wt_ref[...].astype(F32)
    wrow_ref[...] = jnp.concatenate([weights[j : j + 1] for j in range(per_token)], axis=1)
    owner = lax.div(flat, rows_dev)
    row = lax.rem(flat, rows_dev)
    owner_z = lax.rem(lax.div(owner, CORES), depth)
    cells_row = (
        lax.div(owner, depth * CORES) * CORES + lax.rem(owner, CORES)
    ) * parts + lax.div(row, quarter)
    trows = owner_z * quarter + lax.rem(row, quarter)
    cell_ref[...] = cells_row
    below = lax.broadcasted_iota(jnp.int32, (block, block), 0) < lax.broadcasted_iota(
        jnp.int32, (block, block), 1
    )
    below = below.astype(F32).astype(BF)
    carry = jnp.zeros((cells, 1), F32)
    asked = jnp.zeros((3 * cells, LANES), F32)
    ranks = []
    for b in range(count // block):
        cell = cells_row[:, b * block : (b + 1) * block]
        trow = trows[:, b * block : (b + 1) * block]
        here = (lax.broadcasted_iota(jnp.int32, (cells, block), 0) == cell).astype(F32)
        before = jnp.dot(here.astype(BF), below, preferred_element_type=F32) + carry
        carry = carry + jnp.sum(here, axis=1, keepdims=True)
        rank = jnp.sum(here * before, axis=0, keepdims=True).astype(jnp.int32)
        ranks.append(rank)
        place = (lax.broadcasted_iota(jnp.int32, (LANES, block), 0) == rank).astype(F32)
        high = (trow >> 5).astype(F32)
        low = (trow & 31).astype(F32)
        told = jnp.concatenate([here, here * high, here * low], axis=0)
        asked = asked + lax.dot_general(
            told.astype(BF), place.astype(BF), NT, preferred_element_type=F32
        )
    there = asked[:cells]
    rows = (asked[cells : 2 * cells] * 32.0 + asked[2 * cells :]).astype(jnp.int32)
    rows = jnp.where(there > 0.5, rows, -1)
    lane = lax.broadcasted_iota(jnp.int32, (cells, LANES), 1)
    over = (jnp.max(carry) > CAP).astype(jnp.int32)
    req_ref[...] = jnp.where(lane == LANES - 1, over, rows)
    rank_row = jnp.concatenate(ranks, axis=1)
    rank_ref[...] = rank_row
    slots = cells_row * CAP + rank_row
    by_row = jnp.concatenate([slots[:, j * tok : (j + 1) * tok] for j in range(per_token)], axis=0)
    slot_ref[...] = by_row.T
    pcol_ref[...] = lax.rem(by_token, proj_count).T
    wcol_ref[...] = weights.T


def send_kernel(
    group,
    tg_ref,
    proj_ref,
    pcol_ref,
    cell_ref,
    rank_ref,
    wt_ref,
    out_ref,
    grads,
    projs,
    chosen,
    made,
    in_sems,
    out_sems,
):
    tok, per_token = pcol_ref.shape
    count = cell_ref.shape[1]
    proj_count = proj_ref.shape[0]
    come = [pltpu.make_async_copy(tg_ref, grads, in_sems.at[proj_count])]
    for p in range(proj_count):
        come.append(pltpu.make_async_copy(proj_ref.at[p], projs.at[p], in_sems.at[p]))
    for copy in come:
        copy.start()
    at = lax.broadcasted_iota(jnp.int32, (CAP, count), 0) == rank_ref[...]
    place = jnp.where(at, wt_ref[...], 0.0).astype(BF)
    come[0].wait()
    for p in range(proj_count):
        come[p + 1].wait()
        back = lax.dot_general(grads[...], projs[p], NT, preferred_element_type=F32).astype(BF)
        for j in range(per_token):
            span = pl.ds(j * tok, tok)
            if p == 0:
                chosen[span, :] = back
            else:
                chosen[span, :] = jnp.where(pcol_ref[:, j : j + 1] == p, back, chosen[span, :])
    copies = []
    for g in range(made.shape[0] // (group * CAP)):
        parts = []
        for d in range(group):
            here = (cell_ref[...] == g * group + d).astype(F32).astype(BF)
            parts.append(place * here)
        pick = jnp.concatenate(parts, axis=0)
        span = pl.ds(g * group * CAP, group * CAP)
        made[span, :] = jnp.dot(pick, chosen[...], preferred_element_type=F32).astype(BF)
        copies.append(pltpu.make_async_copy(made.at[span, :], out_ref.at[span, :], out_sems.at[g]))
        copies[-1].start()
    for copy in copies:
        copy.wait()


def look_kernel(group, got_ref, z_ref, *refs):
    *pieces, out_ref, table, made, in_sems, out_sems = refs
    rows = pieces[0].shape[0]
    cells = got_ref.shape[0]
    depth = len(pieces)
    come = [
        pltpu.make_async_copy(piece, table.at[pl.ds(k * rows, rows), :], in_sems.at[k])
        for k, piece in enumerate(pieces)
    ]
    for copy in come:
        copy.start()
    told = got_ref[...]
    from_z = lax.rem(lax.div(told, rows) + depth - z_ref[0], depth)
    asked = jnp.where(told < 0, -1, from_z * rows + lax.rem(told, rows)).T
    lane = lax.broadcasted_iota(jnp.int32, (CAP, depth * rows), 1)
    for copy in come:
        copy.wait()
    copies = []
    for g in range(cells // group):
        parts = []
        for d in range(g * group, (g + 1) * group):
            parts.append((lane == asked[:CAP, d : d + 1]).astype(F32).astype(BF))
        pick = jnp.concatenate(parts, axis=0)
        span = pl.ds(g * group * CAP, group * CAP)
        made[span, :] = jnp.dot(pick, table[...], preferred_element_type=F32).astype(BF)
        copies.append(pltpu.make_async_copy(made.at[span, :], out_ref.at[span, :], out_sems.at[g]))
        copies[-1].start()
    for copy in copies:
        copy.wait()


def sum_kernel(ids_ref, flags_ref, got_ref, *out_refs):
    rows = out_refs[0].shape[0]
    slots = ids_ref.shape[1]
    over = jnp.where(jnp.max(flags_ref[...]) > 0, OVER, 0.0)
    for k, out_ref in enumerate(out_refs):
        pick = lax.broadcasted_iota(jnp.int32, (rows, slots), 0) == ids_ref[...] - k * rows
        part = jnp.dot(pick.astype(F32).astype(BF), got_ref[...], preferred_element_type=F32)
        out_ref[...] = (part + over).astype(out_ref.dtype)


def out_kernel(
    slot_ref, pcol_ref, wcol_ref, ret_ref, proj_ref, out_ref, projs, made, in_sems, out_sems
):
    tok, per_token = slot_ref.shape
    slots = ret_ref.shape[0]
    proj_count, width, out_width = proj_ref.shape
    chunks = made.shape[0]
    chunk = out_width // chunks
    spans = [pl.ds(n * chunk, chunk) for n in range(chunks)]
    come = [
        pltpu.make_async_copy(proj_ref.at[:, :, span], projs.at[:, :, span], in_sems.at[n])
        for n, span in enumerate(spans)
    ]
    for copy in come:
        copy.start()
    lane = lax.broadcasted_iota(jnp.int32, (tok, slots), 1)
    pick = [(lane == slot_ref[:, j : j + 1]).astype(F32).astype(BF) for j in range(per_token)]
    rows = jnp.dot(jnp.concatenate(pick, axis=0), ret_ref[...], preferred_element_type=F32)
    sums = []
    for p in range(proj_count):
        weight = [
            jnp.where(pcol_ref[:, j : j + 1] == p, wcol_ref[:, j : j + 1], 0.0)
            for j in range(per_token)
        ]
        parts = [rows[j * tok : (j + 1) * tok] * weight[j] for j in range(per_token)]
        sums.append(functools.reduce(lambda a, b: a + b, parts).astype(BF))
    mixed = jnp.concatenate(sums, axis=1)
    copies = []
    for n, span in enumerate(spans):
        come[n].wait()
        made[n] = jnp.dot(
            mixed,
            projs[:, :, span].reshape(proj_count * width, chunk),
            preferred_element_type=F32,
        ).astype(BF)
        copies.append(pltpu.make_async_copy(made.at[n], out_ref.at[:, span], out_sems.at[n]))
        copies[-1].start()
    for copy in copies:
        copy.wait()


def short_way(picks, pick_weights, token_grads, values, first_moment, second_moment, projectors):
    plane = ("y", "c", "x")
    cells = lax.axis_size(plane)
    depth = lax.axis_size("z")
    parts = lax.axis_size("x")
    rows_dev, width = values.shape
    quarter = rows_dev // parts
    tok, per_token = picks.shape
    proj_count, _, out_width = projectors.shape
    total = tok * per_token
    slots = cells * CAP
    table_rows = depth * quarter
    start = lax.axis_index("x") * quarter
    old_rows = lax.dynamic_slice_in_dim(values, start, quarter, 0)

    hbm = pl.BlockSpec(memory_space=pl.ANY)
    vmem = pl.BlockSpec(memory_space=pltpu.VMEM)
    i32 = lambda *shape: jax.ShapeDtypeStruct(shape, jnp.int32)
    f32 = lambda *shape: jax.ShapeDtypeStruct(shape, F32)
    cell, rank, wt_row, requests, pcol, slot_col, wcol = call(
        functools.partial(rank_kernel, (cells, depth, parts, rows_dev, proj_count)),
        (
            i32(1, total),
            i32(1, total),
            f32(1, total),
            i32(cells, LANES),
            i32(tok, per_token),
            i32(tok, per_token),
            f32(tok, per_token),
        ),
        60,
        in_specs=[vmem] * 2,
        out_specs=(vmem,) * 7,
        cost=cost(2 * total * cells * 400, 20000),
    )(picks.T, pick_weights.T)
    received = lax.all_to_all(requests, plane, split_axis=0, concat_axis=0, tiled=True)

    onward = [(i, (i + 1) % depth) for i in range(depth)]
    backward = [(i, (i - 1) % depth) for i in range(depth)]
    pieces = [old_rows] + [None] * (depth - 1)
    for k in range(1, depth // 2 + 1):
        pieces[k] = lax.ppermute(pieces[k - 1], "z", backward)
        if k < depth // 2:
            pieces[depth - k] = lax.ppermute(pieces[(depth - k + 1) % depth], "z", onward)

    group = 8
    sent = call(
        functools.partial(send_kernel, group),
        jax.ShapeDtypeStruct((slots, width), BF),
        60,
        in_specs=[hbm] * 2 + [vmem] * 4,
        out_specs=hbm,
        scratch=[
            pltpu.VMEM((tok, out_width), BF),
            pltpu.VMEM(projectors.shape, BF),
            pltpu.VMEM((total, width), BF),
            pltpu.VMEM((slots, width), BF),
            pltpu.SemaphoreType.DMA((proj_count + 1,)),
            pltpu.SemaphoreType.DMA((cells // group,)),
        ],
        cost=cost(2 * width * (tok * proj_count * out_width + slots * total), 12000000),
    )(token_grads, projectors, pcol, cell, rank, wt_row)
    got = lax.all_to_all(
        sent.reshape(cells, CAP, width), plane, split_axis=0, concat_axis=0, tiled=True
    ).reshape(slots, width)

    z_here = lax.axis_index("z")
    told = received[:, :CAP]
    from_z = lax.rem(lax.div(told, quarter) + depth - z_here, depth)
    asked = jnp.where(told < 0, -1, from_z * quarter + lax.rem(told, quarter))
    flags = received[:, LANES - 1 :]
    looked = call(
        functools.partial(look_kernel, group),
        jax.ShapeDtypeStruct((slots, width), BF),
        60,
        in_specs=[vmem, pl.BlockSpec(memory_space=pltpu.SMEM)] + [hbm] * depth,
        out_specs=hbm,
        scratch=[
            pltpu.VMEM((table_rows, width), BF),
            pltpu.VMEM((slots, width), BF),
            pltpu.SemaphoreType.DMA((depth,)),
            pltpu.SemaphoreType.DMA((cells // group,)),
        ],
        cost=cost(2 * width * slots * table_rows, 4000000),
    )(received, z_here.reshape(1), *pieces)
    sums = call(
        sum_kernel,
        (jax.ShapeDtypeStruct((quarter, width), BF),) * depth,
        16,
        in_specs=[vmem] * 3,
        out_specs=(vmem,) * depth,
        cost=cost(2 * width * slots * table_rows, 4000000),
    )(asked.reshape(1, slots), flags, got)
    looked, *sums = lax.optimization_barrier((looked, *sums))
    returned = lax.all_to_all(
        looked.reshape(cells, CAP, width), plane, split_axis=0, concat_axis=0, tiled=True
    ).reshape(slots, width)

    ahead = sums[depth // 2]
    behind = sums[depth // 2 + 1]
    for k in range(depth // 2 - 1, 0, -1):
        ahead = (lax.ppermute(ahead, "z", onward).astype(F32) + sums[k].astype(F32)).astype(BF)
        if k > 1:
            behind = (
                lax.ppermute(behind, "z", backward).astype(F32) + sums[depth - k + 1].astype(F32)
            ).astype(BF)
    share = (
        sums[0].astype(F32)
        + lax.ppermute(ahead, "z", onward).astype(F32)
        + lax.ppermute(behind, "z", backward).astype(F32)
    )
    flag = share[0, 0] > 0.5 * OVER
    new_first, new_second, new_part = adam_rows(old_rows, share, first_moment, second_moment)
    new_parts = spread(new_part)

    chunks = 4
    layer_out = call(
        out_kernel,
        jax.ShapeDtypeStruct((tok, out_width), BF),
        48,
        in_specs=[vmem] * 4 + [hbm],
        out_specs=hbm,
        scratch=[
            pltpu.VMEM(projectors.shape, BF),
            pltpu.VMEM((chunks, tok, out_width // chunks), BF),
            pltpu.SemaphoreType.DMA((chunks,)),
            pltpu.SemaphoreType.DMA((chunks,)),
        ],
        cost=cost(2 * width * (tok * proj_count * out_width + slots * total), 13000000),
    )(slot_col, pcol, wcol, returned, projectors)
    return flag, (layer_out, new_parts, new_first, new_second)


def join_kernel(x_ref, *refs):
    *pieces, out_ref = refs
    parts = len(pieces)
    rows = pieces[0].shape[0]
    for k, piece in enumerate(pieces):
        first = lax.rem(x_ref[0] + parts - k, parts) * rows
        out_ref[pl.ds(pl.multiple_of(first, rows), rows), :] = piece[...]


def on_device(*args):
    flag, outs = short_way(*args)
    layer_out, new_parts, new_first, new_second = lax.cond(
        flag, lambda given, done: long_way(*given), lambda given, done: done, args, outs
    )
    rows, width = new_parts[0].shape
    vmem = pl.BlockSpec(memory_space=pltpu.VMEM)
    new_values = call(
        join_kernel,
        jax.ShapeDtypeStruct((len(new_parts) * rows, width), BF),
        60,
        in_specs=[pl.BlockSpec(memory_space=pltpu.SMEM)] + [vmem] * len(new_parts),
        out_specs=vmem,
    )(lax.axis_index("x").reshape(1), *new_parts)
    return layer_out, new_values, new_first, new_second


def solution(mesh):
    mem, dp = mesh.devices.shape
    grid = Mesh(
        mesh.devices.reshape(mem // (Z_CHIPS * CORES), Z_CHIPS, CORES, dp), ("y", "z", "c", "x")
    )
    every = P(("y", "z", "c", "x"), None)
    slab = P(("y", "z", "c"), None)
    return jax.shard_map(
        on_device,
        mesh=grid,
        in_specs=(every, every, every, slab, every, every, P()),
        out_specs=(every, slab, every, every),
        check_vma=False,
    )
```

```python
import functools

import jax
import jax.numpy as jnp
from jax import lax
from jax.experimental import pallas as pl
from jax.experimental.pallas import tpu as pltpu
from jax.sharding import Mesh
from jax.sharding import PartitionSpec as P

beta_one = 0.9
beta_two = 0.999
corr_one = 1.0 - 0.9**50
corr_two = 1.0 - 0.999**50
learn_rate = 0.05
adam_eps = 1e-08

Z_CHIPS = 8
CORES = 2
CAP = 72
LANES = 128
OVER = 1e30
BF = jnp.bfloat16
F32 = jnp.float32
NT = (((1,), (1,)), ((), ()))


def adam_rows(old_rows, slab_grad, first_moment, second_moment):
    new_first = beta_one * first_moment + (1.0 - beta_one) * slab_grad
    new_second = beta_two * second_moment + (1.0 - beta_two) * slab_grad * slab_grad
    update_step = new_first / corr_one / (jnp.sqrt(new_second / corr_two) + adam_eps)
    updated = (old_rows.astype(jnp.float32) - learn_rate * update_step).astype(jnp.bfloat16)
    return (new_first, new_second, updated)


def spread(new_part):
    parts = lax.axis_size("x")
    return [new_part] + [
        lax.ppermute(new_part, "x", [(i, (i + k) % parts) for i in range(parts)])
        for k in range(1, parts)
    ]


def long_way(picks, pick_weights, token_grads, values, first_moment, second_moment, projectors):
    mem = ("y", "z", "c")
    owners = lax.axis_size(mem)
    rows_dev, width = values.shape
    tok_count, per_token = picks.shape
    proj_count, _, out_width = projectors.shape
    total_picks = tok_count * per_token
    capacity = 2 * total_picks // owners
    slots = owners * capacity
    swap = lambda rows: lax.all_to_all(rows, mem, split_axis=0, concat_axis=0, tiled=True)
    flat_picks = picks.reshape(-1)
    owner_ids = flat_picks // rows_dev
    local_rows = flat_picks - owner_ids * rows_dev
    member = (owner_ids[:, None] == jnp.arange(owners, dtype=jnp.int32)[None, :]).astype(jnp.int32)
    before = jnp.cumsum(member, axis=0) - member
    slot_ids = owner_ids * capacity + jnp.sum(before * member, axis=1)
    number = jnp.arange(total_picks, dtype=jnp.int32)
    pick_in = jnp.full((slots,), total_picks, jnp.int32).at[slot_ids].set(number)
    in_slots = lambda per_pick: jnp.concatenate([per_pick, jnp.zeros((1,), per_pick.dtype)])[pick_in]
    proj_ids = picks % proj_count
    requests = in_slots(local_rows).reshape(owners, capacity)
    received = swap(requests)
    returned = swap(values[received])
    _, back_grads = lax.scan(
        lambda none, proj: (
            none,
            lax.dot_general(token_grads, proj, NT, preferred_element_type=F32).astype(BF),
        ),
        0,
        projectors,
    )
    back_rows = in_slots(proj_ids.reshape(-1) * tok_count + number // per_token)
    send_rows = back_grads.reshape(proj_count * tok_count, width)[back_rows]
    got_rows = swap(send_rows.reshape(owners, capacity, width)).reshape(slots, width)
    got_wts = swap(in_slots(pick_weights.reshape(-1)).reshape(owners, capacity)).reshape(slots)
    picked = returned.reshape(slots, width)[slot_ids].reshape(tok_count, per_token, width)
    mixing = jnp.where(
        proj_ids[..., None] == jnp.arange(proj_count, dtype=jnp.int32),
        pick_weights[..., None],
        jnp.zeros((), BF),
    )
    proj_sums = jnp.einsum("tjp,tjd->ptd", mixing, picked, preferred_element_type=F32).astype(BF)
    layer_out, _ = lax.scan(
        lambda acc, part: (acc + jnp.dot(*part, preferred_element_type=F32), None),
        jnp.zeros((tok_count, out_width), F32),
        (proj_sums, projectors),
    )
    chunk = slots // 20

    def add_chunk(acc, part):
        ids, wts, rows = part
        place = jnp.arange(rows_dev, dtype=jnp.int32)[:, None] == ids[None, :]
        place = jnp.where(place, wts[None, :], jnp.zeros((), BF))
        return acc + jnp.dot(place, rows, preferred_element_type=F32), None

    slab_grad, _ = lax.scan(
        add_chunk,
        jnp.zeros((rows_dev, width), F32),
        (
            received.reshape(-1, chunk),
            got_wts.reshape(-1, chunk),
            got_rows.reshape(-1, chunk, width),
        ),
    )
    quarter = first_moment.shape[0]
    share = jnp.sum(
        lax.all_to_all(
            slab_grad.reshape(-1, quarter, width), "x", split_axis=0, concat_axis=0, tiled=True
        ),
        axis=0,
    )
    old_rows = lax.dynamic_slice_in_dim(values, lax.axis_index("x") * quarter, quarter, 0)
    new_first, new_second, new_part = adam_rows(old_rows, share, first_moment, second_moment)
    return layer_out.astype(BF), spread(new_part), new_first, new_second


def call(kernel, out_shape, vmem, grid=None, in_specs=None, out_specs=None, scratch=(), cost=None):
    extra = {} if grid is None else {"grid": grid}
    if in_specs is not None:
        extra["in_specs"] = in_specs
    if out_specs is not None:
        extra["out_specs"] = out_specs
    return pl.pallas_call(
        kernel,
        out_shape=out_shape,
        scratch_shapes=list(scratch),
        compiler_params=pltpu.CompilerParams(vmem_limit_bytes=vmem * 1024 * 1024),
        cost_estimate=cost,
        **extra,
    )


def cost(flops, nbytes):
    return pl.CostEstimate(flops=flops, bytes_accessed=nbytes, transcendentals=0)


def rank_kernel(
    sizes, pick_ref, wt_ref, cell_ref, rank_ref, wrow_ref, req_ref, pcol_ref, slot_ref, wcol_ref
):
    cells, depth, parts, rows_dev, proj_count = sizes
    per_token, tok = pick_ref.shape
    count = per_token * tok
    quarter = rows_dev // parts
    block = 256
    by_token = pick_ref[...]
    flat = jnp.concatenate([by_token[j : j + 1] for j in range(per_token)], axis=1)
    weights = wt_ref[...].astype(F32)
    wrow_ref[...] = jnp.concatenate([weights[j : j + 1] for j in range(per_token)], axis=1)
    owner = lax.div(flat, rows_dev)
    row = lax.rem(flat, rows_dev)
    owner_z = lax.rem(lax.div(owner, CORES), depth)
    cells_row = (
        lax.div(owner, depth * CORES) * CORES + lax.rem(owner, CORES)
    ) * parts + lax.div(row, quarter)
    trows = owner_z * quarter + lax.rem(row, quarter)
    cell_ref[...] = cells_row
    below = lax.broadcasted_iota(jnp.int32, (block, block), 0) < lax.broadcasted_iota(
        jnp.int32, (block, block), 1
    )
    below = below.astype(F32).astype(BF)
    carry = jnp.zeros((cells, 1), F32)
    asked = jnp.zeros((3 * cells, LANES), F32)
    ranks = []
    for b in range(count // block):
        cell = cells_row[:, b * block : (b + 1) * block]
        trow = trows[:, b * block : (b + 1) * block]
        here = (lax.broadcasted_iota(jnp.int32, (cells, block), 0) == cell).astype(F32)
        before = jnp.dot(here.astype(BF), below, preferred_element_type=F32) + carry
        carry = carry + jnp.sum(here, axis=1, keepdims=True)
        rank = jnp.sum(here * before, axis=0, keepdims=True).astype(jnp.int32)
        ranks.append(rank)
        place = (lax.broadcasted_iota(jnp.int32, (LANES, block), 0) == rank).astype(F32)
        high = (trow >> 5).astype(F32)
        low = (trow & 31).astype(F32)
        told = jnp.concatenate([here, here * high, here * low], axis=0)
        asked = asked + lax.dot_general(
            told.astype(BF), place.astype(BF), NT, preferred_element_type=F32
        )
    there = asked[:cells]
    rows = (asked[cells : 2 * cells] * 32.0 + asked[2 * cells :]).astype(jnp.int32)
    rows = jnp.where(there > 0.5, rows, -1)
    lane = lax.broadcasted_iota(jnp.int32, (cells, LANES), 1)
    over = (jnp.max(carry) > CAP).astype(jnp.int32)
    req_ref[...] = jnp.where(lane == LANES - 1, over, rows)
    rank_row = jnp.concatenate(ranks, axis=1)
    rank_ref[...] = rank_row
    slots = cells_row * CAP + rank_row
    by_row = jnp.concatenate([slots[:, j * tok : (j + 1) * tok] for j in range(per_token)], axis=0)
    slot_ref[...] = by_row.T
    pcol_ref[...] = lax.rem(by_token, proj_count).T
    wcol_ref[...] = weights.T


def send_kernel(
    group,
    tg_ref,
    proj_ref,
    pcol_ref,
    cell_ref,
    rank_ref,
    wt_ref,
    out_ref,
    grads,
    projs,
    chosen,
    made,
    in_sems,
    out_sems,
):
    tok, per_token = pcol_ref.shape
    count = cell_ref.shape[1]
    proj_count = proj_ref.shape[0]
    come = [pltpu.make_async_copy(tg_ref, grads, in_sems.at[proj_count])]
    for p in range(proj_count):
        come.append(pltpu.make_async_copy(proj_ref.at[p], projs.at[p], in_sems.at[p]))
    for copy in come:
        copy.start()
    at = lax.broadcasted_iota(jnp.int32, (CAP, count), 0) == rank_ref[...]
    place = jnp.where(at, wt_ref[...], 0.0).astype(BF)
    come[0].wait()
    for p in range(proj_count):
        come[p + 1].wait()
        back = lax.dot_general(grads[...], projs[p], NT, preferred_element_type=F32).astype(BF)
        for j in range(per_token):
            span = pl.ds(j * tok, tok)
            if p == 0:
                chosen[span, :] = back
            else:
                chosen[span, :] = jnp.where(pcol_ref[:, j : j + 1] == p, back, chosen[span, :])
    copies = []
    for g in range(made.shape[0] // (group * CAP)):
        parts = []
        for d in range(group):
            here = (cell_ref[...] == g * group + d).astype(F32).astype(BF)
            parts.append(place * here)
        pick = jnp.concatenate(parts, axis=0)
        span = pl.ds(g * group * CAP, group * CAP)
        made[span, :] = jnp.dot(pick, chosen[...], preferred_element_type=F32).astype(BF)
        copies.append(pltpu.make_async_copy(made.at[span, :], out_ref.at[span, :], out_sems.at[g]))
        copies[-1].start()
    for copy in copies:
        copy.wait()


def look_kernel(group, got_ref, z_ref, *refs):
    *pieces, out_ref, table, made, in_sems, out_sems = refs
    rows = pieces[0].shape[0]
    cells = got_ref.shape[0]
    depth = len(pieces)
    come = [
        pltpu.make_async_copy(piece, table.at[pl.ds(k * rows, rows), :], in_sems.at[k])
        for k, piece in enumerate(pieces)
    ]
    for copy in come:
        copy.start()
    told = got_ref[...]
    from_z = lax.rem(lax.div(told, rows) + depth - z_ref[0], depth)
    asked = jnp.where(told < 0, -1, from_z * rows + lax.rem(told, rows)).T
    lane = lax.broadcasted_iota(jnp.int32, (CAP, depth * rows), 1)
    for copy in come:
        copy.wait()
    copies = []
    for g in range(cells // group):
        parts = []
        for d in range(g * group, (g + 1) * group):
            parts.append((lane == asked[:CAP, d : d + 1]).astype(F32).astype(BF))
        pick = jnp.concatenate(parts, axis=0)
        span = pl.ds(g * group * CAP, group * CAP)
        made[span, :] = jnp.dot(pick, table[...], preferred_element_type=F32).astype(BF)
        copies.append(pltpu.make_async_copy(made.at[span, :], out_ref.at[span, :], out_sems.at[g]))
        copies[-1].start()
    for copy in copies:
        copy.wait()


def sum_kernel(ids_ref, flags_ref, got_ref, *out_refs):
    rows = out_refs[0].shape[0]
    slots = ids_ref.shape[1]
    over = jnp.where(jnp.max(flags_ref[...]) > 0, OVER, 0.0)
    for k, out_ref in enumerate(out_refs):
        pick = lax.broadcasted_iota(jnp.int32, (rows, slots), 0) == ids_ref[...] - k * rows
        part = jnp.dot(pick.astype(F32).astype(BF), got_ref[...], preferred_element_type=F32)
        out_ref[...] = (part + over).astype(out_ref.dtype)


def out_kernel(
    slot_ref, pcol_ref, wcol_ref, ret_ref, proj_ref, out_ref, projs, made, in_sems, out_sems
):
    tok, per_token = slot_ref.shape
    slots = ret_ref.shape[0]
    proj_count, width, out_width = proj_ref.shape
    chunks = made.shape[0]
    chunk = out_width // chunks
    spans = [pl.ds(n * chunk, chunk) for n in range(chunks)]
    come = [
        pltpu.make_async_copy(proj_ref.at[:, :, span], projs.at[:, :, span], in_sems.at[n])
        for n, span in enumerate(spans)
    ]
    for copy in come:
        copy.start()
    lane = lax.broadcasted_iota(jnp.int32, (tok, slots), 1)
    pick = [(lane == slot_ref[:, j : j + 1]).astype(F32).astype(BF) for j in range(per_token)]
    rows = jnp.dot(jnp.concatenate(pick, axis=0), ret_ref[...], preferred_element_type=F32)
    sums = []
    for p in range(proj_count):
        weight = [
            jnp.where(pcol_ref[:, j : j + 1] == p, wcol_ref[:, j : j + 1], 0.0)
            for j in range(per_token)
        ]
        parts = [rows[j * tok : (j + 1) * tok] * weight[j] for j in range(per_token)]
        sums.append(functools.reduce(lambda a, b: a + b, parts).astype(BF))
    mixed = jnp.concatenate(sums, axis=1)
    copies = []
    for n, span in enumerate(spans):
        come[n].wait()
        made[n] = jnp.dot(
            mixed,
            projs[:, :, span].reshape(proj_count * width, chunk),
            preferred_element_type=F32,
        ).astype(BF)
        copies.append(pltpu.make_async_copy(made.at[n], out_ref.at[:, span], out_sems.at[n]))
        copies[-1].start()
    for copy in copies:
        copy.wait()


def short_way(picks, pick_weights, token_grads, values, first_moment, second_moment, projectors):
    plane = ("y", "c", "x")
    cells = lax.axis_size(plane)
    depth = lax.axis_size("z")
    parts = lax.axis_size("x")
    rows_dev, width = values.shape
    quarter = rows_dev // parts
    tok, per_token = picks.shape
    proj_count, _, out_width = projectors.shape
    total = tok * per_token
    slots = cells * CAP
    table_rows = depth * quarter
    start = lax.axis_index("x") * quarter
    old_rows = lax.dynamic_slice_in_dim(values, start, quarter, 0)

    hbm = pl.BlockSpec(memory_space=pl.ANY)
    vmem = pl.BlockSpec(memory_space=pltpu.VMEM)
    i32 = lambda *shape: jax.ShapeDtypeStruct(shape, jnp.int32)
    f32 = lambda *shape: jax.ShapeDtypeStruct(shape, F32)
    cell, rank, wt_row, requests, pcol, slot_col, wcol = call(
        functools.partial(rank_kernel, (cells, depth, parts, rows_dev, proj_count)),
        (
            i32(1, total),
            i32(1, total),
            f32(1, total),
            i32(cells, LANES),
            i32(tok, per_token),
            i32(tok, per_token),
            f32(tok, per_token),
        ),
        60,
        in_specs=[vmem] * 2,
        out_specs=(vmem,) * 7,
        cost=cost(2 * total * cells * 400, 20000),
    )(picks.T, pick_weights.T)
    received = lax.all_to_all(requests, plane, split_axis=0, concat_axis=0, tiled=True)

    onward = [(i, (i + 1) % depth) for i in range(depth)]
    backward = [(i, (i - 1) % depth) for i in range(depth)]
    pieces = [old_rows] + [None] * (depth - 1)
    for k in range(1, depth // 2 + 1):
        pieces[k] = lax.ppermute(pieces[k - 1], "z", backward)
        if k < depth // 2:
            pieces[depth - k] = lax.ppermute(pieces[(depth - k + 1) % depth], "z", onward)

    group = 8
    sent = call(
        functools.partial(send_kernel, group),
        jax.ShapeDtypeStruct((slots, width), BF),
        60,
        in_specs=[hbm] * 2 + [vmem] * 4,
        out_specs=hbm,
        scratch=[
            pltpu.VMEM((tok, out_width), BF),
            pltpu.VMEM(projectors.shape, BF),
            pltpu.VMEM((total, width), BF),
            pltpu.VMEM((slots, width), BF),
            pltpu.SemaphoreType.DMA((proj_count + 1,)),
            pltpu.SemaphoreType.DMA((cells // group,)),
        ],
        cost=cost(2 * width * (tok * proj_count * out_width + slots * total), 12000000),
    )(token_grads, projectors, pcol, cell, rank, wt_row)
    got = lax.all_to_all(
        sent.reshape(cells, CAP, width), plane, split_axis=0, concat_axis=0, tiled=True
    ).reshape(slots, width)

    z_here = lax.axis_index("z")
    told = received[:, :CAP]
    from_z = lax.rem(lax.div(told, quarter) + depth - z_here, depth)
    asked = jnp.where(told < 0, -1, from_z * quarter + lax.rem(told, quarter))
    flags = received[:, LANES - 1 :]
    looked = call(
        functools.partial(look_kernel, group),
        jax.ShapeDtypeStruct((slots, width), BF),
        60,
        in_specs=[vmem, pl.BlockSpec(memory_space=pltpu.SMEM)] + [hbm] * depth,
        out_specs=hbm,
        scratch=[
            pltpu.VMEM((table_rows, width), BF),
            pltpu.VMEM((slots, width), BF),
            pltpu.SemaphoreType.DMA((depth,)),
            pltpu.SemaphoreType.DMA((cells // group,)),
        ],
        cost=cost(2 * width * slots * table_rows, 4000000),
    )(received, z_here.reshape(1), *pieces)
    sums = call(
        sum_kernel,
        (jax.ShapeDtypeStruct((quarter, width), BF),) * depth,
        16,
        in_specs=[vmem] * 3,
        out_specs=(vmem,) * depth,
        cost=cost(2 * width * slots * table_rows, 4000000),
    )(asked.reshape(1, slots), flags, got)
    looked, *sums = lax.optimization_barrier((looked, *sums))
    returned = lax.all_to_all(
        looked.reshape(cells, CAP, width), plane, split_axis=0, concat_axis=0, tiled=True
    ).reshape(slots, width)

    ahead = sums[depth // 2]
    behind = sums[depth // 2 + 1]
    for k in range(depth // 2 - 1, 0, -1):
        ahead = (lax.ppermute(ahead, "z", onward).astype(F32) + sums[k].astype(F32)).astype(BF)
        if k > 1:
            behind = (
                lax.ppermute(behind, "z", backward).astype(F32) + sums[depth - k + 1].astype(F32)
            ).astype(BF)
    share = (
        sums[0].astype(F32)
        + lax.ppermute(ahead, "z", onward).astype(F32)
        + lax.ppermute(behind, "z", backward).astype(F32)
    )
    flag = share[0, 0] > 0.5 * OVER
    new_first, new_second, new_part = adam_rows(old_rows, share, first_moment, second_moment)
    new_parts = spread(new_part)

    chunks = 4
    layer_out = call(
        out_kernel,
        jax.ShapeDtypeStruct((tok, out_width), BF),
        48,
        in_specs=[vmem] * 4 + [hbm],
        out_specs=hbm,
        scratch=[
            pltpu.VMEM(projectors.shape, BF),
            pltpu.VMEM((chunks, tok, out_width // chunks), BF),
            pltpu.SemaphoreType.DMA((chunks,)),
            pltpu.SemaphoreType.DMA((chunks,)),
        ],
        cost=cost(2 * width * (tok * proj_count * out_width + slots * total), 13000000),
    )(slot_col, pcol, wcol, returned, projectors)
    return flag, (layer_out, new_parts, new_first, new_second)


def on_device(*args):
    flag, outs = short_way(*args)
    layer_out, new_parts, new_first, new_second = lax.cond(
        flag, lambda given, done: long_way(*given), lambda given, done: done, args, outs
    )
    parts = len(new_parts)
    x_here = lax.axis_index("x")
    new_values = new_parts[0][None]
    for k, piece in enumerate(new_parts[1:], 1):
        mine = jnp.arange(parts, dtype=jnp.int32) == lax.rem(x_here + parts - k, parts)
        new_values = jnp.where(mine[:, None, None], piece[None], new_values)
    new_values = new_values.reshape(-1, new_values.shape[2])
    return layer_out, new_values, new_first, new_second


def solution(mesh):
    mem, dp = mesh.devices.shape
    grid = Mesh(
        mesh.devices.reshape(mem // (Z_CHIPS * CORES), Z_CHIPS, CORES, dp), ("y", "z", "c", "x")
    )
    every = P(("y", "z", "c", "x"), None)
    slab = P(("y", "z", "c"), None)
    return jax.shard_map(
        on_device,
        mesh=grid,
        in_specs=(every, every, every, slab, every, every, P()),
        out_specs=(every, slab, every, every),
        check_vma=False,
    )
```

```python
import functools

import jax
import jax.numpy as jnp
from jax import lax
from jax.experimental import pallas as pl
from jax.experimental.pallas import tpu as pltpu
from jax.sharding import Mesh
from jax.sharding import PartitionSpec as P

beta_one = 0.9
beta_two = 0.999
corr_one = 1.0 - 0.9**50
corr_two = 1.0 - 0.999**50
learn_rate = 0.05
adam_eps = 1e-08

Z_CHIPS = 8
CORES = 2
CAP = 72
LANES = 128
OVER = 1e30
BF = jnp.bfloat16
F32 = jnp.float32
NT = (((1,), (1,)), ((), ()))


def adam_rows(old_rows, slab_grad, first_moment, second_moment):
    new_first = beta_one * first_moment + (1.0 - beta_one) * slab_grad
    new_second = beta_two * second_moment + (1.0 - beta_two) * slab_grad * slab_grad
    update_step = new_first / corr_one / (jnp.sqrt(new_second / corr_two) + adam_eps)
    updated = (old_rows.astype(jnp.float32) - learn_rate * update_step).astype(jnp.bfloat16)
    return (new_first, new_second, updated)


def spread(new_part):
    parts = lax.axis_size("x")
    return [new_part] + [
        lax.ppermute(new_part, "x", [(i, (i + k) % parts) for i in range(parts)])
        for k in range(1, parts)
    ]


def long_way(picks, pick_weights, token_grads, values, first_moment, second_moment, projectors):
    mem = ("y", "z", "c")
    owners = lax.axis_size(mem)
    rows_dev, width = values.shape
    tok_count, per_token = picks.shape
    proj_count, _, out_width = projectors.shape
    total_picks = tok_count * per_token
    capacity = 2 * total_picks // owners
    slots = owners * capacity
    swap = lambda rows: lax.all_to_all(rows, mem, split_axis=0, concat_axis=0, tiled=True)
    flat_picks = picks.reshape(-1)
    owner_ids = flat_picks // rows_dev
    local_rows = flat_picks - owner_ids * rows_dev
    member = (owner_ids[:, None] == jnp.arange(owners, dtype=jnp.int32)[None, :]).astype(jnp.int32)
    before = jnp.cumsum(member, axis=0) - member
    slot_ids = owner_ids * capacity + jnp.sum(before * member, axis=1)
    number = jnp.arange(total_picks, dtype=jnp.int32)
    pick_in = jnp.full((slots,), total_picks, jnp.int32).at[slot_ids].set(number)
    in_slots = lambda per_pick: jnp.concatenate([per_pick, jnp.zeros((1,), per_pick.dtype)])[pick_in]
    proj_ids = picks % proj_count
    requests = in_slots(local_rows).reshape(owners, capacity)
    received = swap(requests)
    returned = swap(values[received])
    _, back_grads = lax.scan(
        lambda none, proj: (
            none,
            lax.dot_general(token_grads, proj, NT, preferred_element_type=F32).astype(BF),
        ),
        0,
        projectors,
    )
    back_rows = in_slots(proj_ids.reshape(-1) * tok_count + number // per_token)
    send_rows = back_grads.reshape(proj_count * tok_count, width)[back_rows]
    got_rows = swap(send_rows.reshape(owners, capacity, width)).reshape(slots, width)
    got_wts = swap(in_slots(pick_weights.reshape(-1)).reshape(owners, capacity)).reshape(slots)
    picked = returned.reshape(slots, width)[slot_ids].reshape(tok_count, per_token, width)
    mixing = jnp.where(
        proj_ids[..., None] == jnp.arange(proj_count, dtype=jnp.int32),
        pick_weights[..., None],
        jnp.zeros((), BF),
    )
    proj_sums = jnp.einsum("tjp,tjd->ptd", mixing, picked, preferred_element_type=F32).astype(BF)
    layer_out, _ = lax.scan(
        lambda acc, part: (acc + jnp.dot(*part, preferred_element_type=F32), None),
        jnp.zeros((tok_count, out_width), F32),
        (proj_sums, projectors),
    )
    chunk = slots // 20

    def add_chunk(acc, part):
        ids, wts, rows = part
        place = jnp.arange(rows_dev, dtype=jnp.int32)[:, None] == ids[None, :]
        place = jnp.where(place, wts[None, :], jnp.zeros((), BF))
        return acc + jnp.dot(place, rows, preferred_element_type=F32), None

    slab_grad, _ = lax.scan(
        add_chunk,
        jnp.zeros((rows_dev, width), F32),
        (
            received.reshape(-1, chunk),
            got_wts.reshape(-1, chunk),
            got_rows.reshape(-1, chunk, width),
        ),
    )
    quarter = first_moment.shape[0]
    share = jnp.sum(
        lax.all_to_all(
            slab_grad.reshape(-1, quarter, width), "x", split_axis=0, concat_axis=0, tiled=True
        ),
        axis=0,
    )
    old_rows = lax.dynamic_slice_in_dim(values, lax.axis_index("x") * quarter, quarter, 0)
    new_first, new_second, new_part = adam_rows(old_rows, share, first_moment, second_moment)
    return layer_out.astype(BF), spread(new_part), new_first, new_second


def call(kernel, out_shape, vmem, grid=None, in_specs=None, out_specs=None, scratch=(), cost=None):
    extra = {} if grid is None else {"grid": grid}
    if in_specs is not None:
        extra["in_specs"] = in_specs
    if out_specs is not None:
        extra["out_specs"] = out_specs
    return pl.pallas_call(
        kernel,
        out_shape=out_shape,
        scratch_shapes=list(scratch),
        compiler_params=pltpu.CompilerParams(vmem_limit_bytes=vmem * 1024 * 1024),
        cost_estimate=cost,
        **extra,
    )


def cost(flops, nbytes):
    return pl.CostEstimate(flops=flops, bytes_accessed=nbytes, transcendentals=0)


def rank_kernel(
    sizes, pick_ref, wt_ref, cell_ref, rank_ref, wrow_ref, req_ref, cols_ref
):
    cells, depth, parts, rows_dev, proj_count = sizes
    per_token, tok = pick_ref.shape
    count = per_token * tok
    quarter = rows_dev // parts
    block = 256
    by_token = pick_ref[...]
    flat = jnp.concatenate([by_token[j : j + 1] for j in range(per_token)], axis=1)
    weights = wt_ref[...].astype(F32)
    wrow_ref[...] = jnp.concatenate([weights[j : j + 1] for j in range(per_token)], axis=1)
    owner = lax.div(flat, rows_dev)
    row = lax.rem(flat, rows_dev)
    owner_z = lax.rem(lax.div(owner, CORES), depth)
    cells_row = (
        lax.div(owner, depth * CORES) * CORES + lax.rem(owner, CORES)
    ) * parts + lax.div(row, quarter)
    trows = owner_z * quarter + lax.rem(row, quarter)
    cell_ref[...] = cells_row
    below = lax.broadcasted_iota(jnp.int32, (block, block), 0) < lax.broadcasted_iota(
        jnp.int32, (block, block), 1
    )
    below = below.astype(F32).astype(BF)
    carry = jnp.zeros((cells, 1), F32)
    asked = jnp.zeros((3 * cells, LANES), F32)
    ranks = []
    for b in range(count // block):
        cell = cells_row[:, b * block : (b + 1) * block]
        trow = trows[:, b * block : (b + 1) * block]
        here = (lax.broadcasted_iota(jnp.int32, (cells, block), 0) == cell).astype(F32)
        before = jnp.dot(here.astype(BF), below, preferred_element_type=F32) + carry
        carry = carry + jnp.sum(here, axis=1, keepdims=True)
        rank = jnp.sum(here * before, axis=0, keepdims=True).astype(jnp.int32)
        ranks.append(rank)
        place = (lax.broadcasted_iota(jnp.int32, (LANES, block), 0) == rank).astype(F32)
        high = (trow >> 5).astype(F32)
        low = (trow & 31).astype(F32)
        told = jnp.concatenate([here, here * high, here * low], axis=0)
        asked = asked + lax.dot_general(
            told.astype(BF), place.astype(BF), NT, preferred_element_type=F32
        )
    there = asked[:cells]
    rows = (asked[cells : 2 * cells] * 32.0 + asked[2 * cells :]).astype(jnp.int32)
    rows = jnp.where(there > 0.5, rows, -1)
    lane = lax.broadcasted_iota(jnp.int32, (cells, LANES), 1)
    over = (jnp.max(carry) > CAP).astype(jnp.int32)
    req_ref[...] = jnp.where(lane == LANES - 1, over, rows)
    rank_row = jnp.concatenate(ranks, axis=1)
    rank_ref[...] = rank_row
    slots = cells_row * CAP + rank_row
    by_row = jnp.concatenate([slots[:, j * tok : (j + 1) * tok] for j in range(per_token)], axis=0)
    projs = lax.rem(by_token, proj_count)
    blank = jnp.zeros((LANES - 3 * per_token, tok), F32)
    cols_ref[...] = jnp.concatenate(
        [projs.astype(F32), by_row.astype(F32), weights, blank], axis=0
    ).T


def send_kernel(
    group,
    tg_ref,
    proj_ref,
    cols_ref,
    cell_ref,
    rank_ref,
    wt_ref,
    out_ref,
    grads,
    projs,
    chosen,
    made,
    in_sems,
    out_sems,
):
    tok = cols_ref.shape[0]
    count = cell_ref.shape[1]
    per_token = count // tok
    proj_count = proj_ref.shape[0]
    come = [pltpu.make_async_copy(tg_ref, grads, in_sems.at[proj_count])]
    for p in range(proj_count):
        come.append(pltpu.make_async_copy(proj_ref.at[p], projs.at[p], in_sems.at[p]))
    for copy in come:
        copy.start()
    at = lax.broadcasted_iota(jnp.int32, (CAP, count), 0) == rank_ref[...]
    place = jnp.where(at, wt_ref[...], 0.0).astype(BF)
    come[0].wait()
    for p in range(proj_count):
        come[p + 1].wait()
        back = lax.dot_general(grads[...], projs[p], NT, preferred_element_type=F32).astype(BF)
        for j in range(per_token):
            span = pl.ds(j * tok, tok)
            if p == 0:
                chosen[span, :] = back
            else:
                chosen[span, :] = jnp.where(cols_ref[:, j : j + 1] == p, back, chosen[span, :])
    copies = []
    for g in range(made.shape[0] // (group * CAP)):
        parts = []
        for d in range(group):
            here = (cell_ref[...] == g * group + d).astype(F32).astype(BF)
            parts.append(place * here)
        pick = jnp.concatenate(parts, axis=0)
        span = pl.ds(g * group * CAP, group * CAP)
        made[span, :] = jnp.dot(pick, chosen[...], preferred_element_type=F32).astype(BF)
        copies.append(pltpu.make_async_copy(made.at[span, :], out_ref.at[span, :], out_sems.at[g]))
        copies[-1].start()
    for copy in copies:
        copy.wait()


def look_kernel(group, got_ref, z_ref, *refs):
    *pieces, out_ref, table, made, out_sems = refs
    rows = pieces[0].shape[0]
    cells = got_ref.shape[0]
    depth = len(pieces)
    for k, piece in enumerate(pieces):
        table[pl.ds(k * rows, rows), :] = piece[...]
    told = got_ref[...]
    from_z = lax.rem(lax.div(told, rows) + depth - z_ref[0], depth)
    asked = jnp.where(told < 0, -1, from_z * rows + lax.rem(told, rows)).T
    lane = lax.broadcasted_iota(jnp.int32, (CAP, depth * rows), 1)
    copies = []
    for g in range(cells // group):
        parts = []
        for d in range(g * group, (g + 1) * group):
            parts.append((lane == asked[:CAP, d : d + 1]).astype(F32).astype(BF))
        pick = jnp.concatenate(parts, axis=0)
        span = pl.ds(g * group * CAP, group * CAP)
        made[span, :] = jnp.dot(pick, table[...], preferred_element_type=F32).astype(BF)
        copies.append(pltpu.make_async_copy(made.at[span, :], out_ref.at[span, :], out_sems.at[g]))
        copies[-1].start()
    for copy in copies:
        copy.wait()


def sum_kernel(ids_ref, flags_ref, got_ref, *out_refs):
    rows = out_refs[0].shape[0]
    slots = ids_ref.shape[1]
    over = jnp.where(jnp.max(flags_ref[...]) > 0, OVER, 0.0)
    for k, out_ref in enumerate(out_refs):
        pick = lax.broadcasted_iota(jnp.int32, (rows, slots), 0) == ids_ref[...] - k * rows
        part = jnp.dot(pick.astype(F32).astype(BF), got_ref[...], preferred_element_type=F32)
        out_ref[...] = (part + over).astype(out_ref.dtype)


def out_kernel(
    per_token, cols_ref, ret_ref, proj_ref, out_ref, projs, made, in_sems, out_sems
):
    tok = cols_ref.shape[0]
    slots = ret_ref.shape[0]
    proj_count, width, out_width = proj_ref.shape
    chunks = made.shape[0]
    chunk = out_width // chunks
    spans = [pl.ds(n * chunk, chunk) for n in range(chunks)]
    come = [
        pltpu.make_async_copy(proj_ref.at[:, :, span], projs.at[:, :, span], in_sems.at[n])
        for n, span in enumerate(spans)
    ]
    for copy in come:
        copy.start()
    lane = lax.broadcasted_iota(jnp.int32, (tok, slots), 1)
    slot = cols_ref[:, per_token : 2 * per_token].astype(jnp.int32)
    pick = [(lane == slot[:, j : j + 1]).astype(F32).astype(BF) for j in range(per_token)]
    rows = jnp.dot(jnp.concatenate(pick, axis=0), ret_ref[...], preferred_element_type=F32)
    sums = []
    for p in range(proj_count):
        weight = [
            jnp.where(
                cols_ref[:, j : j + 1] == p,
                cols_ref[:, 2 * per_token + j : 2 * per_token + j + 1],
                0.0,
            )
            for j in range(per_token)
        ]
        parts = [rows[j * tok : (j + 1) * tok] * weight[j] for j in range(per_token)]
        sums.append(functools.reduce(lambda a, b: a + b, parts).astype(BF))
    mixed = jnp.concatenate(sums, axis=1)
    copies = []
    for n, span in enumerate(spans):
        come[n].wait()
        made[n] = jnp.dot(
            mixed,
            projs[:, :, span].reshape(proj_count * width, chunk),
            preferred_element_type=F32,
        ).astype(BF)
        copies.append(pltpu.make_async_copy(made.at[n], out_ref.at[:, span], out_sems.at[n]))
        copies[-1].start()
    for copy in copies:
        copy.wait()


def short_way(picks, pick_weights, token_grads, values, first_moment, second_moment, projectors):
    plane = ("y", "c", "x")
    cells = lax.axis_size(plane)
    depth = lax.axis_size("z")
    parts = lax.axis_size("x")
    rows_dev, width = values.shape
    quarter = rows_dev // parts
    tok, per_token = picks.shape
    proj_count, _, out_width = projectors.shape
    total = tok * per_token
    slots = cells * CAP
    table_rows = depth * quarter
    start = lax.axis_index("x") * quarter
    old_rows = lax.dynamic_slice_in_dim(values, start, quarter, 0)

    hbm = pl.BlockSpec(memory_space=pl.ANY)
    vmem = pl.BlockSpec(memory_space=pltpu.VMEM)
    i32 = lambda *shape: jax.ShapeDtypeStruct(shape, jnp.int32)
    f32 = lambda *shape: jax.ShapeDtypeStruct(shape, F32)
    cell, rank, wt_row, requests, cols = call(
        functools.partial(rank_kernel, (cells, depth, parts, rows_dev, proj_count)),
        (
            i32(1, total),
            i32(1, total),
            f32(1, total),
            i32(cells, LANES),
            f32(tok, LANES),
        ),
        60,
        in_specs=[vmem] * 2,
        out_specs=(vmem,) * 5,
        cost=cost(2 * total * cells * 400, 20000),
    )(picks.T, pick_weights.T)
    received = lax.all_to_all(requests, plane, split_axis=0, concat_axis=0, tiled=True)

    onward = [(i, (i + 1) % depth) for i in range(depth)]
    backward = [(i, (i - 1) % depth) for i in range(depth)]
    pieces = [old_rows] + [None] * (depth - 1)
    for k in range(1, depth // 2 + 1):
        pieces[k] = lax.ppermute(pieces[k - 1], "z", backward)
        if k < depth // 2:
            pieces[depth - k] = lax.ppermute(pieces[(depth - k + 1) % depth], "z", onward)

    group = 8
    sent = call(
        functools.partial(send_kernel, group),
        jax.ShapeDtypeStruct((slots, width), BF),
        60,
        in_specs=[hbm] * 2 + [vmem] * 4,
        out_specs=hbm,
        scratch=[
            pltpu.VMEM((tok, out_width), BF),
            pltpu.VMEM(projectors.shape, BF),
            pltpu.VMEM((total, width), BF),
            pltpu.VMEM((slots, width), BF),
            pltpu.SemaphoreType.DMA((proj_count + 1,)),
            pltpu.SemaphoreType.DMA((cells // group,)),
        ],
        cost=cost(2 * width * (tok * proj_count * out_width + slots * total), 12000000),
    )(token_grads, projectors, cols, cell, rank, wt_row)
    got = lax.all_to_all(
        sent.reshape(cells, CAP, width), plane, split_axis=0, concat_axis=0, tiled=True
    ).reshape(slots, width)

    z_here = lax.axis_index("z")
    told = received[:, :CAP]
    from_z = lax.rem(lax.div(told, quarter) + depth - z_here, depth)
    asked = jnp.where(told < 0, -1, from_z * quarter + lax.rem(told, quarter))
    flags = received[:, LANES - 1 :]
    looked = call(
        functools.partial(look_kernel, group),
        jax.ShapeDtypeStruct((slots, width), BF),
        24,
        in_specs=[vmem, pl.BlockSpec(memory_space=pltpu.SMEM)] + [vmem] * depth,
        out_specs=hbm,
        scratch=[
            pltpu.VMEM((table_rows, width), BF),
            pltpu.VMEM((slots, width), BF),
            pltpu.SemaphoreType.DMA((cells // group,)),
        ],
        cost=cost(2 * width * slots * table_rows, 4000000),
    )(received, z_here.reshape(1), *pieces)
    sums = call(
        sum_kernel,
        (jax.ShapeDtypeStruct((quarter, width), BF),) * depth,
        16,
        in_specs=[vmem] * 3,
        out_specs=(vmem,) * depth,
        cost=cost(2 * width * slots * table_rows, 4000000),
    )(asked.reshape(1, slots), flags, got)
    looked, *sums = lax.optimization_barrier((looked, *sums))
    returned = lax.all_to_all(
        looked.reshape(cells, CAP, width), plane, split_axis=0, concat_axis=0, tiled=True
    ).reshape(slots, width)

    ahead = sums[depth // 2]
    behind = sums[depth // 2 + 1]
    for k in range(depth // 2 - 1, 0, -1):
        ahead = (lax.ppermute(ahead, "z", onward).astype(F32) + sums[k].astype(F32)).astype(BF)
        if k > 1:
            behind = (
                lax.ppermute(behind, "z", backward).astype(F32) + sums[depth - k + 1].astype(F32)
            ).astype(BF)
    share = (
        sums[0].astype(F32)
        + lax.ppermute(ahead, "z", onward).astype(F32)
        + lax.ppermute(behind, "z", backward).astype(F32)
    )
    flag = share[0, 0] > 0.5 * OVER
    new_first, new_second, new_part = adam_rows(old_rows, share, first_moment, second_moment)
    new_parts = spread(new_part)

    chunks = 4
    layer_out = call(
        functools.partial(out_kernel, per_token),
        jax.ShapeDtypeStruct((tok, out_width), BF),
        48,
        in_specs=[vmem] * 2 + [hbm],
        out_specs=hbm,
        scratch=[
            pltpu.VMEM(projectors.shape, BF),
            pltpu.VMEM((chunks, tok, out_width // chunks), BF),
            pltpu.SemaphoreType.DMA((chunks,)),
            pltpu.SemaphoreType.DMA((chunks,)),
        ],
        cost=cost(2 * width * (tok * proj_count * out_width + slots * total), 13000000),
    )(cols, returned, projectors)
    return flag, (layer_out, new_parts, new_first, new_second)


def join_kernel(x_ref, *refs):
    *pieces, out_ref = refs
    parts = len(pieces)
    rows = pieces[0].shape[0]
    for k, piece in enumerate(pieces):
        first = lax.rem(x_ref[0] + parts - k, parts) * rows
        out_ref[pl.ds(pl.multiple_of(first, rows), rows), :] = piece[...]


def on_device(*args):
    flag, outs = short_way(*args)
    layer_out, new_parts, new_first, new_second = lax.cond(
        flag, lambda given, done: long_way(*given), lambda given, done: done, args, outs
    )
    rows, width = new_parts[0].shape
    vmem = pl.BlockSpec(memory_space=pltpu.VMEM)
    new_values = call(
        join_kernel,
        jax.ShapeDtypeStruct((len(new_parts) * rows, width), BF),
        60,
        in_specs=[pl.BlockSpec(memory_space=pltpu.SMEM)] + [vmem] * len(new_parts),
        out_specs=vmem,
    )(lax.axis_index("x").reshape(1), *new_parts)
    return layer_out, new_values, new_first, new_second


def solution(mesh):
    mem, dp = mesh.devices.shape
    grid = Mesh(
        mesh.devices.reshape(mem // (Z_CHIPS * CORES), Z_CHIPS, CORES, dp), ("y", "z", "c", "x")
    )
    every = P(("y", "z", "c", "x"), None)
    slab = P(("y", "z", "c"), None)
    return jax.shard_map(
        on_device,
        mesh=grid,
        in_specs=(every, every, every, slab, every, every, P()),
        out_specs=(every, slab, every, every),
        check_vma=False,
    )
```

```python
import functools

import jax
import jax.numpy as jnp
from jax import lax
from jax.experimental import pallas as pl
from jax.experimental.pallas import tpu as pltpu
from jax.sharding import Mesh
from jax.sharding import PartitionSpec as P

beta_one = 0.9
beta_two = 0.999
corr_one = 1.0 - 0.9**50
corr_two = 1.0 - 0.999**50
learn_rate = 0.05
adam_eps = 1e-08

Z_CHIPS = 8
CORES = 2
CAP = 72
LANES = 128
OVER = 1e30
BF = jnp.bfloat16
F32 = jnp.float32
NT = (((1,), (1,)), ((), ()))


def adam_rows(old_rows, slab_grad, first_moment, second_moment):
    new_first = beta_one * first_moment + (1.0 - beta_one) * slab_grad
    new_second = beta_two * second_moment + (1.0 - beta_two) * slab_grad * slab_grad
    update_step = new_first / corr_one / (jnp.sqrt(new_second / corr_two) + adam_eps)
    updated = (old_rows.astype(jnp.float32) - learn_rate * update_step).astype(jnp.bfloat16)
    return (new_first, new_second, updated)


def spread(new_part):
    parts = lax.axis_size("x")
    return [new_part] + [
        lax.ppermute(new_part, "x", [(i, (i + k) % parts) for i in range(parts)])
        for k in range(1, parts)
    ]


def long_way(picks, pick_weights, token_grads, values, first_moment, second_moment, projectors):
    mem = ("y", "z", "c")
    owners = lax.axis_size(mem)
    rows_dev, width = values.shape
    tok_count, per_token = picks.shape
    proj_count, _, out_width = projectors.shape
    total_picks = tok_count * per_token
    capacity = 2 * total_picks // owners
    slots = owners * capacity
    swap = lambda rows: lax.all_to_all(rows, mem, split_axis=0, concat_axis=0, tiled=True)
    flat_picks = picks.reshape(-1)
    owner_ids = flat_picks // rows_dev
    local_rows = flat_picks - owner_ids * rows_dev
    member = (owner_ids[:, None] == jnp.arange(owners, dtype=jnp.int32)[None, :]).astype(jnp.int32)
    before = jnp.cumsum(member, axis=0) - member
    slot_ids = owner_ids * capacity + jnp.sum(before * member, axis=1)
    number = jnp.arange(total_picks, dtype=jnp.int32)
    pick_in = jnp.full((slots,), total_picks, jnp.int32).at[slot_ids].set(number)
    in_slots = lambda per_pick: jnp.concatenate([per_pick, jnp.zeros((1,), per_pick.dtype)])[pick_in]
    proj_ids = picks % proj_count
    requests = in_slots(local_rows).reshape(owners, capacity)
    received = swap(requests)
    returned = swap(values[received])
    _, back_grads = lax.scan(
        lambda none, proj: (
            none,
            lax.dot_general(token_grads, proj, NT, preferred_element_type=F32).astype(BF),
        ),
        0,
        projectors,
    )
    back_rows = in_slots(proj_ids.reshape(-1) * tok_count + number // per_token)
    send_rows = back_grads.reshape(proj_count * tok_count, width)[back_rows]
    got_rows = swap(send_rows.reshape(owners, capacity, width)).reshape(slots, width)
    got_wts = swap(in_slots(pick_weights.reshape(-1)).reshape(owners, capacity)).reshape(slots)
    picked = returned.reshape(slots, width)[slot_ids].reshape(tok_count, per_token, width)
    mixing = jnp.where(
        proj_ids[..., None] == jnp.arange(proj_count, dtype=jnp.int32),
        pick_weights[..., None],
        jnp.zeros((), BF),
    )
    proj_sums = jnp.einsum("tjp,tjd->ptd", mixing, picked, preferred_element_type=F32).astype(BF)
    layer_out, _ = lax.scan(
        lambda acc, part: (acc + jnp.dot(*part, preferred_element_type=F32), None),
        jnp.zeros((tok_count, out_width), F32),
        (proj_sums, projectors),
    )
    chunk = slots // 20

    def add_chunk(acc, part):
        ids, wts, rows = part
        place = jnp.arange(rows_dev, dtype=jnp.int32)[:, None] == ids[None, :]
        place = jnp.where(place, wts[None, :], jnp.zeros((), BF))
        return acc + jnp.dot(place, rows, preferred_element_type=F32), None

    slab_grad, _ = lax.scan(
        add_chunk,
        jnp.zeros((rows_dev, width), F32),
        (
            received.reshape(-1, chunk),
            got_wts.reshape(-1, chunk),
            got_rows.reshape(-1, chunk, width),
        ),
    )
    quarter = first_moment.shape[0]
    share = jnp.sum(
        lax.all_to_all(
            slab_grad.reshape(-1, quarter, width), "x", split_axis=0, concat_axis=0, tiled=True
        ),
        axis=0,
    )
    old_rows = lax.dynamic_slice_in_dim(values, lax.axis_index("x") * quarter, quarter, 0)
    new_first, new_second, new_part = adam_rows(old_rows, share, first_moment, second_moment)
    return layer_out.astype(BF), spread(new_part), new_first, new_second


def call(kernel, out_shape, vmem, grid=None, in_specs=None, out_specs=None, scratch=(), cost=None):
    extra = {} if grid is None else {"grid": grid}
    if in_specs is not None:
        extra["in_specs"] = in_specs
    if out_specs is not None:
        extra["out_specs"] = out_specs
    return pl.pallas_call(
        kernel,
        out_shape=out_shape,
        scratch_shapes=list(scratch),
        compiler_params=pltpu.CompilerParams(vmem_limit_bytes=vmem * 1024 * 1024),
        cost_estimate=cost,
        **extra,
    )


def cost(flops, nbytes):
    return pl.CostEstimate(flops=flops, bytes_accessed=nbytes, transcendentals=0)


def rank_kernel(
    sizes, pick_ref, wt_ref, cell_ref, rank_ref, wrow_ref, req_ref, cols_ref
):
    cells, depth, parts, rows_dev, proj_count = sizes
    per_token, tok = pick_ref.shape
    count = per_token * tok
    quarter = rows_dev // parts
    block = 256
    by_token = pick_ref[...]
    flat = jnp.concatenate([by_token[j : j + 1] for j in range(per_token)], axis=1)
    weights = wt_ref[...].astype(F32)
    wrow_ref[...] = jnp.concatenate([weights[j : j + 1] for j in range(per_token)], axis=1)
    owner = lax.div(flat, rows_dev)
    row = lax.rem(flat, rows_dev)
    owner_z = lax.rem(lax.div(owner, CORES), depth)
    cells_row = (
        lax.div(owner, depth * CORES) * CORES + lax.rem(owner, CORES)
    ) * parts + lax.div(row, quarter)
    trows = owner_z * quarter + lax.rem(row, quarter)
    cell_ref[...] = cells_row
    below = lax.broadcasted_iota(jnp.int32, (block, block), 0) < lax.broadcasted_iota(
        jnp.int32, (block, block), 1
    )
    below = below.astype(F32).astype(BF)
    carry = jnp.zeros((cells, 1), F32)
    asked = jnp.zeros((3 * cells, LANES), F32)
    ranks = []
    for b in range(count // block):
        cell = cells_row[:, b * block : (b + 1) * block]
        trow = trows[:, b * block : (b + 1) * block]
        here = (lax.broadcasted_iota(jnp.int32, (cells, block), 0) == cell).astype(F32)
        before = jnp.dot(here.astype(BF), below, preferred_element_type=F32) + carry
        carry = carry + jnp.sum(here, axis=1, keepdims=True)
        rank = jnp.sum(here * before, axis=0, keepdims=True).astype(jnp.int32)
        ranks.append(rank)
        place = (lax.broadcasted_iota(jnp.int32, (LANES, block), 0) == rank).astype(F32)
        high = (trow >> 5).astype(F32)
        low = (trow & 31).astype(F32)
        told = jnp.concatenate([here, here * high, here * low], axis=0)
        asked = asked + lax.dot_general(
            told.astype(BF), place.astype(BF), NT, preferred_element_type=F32
        )
    there = asked[:cells]
    rows = (asked[cells : 2 * cells] * 32.0 + asked[2 * cells :]).astype(jnp.int32)
    rows = jnp.where(there > 0.5, rows, -1)
    lane = lax.broadcasted_iota(jnp.int32, (cells, LANES), 1)
    over = (jnp.max(carry) > CAP).astype(jnp.int32)
    req_ref[...] = jnp.where(lane == LANES - 1, over, rows)
    rank_row = jnp.concatenate(ranks, axis=1)
    rank_ref[...] = rank_row
    slots = cells_row * CAP + rank_row
    by_row = jnp.concatenate([slots[:, j * tok : (j + 1) * tok] for j in range(per_token)], axis=0)
    projs = lax.rem(by_token, proj_count)
    blank = jnp.zeros((LANES - 3 * per_token, tok), F32)
    cols_ref[...] = jnp.concatenate(
        [projs.astype(F32), by_row.astype(F32), weights, blank], axis=0
    ).T


def send_kernel(
    group,
    tg_ref,
    proj_ref,
    cols_ref,
    cell_ref,
    rank_ref,
    wt_ref,
    out_ref,
    grads,
    projs,
    chosen,
    made,
    in_sems,
    out_sems,
):
    tok = cols_ref.shape[0]
    count = cell_ref.shape[1]
    per_token = count // tok
    proj_count = proj_ref.shape[0]
    come = [pltpu.make_async_copy(tg_ref, grads, in_sems.at[proj_count])]
    for p in range(proj_count):
        come.append(pltpu.make_async_copy(proj_ref.at[p], projs.at[p], in_sems.at[p]))
    for copy in come:
        copy.start()
    at = lax.broadcasted_iota(jnp.int32, (CAP, count), 0) == rank_ref[...]
    place = jnp.where(at, wt_ref[...], 0.0).astype(BF)
    come[0].wait()
    for p in range(proj_count):
        come[p + 1].wait()
        back = lax.dot_general(grads[...], projs[p], NT, preferred_element_type=F32).astype(BF)
        for j in range(per_token):
            span = pl.ds(j * tok, tok)
            if p == 0:
                chosen[span, :] = back
            else:
                chosen[span, :] = jnp.where(cols_ref[:, j : j + 1] == p, back, chosen[span, :])
    copies = []
    for g in range(made.shape[0] // (group * CAP)):
        parts = []
        for d in range(group):
            here = (cell_ref[...] == g * group + d).astype(F32).astype(BF)
            parts.append(place * here)
        pick = jnp.concatenate(parts, axis=0)
        span = pl.ds(g * group * CAP, group * CAP)
        made[span, :] = jnp.dot(pick, chosen[...], preferred_element_type=F32).astype(BF)
        copies.append(pltpu.make_async_copy(made.at[span, :], out_ref.at[span, :], out_sems.at[g]))
        copies[-1].start()
    for copy in copies:
        copy.wait()


def look_kernel(group, got_ref, z_ref, *refs):
    *pieces, out_ref, table, made, out_sems = refs
    rows = pieces[0].shape[0]
    cells = got_ref.shape[0]
    depth = len(pieces)
    for k, piece in enumerate(pieces):
        table[pl.ds(k * rows, rows), :] = piece[...]
    told = got_ref[...]
    from_z = lax.rem(lax.div(told, rows) + depth - z_ref[0], depth)
    asked = jnp.where(told < 0, -1, from_z * rows + lax.rem(told, rows)).T
    lane = lax.broadcasted_iota(jnp.int32, (CAP, depth * rows), 1)
    copies = []
    for g in range(cells // group):
        parts = []
        for d in range(g * group, (g + 1) * group):
            parts.append((lane == asked[:CAP, d : d + 1]).astype(F32).astype(BF))
        pick = jnp.concatenate(parts, axis=0)
        span = pl.ds(g * group * CAP, group * CAP)
        made[span, :] = jnp.dot(pick, table[...], preferred_element_type=F32).astype(BF)
        copies.append(pltpu.make_async_copy(made.at[span, :], out_ref.at[span, :], out_sems.at[g]))
        copies[-1].start()
    for copy in copies:
        copy.wait()


def sum_kernel(ids_ref, flags_ref, got_ref, *out_refs):
    rows = out_refs[0].shape[0]
    slots = ids_ref.shape[1]
    over = jnp.where(jnp.max(flags_ref[...]) > 0, OVER, 0.0)
    for k, out_ref in enumerate(out_refs):
        pick = lax.broadcasted_iota(jnp.int32, (rows, slots), 0) == ids_ref[...] - k * rows
        part = jnp.dot(pick.astype(F32).astype(BF), got_ref[...], preferred_element_type=F32)
        out_ref[...] = (part + over).astype(out_ref.dtype)


def out_kernel(
    per_token, cols_ref, ret_ref, proj_ref, out_ref, projs, made, in_sems, out_sems
):
    tok = cols_ref.shape[0]
    slots = ret_ref.shape[0]
    proj_count, width, out_width = proj_ref.shape
    chunks = made.shape[0]
    chunk = out_width // chunks
    spans = [pl.ds(n * chunk, chunk) for n in range(chunks)]
    come = [
        pltpu.make_async_copy(proj_ref.at[:, :, span], projs.at[:, :, span], in_sems.at[n])
        for n, span in enumerate(spans)
    ]
    for copy in come:
        copy.start()
    lane = lax.broadcasted_iota(jnp.int32, (tok, slots), 1)
    slot = cols_ref[:, per_token : 2 * per_token].astype(jnp.int32)
    pick = [(lane == slot[:, j : j + 1]).astype(F32).astype(BF) for j in range(per_token)]
    rows = jnp.dot(jnp.concatenate(pick, axis=0), ret_ref[...], preferred_element_type=F32)
    sums = []
    for p in range(proj_count):
        weight = [
            jnp.where(
                cols_ref[:, j : j + 1] == p,
                cols_ref[:, 2 * per_token + j : 2 * per_token + j + 1],
                0.0,
            )
            for j in range(per_token)
        ]
        parts = [rows[j * tok : (j + 1) * tok] * weight[j] for j in range(per_token)]
        sums.append(functools.reduce(lambda a, b: a + b, parts).astype(BF))
    mixed = jnp.concatenate(sums, axis=1)
    copies = []
    for n, span in enumerate(spans):
        come[n].wait()
        made[n] = jnp.dot(
            mixed,
            projs[:, :, span].reshape(proj_count * width, chunk),
            preferred_element_type=F32,
        ).astype(BF)
        copies.append(pltpu.make_async_copy(made.at[n], out_ref.at[:, span], out_sems.at[n]))
        copies[-1].start()
    for copy in copies:
        copy.wait()


def short_way(picks, pick_weights, token_grads, values, first_moment, second_moment, projectors):
    plane = ("y", "c", "x")
    cells = lax.axis_size(plane)
    depth = lax.axis_size("z")
    parts = lax.axis_size("x")
    rows_dev, width = values.shape
    quarter = rows_dev // parts
    tok, per_token = picks.shape
    proj_count, _, out_width = projectors.shape
    total = tok * per_token
    slots = cells * CAP
    table_rows = depth * quarter
    start = lax.axis_index("x") * quarter
    old_rows = lax.dynamic_slice_in_dim(values, start, quarter, 0)

    hbm = pl.BlockSpec(memory_space=pl.ANY)
    vmem = pl.BlockSpec(memory_space=pltpu.VMEM)
    i32 = lambda *shape: jax.ShapeDtypeStruct(shape, jnp.int32)
    f32 = lambda *shape: jax.ShapeDtypeStruct(shape, F32)
    cell, rank, wt_row, requests, cols = call(
        functools.partial(rank_kernel, (cells, depth, parts, rows_dev, proj_count)),
        (
            i32(1, total),
            i32(1, total),
            f32(1, total),
            i32(cells, LANES),
            f32(tok, LANES),
        ),
        60,
        in_specs=[vmem] * 2,
        out_specs=(vmem,) * 5,
        cost=cost(2 * total * cells * 400, 20000),
    )(picks.T, pick_weights.T)
    received = lax.all_to_all(requests, plane, split_axis=0, concat_axis=0, tiled=True)

    along = lambda rows, k: lax.ppermute(rows, "z", [(i, (i + k) % depth) for i in range(depth)])
    half = depth // 2
    pieces = [old_rows] + [None] * (depth - 1)
    for k in range(1, half):
        pieces[k] = along(pieces[k - 1], -1)
        pieces[depth - k] = along(pieces[(depth - k + 1) % depth], 1)
    pieces[half] = along(pieces[1], 1 - half)

    group = 8
    sent = call(
        functools.partial(send_kernel, group),
        jax.ShapeDtypeStruct((slots, width), BF),
        60,
        in_specs=[hbm] * 2 + [vmem] * 4,
        out_specs=hbm,
        scratch=[
            pltpu.VMEM((tok, out_width), BF),
            pltpu.VMEM(projectors.shape, BF),
            pltpu.VMEM((total, width), BF),
            pltpu.VMEM((slots, width), BF),
            pltpu.SemaphoreType.DMA((proj_count + 1,)),
            pltpu.SemaphoreType.DMA((cells // group,)),
        ],
        cost=cost(2 * width * (tok * proj_count * out_width + slots * total), 12000000),
    )(token_grads, projectors, cols, cell, rank, wt_row)
    got = lax.all_to_all(
        sent.reshape(cells, CAP, width), plane, split_axis=0, concat_axis=0, tiled=True
    ).reshape(slots, width)

    z_here = lax.axis_index("z")
    told = received[:, :CAP]
    from_z = lax.rem(lax.div(told, quarter) + depth - z_here, depth)
    asked = jnp.where(told < 0, -1, from_z * quarter + lax.rem(told, quarter))
    flags = received[:, LANES - 1 :]
    looked = call(
        functools.partial(look_kernel, group),
        jax.ShapeDtypeStruct((slots, width), BF),
        24,
        in_specs=[vmem, pl.BlockSpec(memory_space=pltpu.SMEM)] + [vmem] * depth,
        out_specs=hbm,
        scratch=[
            pltpu.VMEM((table_rows, width), BF),
            pltpu.VMEM((slots, width), BF),
            pltpu.SemaphoreType.DMA((cells // group,)),
        ],
        cost=cost(2 * width * slots * table_rows, 4000000),
    )(received, z_here.reshape(1), *pieces)
    sums = call(
        sum_kernel,
        (jax.ShapeDtypeStruct((quarter, width), BF),) * depth,
        16,
        in_specs=[vmem] * 3,
        out_specs=(vmem,) * depth,
        cost=cost(2 * width * slots * table_rows, 4000000),
    )(asked.reshape(1, slots), flags, got)
    looked, *sums = lax.optimization_barrier((looked, *sums))
    returned = lax.all_to_all(
        looked.reshape(cells, CAP, width), plane, split_axis=0, concat_axis=0, tiled=True
    ).reshape(slots, width)

    added = lambda *rows: functools.reduce(lambda p, q: p + q, [r.astype(F32) for r in rows])
    far = along(sums[half], half - 1)
    ahead = sums[half - 1]
    behind = sums[half + 1]
    for k in range(half - 2, 0, -1):
        last = [far] if k == 1 else []
        ahead = added(sums[k], along(ahead, 1), *last).astype(BF)
        behind = added(sums[depth - k], along(behind, -1)).astype(BF)
    share = added(sums[0], along(ahead, 1), along(behind, -1))
    flag = share[0, 0] > 0.5 * OVER
    new_first, new_second, new_part = adam_rows(old_rows, share, first_moment, second_moment)
    new_parts = spread(new_part)

    chunks = 4
    layer_out = call(
        functools.partial(out_kernel, per_token),
        jax.ShapeDtypeStruct((tok, out_width), BF),
        48,
        in_specs=[vmem] * 2 + [hbm],
        out_specs=hbm,
        scratch=[
            pltpu.VMEM(projectors.shape, BF),
            pltpu.VMEM((chunks, tok, out_width // chunks), BF),
            pltpu.SemaphoreType.DMA((chunks,)),
            pltpu.SemaphoreType.DMA((chunks,)),
        ],
        cost=cost(2 * width * (tok * proj_count * out_width + slots * total), 13000000),
    )(cols, returned, projectors)
    return flag, (layer_out, new_parts, new_first, new_second)


def join_kernel(x_ref, *refs):
    *pieces, out_ref = refs
    parts = len(pieces)
    rows = pieces[0].shape[0]
    for k, piece in enumerate(pieces):
        first = lax.rem(x_ref[0] + parts - k, parts) * rows
        out_ref[pl.ds(pl.multiple_of(first, rows), rows), :] = piece[...]


def on_device(*args):
    flag, outs = short_way(*args)
    layer_out, new_parts, new_first, new_second = lax.cond(
        flag, lambda given, done: long_way(*given), lambda given, done: done, args, outs
    )
    rows, width = new_parts[0].shape
    vmem = pl.BlockSpec(memory_space=pltpu.VMEM)
    new_values = call(
        join_kernel,
        jax.ShapeDtypeStruct((len(new_parts) * rows, width), BF),
        60,
        in_specs=[pl.BlockSpec(memory_space=pltpu.SMEM)] + [vmem] * len(new_parts),
        out_specs=vmem,
    )(lax.axis_index("x").reshape(1), *new_parts)
    return layer_out, new_values, new_first, new_second


def solution(mesh):
    mem, dp = mesh.devices.shape
    grid = Mesh(
        mesh.devices.reshape(mem // (Z_CHIPS * CORES), Z_CHIPS, CORES, dp), ("y", "z", "c", "x")
    )
    every = P(("y", "z", "c", "x"), None)
    slab = P(("y", "z", "c"), None)
    return jax.shard_map(
        on_device,
        mesh=grid,
        in_specs=(every, every, every, slab, every, every, P()),
        out_specs=(every, slab, every, every),
        check_vma=False,
    )
```

```python
import functools

import jax
import jax.numpy as jnp
from jax import lax
from jax.experimental import pallas as pl
from jax.experimental.pallas import tpu as pltpu
from jax.sharding import Mesh
from jax.sharding import PartitionSpec as P

beta_one = 0.9
beta_two = 0.999
corr_one = 1.0 - 0.9**50
corr_two = 1.0 - 0.999**50
learn_rate = 0.05
adam_eps = 1e-08

Z_CHIPS = 8
CORES = 2
CAP = 72
LANES = 128
OVER = 1e30
BF = jnp.bfloat16
F32 = jnp.float32
NT = (((1,), (1,)), ((), ()))


def adam_rows(old_rows, slab_grad, first_moment, second_moment):
    new_first = beta_one * first_moment + (1.0 - beta_one) * slab_grad
    new_second = beta_two * second_moment + (1.0 - beta_two) * slab_grad * slab_grad
    update_step = new_first / corr_one / (jnp.sqrt(new_second / corr_two) + adam_eps)
    updated = (old_rows.astype(jnp.float32) - learn_rate * update_step).astype(jnp.bfloat16)
    return (new_first, new_second, updated)


def spread(new_part):
    parts = lax.axis_size("x")
    return [new_part] + [
        lax.ppermute(new_part, "x", [(i, (i + k) % parts) for i in range(parts)])
        for k in range(1, parts)
    ]


def long_way(picks, pick_weights, token_grads, values, first_moment, second_moment, projectors):
    mem = ("y", "z", "c")
    owners = lax.axis_size(mem)
    rows_dev, width = values.shape
    tok_count, per_token = picks.shape
    proj_count, _, out_width = projectors.shape
    total_picks = tok_count * per_token
    capacity = 2 * total_picks // owners
    slots = owners * capacity
    swap = lambda rows: lax.all_to_all(rows, mem, split_axis=0, concat_axis=0, tiled=True)
    flat_picks = picks.reshape(-1)
    owner_ids = flat_picks // rows_dev
    local_rows = flat_picks - owner_ids * rows_dev
    member = (owner_ids[:, None] == jnp.arange(owners, dtype=jnp.int32)[None, :]).astype(jnp.int32)
    before = jnp.cumsum(member, axis=0) - member
    slot_ids = owner_ids * capacity + jnp.sum(before * member, axis=1)
    number = jnp.arange(total_picks, dtype=jnp.int32)
    pick_in = jnp.full((slots,), total_picks, jnp.int32).at[slot_ids].set(number)
    in_slots = lambda per_pick: jnp.concatenate([per_pick, jnp.zeros((1,), per_pick.dtype)])[pick_in]
    proj_ids = picks % proj_count
    requests = in_slots(local_rows).reshape(owners, capacity)
    received = swap(requests)
    returned = swap(values[received])
    _, back_grads = lax.scan(
        lambda none, proj: (
            none,
            lax.dot_general(token_grads, proj, NT, preferred_element_type=F32).astype(BF),
        ),
        0,
        projectors,
    )
    back_rows = in_slots(proj_ids.reshape(-1) * tok_count + number // per_token)
    send_rows = back_grads.reshape(proj_count * tok_count, width)[back_rows]
    got_rows = swap(send_rows.reshape(owners, capacity, width)).reshape(slots, width)
    got_wts = swap(in_slots(pick_weights.reshape(-1)).reshape(owners, capacity)).reshape(slots)
    picked = returned.reshape(slots, width)[slot_ids].reshape(tok_count, per_token, width)
    mixing = jnp.where(
        proj_ids[..., None] == jnp.arange(proj_count, dtype=jnp.int32),
        pick_weights[..., None],
        jnp.zeros((), BF),
    )
    proj_sums = jnp.einsum("tjp,tjd->ptd", mixing, picked, preferred_element_type=F32).astype(BF)
    layer_out, _ = lax.scan(
        lambda acc, part: (acc + jnp.dot(*part, preferred_element_type=F32), None),
        jnp.zeros((tok_count, out_width), F32),
        (proj_sums, projectors),
    )
    chunk = slots // 20

    def add_chunk(acc, part):
        ids, wts, rows = part
        place = jnp.arange(rows_dev, dtype=jnp.int32)[:, None] == ids[None, :]
        place = jnp.where(place, wts[None, :], jnp.zeros((), BF))
        return acc + jnp.dot(place, rows, preferred_element_type=F32), None

    slab_grad, _ = lax.scan(
        add_chunk,
        jnp.zeros((rows_dev, width), F32),
        (
            received.reshape(-1, chunk),
            got_wts.reshape(-1, chunk),
            got_rows.reshape(-1, chunk, width),
        ),
    )
    quarter = first_moment.shape[0]
    share = jnp.sum(
        lax.all_to_all(
            slab_grad.reshape(-1, quarter, width), "x", split_axis=0, concat_axis=0, tiled=True
        ),
        axis=0,
    )
    old_rows = lax.dynamic_slice_in_dim(values, lax.axis_index("x") * quarter, quarter, 0)
    new_first, new_second, new_part = adam_rows(old_rows, share, first_moment, second_moment)
    return layer_out.astype(BF), spread(new_part), new_first, new_second


def call(kernel, out_shape, vmem, grid=None, in_specs=None, out_specs=None, scratch=(), cost=None):
    extra = {} if grid is None else {"grid": grid}
    if in_specs is not None:
        extra["in_specs"] = in_specs
    if out_specs is not None:
        extra["out_specs"] = out_specs
    return pl.pallas_call(
        kernel,
        out_shape=out_shape,
        scratch_shapes=list(scratch),
        compiler_params=pltpu.CompilerParams(vmem_limit_bytes=vmem * 1024 * 1024),
        cost_estimate=cost,
        **extra,
    )


def cost(flops, nbytes):
    return pl.CostEstimate(flops=flops, bytes_accessed=nbytes, transcendentals=0)


def rank_kernel(
    sizes, pick_ref, wt_ref, cell_ref, rank_ref, wrow_ref, req_ref, cols_ref
):
    cells, depth, parts, rows_dev, proj_count = sizes
    per_token, tok = pick_ref.shape
    count = per_token * tok
    quarter = rows_dev // parts
    block = 256
    by_token = pick_ref[...]
    flat = jnp.concatenate([by_token[j : j + 1] for j in range(per_token)], axis=1)
    weights = wt_ref[...].astype(F32)
    wrow_ref[...] = jnp.concatenate([weights[j : j + 1] for j in range(per_token)], axis=1)
    owner = lax.div(flat, rows_dev)
    row = lax.rem(flat, rows_dev)
    owner_z = lax.rem(lax.div(owner, CORES), depth)
    cells_row = (
        lax.div(owner, depth * CORES) * CORES + lax.rem(owner, CORES)
    ) * parts + lax.div(row, quarter)
    trows = owner_z * quarter + lax.rem(row, quarter)
    cell_ref[...] = cells_row
    below = lax.broadcasted_iota(jnp.int32, (block, block), 0) < lax.broadcasted_iota(
        jnp.int32, (block, block), 1
    )
    below = below.astype(F32).astype(BF)
    carry = jnp.zeros((cells, 1), F32)
    asked = jnp.zeros((3 * cells, LANES), F32)
    ranks = []
    for b in range(count // block):
        cell = cells_row[:, b * block : (b + 1) * block]
        trow = trows[:, b * block : (b + 1) * block]
        here = (lax.broadcasted_iota(jnp.int32, (cells, block), 0) == cell).astype(F32)
        before = jnp.dot(here.astype(BF), below, preferred_element_type=F32) + carry
        carry = carry + jnp.sum(here, axis=1, keepdims=True)
        rank = jnp.sum(here * before, axis=0, keepdims=True).astype(jnp.int32)
        ranks.append(rank)
        place = (lax.broadcasted_iota(jnp.int32, (LANES, block), 0) == rank).astype(F32)
        high = (trow >> 5).astype(F32)
        low = (trow & 31).astype(F32)
        told = jnp.concatenate([here, here * high, here * low], axis=0)
        asked = asked + lax.dot_general(
            told.astype(BF), place.astype(BF), NT, preferred_element_type=F32
        )
    there = asked[:cells]
    rows = (asked[cells : 2 * cells] * 32.0 + asked[2 * cells :]).astype(jnp.int32)
    rows = jnp.where(there > 0.5, rows, -1)
    lane = lax.broadcasted_iota(jnp.int32, (cells, LANES), 1)
    over = (jnp.max(carry) > CAP).astype(jnp.int32)
    req_ref[...] = jnp.where(lane == LANES - 1, over, rows)
    rank_row = jnp.concatenate(ranks, axis=1)
    rank_ref[...] = rank_row
    slots = cells_row * CAP + rank_row
    by_row = jnp.concatenate([slots[:, j * tok : (j + 1) * tok] for j in range(per_token)], axis=0)
    projs = lax.rem(by_token, proj_count)
    blank = jnp.zeros((LANES - 3 * per_token, tok), F32)
    cols_ref[...] = jnp.concatenate(
        [projs.astype(F32), by_row.astype(F32), weights, blank], axis=0
    ).T


def send_kernel(
    group,
    tg_ref,
    proj_ref,
    cols_ref,
    cell_ref,
    rank_ref,
    wt_ref,
    out_ref,
    grads,
    projs,
    chosen,
    made,
    in_sems,
    out_sems,
):
    tok = cols_ref.shape[0]
    count = cell_ref.shape[1]
    per_token = count // tok
    proj_count = proj_ref.shape[0]
    come = [pltpu.make_async_copy(tg_ref, grads, in_sems.at[proj_count])]
    for p in range(proj_count):
        come.append(pltpu.make_async_copy(proj_ref.at[p], projs.at[p], in_sems.at[p]))
    for copy in come:
        copy.start()
    at = lax.broadcasted_iota(jnp.int32, (CAP, count), 0) == rank_ref[...]
    place = jnp.where(at, wt_ref[...], 0.0).astype(BF)
    come[0].wait()
    for p in range(proj_count):
        come[p + 1].wait()
        back = lax.dot_general(grads[...], projs[p], NT, preferred_element_type=F32).astype(BF)
        for j in range(per_token):
            span = pl.ds(j * tok, tok)
            if p == 0:
                chosen[span, :] = back
            else:
                chosen[span, :] = jnp.where(cols_ref[:, j : j + 1] == p, back, chosen[span, :])
    copies = []
    for g in range(made.shape[0] // (group * CAP)):
        parts = []
        for d in range(group):
            here = (cell_ref[...] == g * group + d).astype(F32).astype(BF)
            parts.append(place * here)
        pick = jnp.concatenate(parts, axis=0)
        span = pl.ds(g * group * CAP, group * CAP)
        made[span, :] = jnp.dot(pick, chosen[...], preferred_element_type=F32).astype(BF)
        copies.append(pltpu.make_async_copy(made.at[span, :], out_ref.at[span, :], out_sems.at[g]))
        copies[-1].start()
    for copy in copies:
        copy.wait()


def look_kernel(group, got_ref, z_ref, *refs):
    *pieces, out_ref, table, made, out_sems = refs
    rows = pieces[0].shape[0]
    cells = got_ref.shape[0]
    depth = len(pieces)
    for k, piece in enumerate(pieces):
        table[pl.ds(k * rows, rows), :] = piece[...]
    told = got_ref[...]
    from_z = lax.rem(lax.div(told, rows) + depth - z_ref[0], depth)
    asked = jnp.where(told < 0, -1, from_z * rows + lax.rem(told, rows)).T
    lane = lax.broadcasted_iota(jnp.int32, (CAP, depth * rows), 1)
    copies = []
    for g in range(cells // group):
        parts = []
        for d in range(g * group, (g + 1) * group):
            parts.append((lane == asked[:CAP, d : d + 1]).astype(F32).astype(BF))
        pick = jnp.concatenate(parts, axis=0)
        span = pl.ds(g * group * CAP, group * CAP)
        made[span, :] = jnp.dot(pick, table[...], preferred_element_type=F32).astype(BF)
        copies.append(pltpu.make_async_copy(made.at[span, :], out_ref.at[span, :], out_sems.at[g]))
        copies[-1].start()
    for copy in copies:
        copy.wait()


def sum_kernel(ids_ref, flags_ref, got_ref, *out_refs):
    rows = out_refs[0].shape[0]
    slots = ids_ref.shape[1]
    over = jnp.where(jnp.max(flags_ref[...]) > 0, OVER, 0.0)
    for k, out_ref in enumerate(out_refs):
        pick = lax.broadcasted_iota(jnp.int32, (rows, slots), 0) == ids_ref[...] - k * rows
        part = jnp.dot(pick.astype(F32).astype(BF), got_ref[...], preferred_element_type=F32)
        out_ref[...] = (part + over).astype(out_ref.dtype)


def out_kernel(
    per_token, cols_ref, ret_ref, proj_ref, out_ref, projs, made, in_sems, out_sems
):
    tok = cols_ref.shape[0]
    slots = ret_ref.shape[0]
    proj_count, width, out_width = proj_ref.shape
    chunks = made.shape[0]
    chunk = out_width // chunks
    spans = [pl.ds(n * chunk, chunk) for n in range(chunks)]
    come = [
        pltpu.make_async_copy(proj_ref.at[:, :, span], projs.at[:, :, span], in_sems.at[n])
        for n, span in enumerate(spans)
    ]
    for copy in come:
        copy.start()
    lane = lax.broadcasted_iota(jnp.int32, (tok, slots), 1)
    slot = cols_ref[:, per_token : 2 * per_token].astype(jnp.int32)
    pick = [(lane == slot[:, j : j + 1]).astype(F32).astype(BF) for j in range(per_token)]
    rows = jnp.dot(jnp.concatenate(pick, axis=0), ret_ref[...], preferred_element_type=F32)
    sums = []
    for p in range(proj_count):
        weight = [
            jnp.where(
                cols_ref[:, j : j + 1] == p,
                cols_ref[:, 2 * per_token + j : 2 * per_token + j + 1],
                0.0,
            )
            for j in range(per_token)
        ]
        parts = [rows[j * tok : (j + 1) * tok] * weight[j] for j in range(per_token)]
        sums.append(functools.reduce(lambda a, b: a + b, parts).astype(BF))
    mixed = jnp.concatenate(sums, axis=1)
    copies = []
    for n, span in enumerate(spans):
        come[n].wait()
        made[n] = jnp.dot(
            mixed,
            projs[:, :, span].reshape(proj_count * width, chunk),
            preferred_element_type=F32,
        ).astype(BF)
        copies.append(pltpu.make_async_copy(made.at[n], out_ref.at[:, span], out_sems.at[n]))
        copies[-1].start()
    for copy in copies:
        copy.wait()


def short_way(picks, pick_weights, token_grads, values, first_moment, second_moment, projectors):
    plane = ("y", "c", "x")
    cells = lax.axis_size(plane)
    depth = lax.axis_size("z")
    parts = lax.axis_size("x")
    rows_dev, width = values.shape
    quarter = rows_dev // parts
    tok, per_token = picks.shape
    proj_count, _, out_width = projectors.shape
    total = tok * per_token
    slots = cells * CAP
    table_rows = depth * quarter
    start = lax.axis_index("x") * quarter
    old_rows = lax.dynamic_slice_in_dim(values, start, quarter, 0)

    hbm = pl.BlockSpec(memory_space=pl.ANY)
    vmem = pl.BlockSpec(memory_space=pltpu.VMEM)
    i32 = lambda *shape: jax.ShapeDtypeStruct(shape, jnp.int32)
    f32 = lambda *shape: jax.ShapeDtypeStruct(shape, F32)
    cell, rank, wt_row, requests, cols = call(
        functools.partial(rank_kernel, (cells, depth, parts, rows_dev, proj_count)),
        (
            i32(1, total),
            i32(1, total),
            f32(1, total),
            i32(cells, LANES),
            f32(tok, LANES),
        ),
        60,
        in_specs=[vmem] * 2,
        out_specs=(vmem,) * 5,
        cost=cost(2 * total * cells * 400, 20000),
    )(picks.T, pick_weights.T)
    received = lax.all_to_all(requests, plane, split_axis=0, concat_axis=0, tiled=True)

    along = lambda rows, k: lax.ppermute(rows, "z", [(i, (i + k) % depth) for i in range(depth)])
    half = depth // 2
    pieces = [old_rows] + [None] * (depth - 1)
    for k in range(1, half):
        pieces[k] = along(pieces[k - 1], -1)
        pieces[depth - k] = along(pieces[(depth - k + 1) % depth], 1)
    pieces[half] = along(pieces[half - 1], -1)

    group = 8
    sent = call(
        functools.partial(send_kernel, group),
        jax.ShapeDtypeStruct((slots, width), BF),
        60,
        in_specs=[hbm] * 2 + [vmem] * 4,
        out_specs=hbm,
        scratch=[
            pltpu.VMEM((tok, out_width), BF),
            pltpu.VMEM(projectors.shape, BF),
            pltpu.VMEM((total, width), BF),
            pltpu.VMEM((slots, width), BF),
            pltpu.SemaphoreType.DMA((proj_count + 1,)),
            pltpu.SemaphoreType.DMA((cells // group,)),
        ],
        cost=cost(2 * width * (tok * proj_count * out_width + slots * total), 12000000),
    )(token_grads, projectors, cols, cell, rank, wt_row)
    got = lax.all_to_all(
        sent.reshape(cells, CAP, width), plane, split_axis=0, concat_axis=0, tiled=True
    ).reshape(slots, width)

    z_here = lax.axis_index("z")
    told = received[:, :CAP]
    from_z = lax.rem(lax.div(told, quarter) + depth - z_here, depth)
    asked = jnp.where(told < 0, -1, from_z * quarter + lax.rem(told, quarter))
    flags = received[:, LANES - 1 :]
    looked = call(
        functools.partial(look_kernel, group),
        jax.ShapeDtypeStruct((slots, width), BF),
        24,
        in_specs=[vmem, pl.BlockSpec(memory_space=pltpu.SMEM)] + [vmem] * depth,
        out_specs=hbm,
        scratch=[
            pltpu.VMEM((table_rows, width), BF),
            pltpu.VMEM((slots, width), BF),
            pltpu.SemaphoreType.DMA((cells // group,)),
        ],
        cost=cost(2 * width * slots * table_rows, 4000000),
    )(received, z_here.reshape(1), *pieces)
    sums = call(
        sum_kernel,
        (jax.ShapeDtypeStruct((quarter, width), BF),) * depth,
        16,
        in_specs=[vmem] * 3,
        out_specs=(vmem,) * depth,
        cost=cost(2 * width * slots * table_rows, 4000000),
    )(asked.reshape(1, slots), flags, got)
    looked, *sums = lax.optimization_barrier((looked, *sums))
    returned = lax.all_to_all(
        looked.reshape(cells, CAP, width), plane, split_axis=0, concat_axis=0, tiled=True
    ).reshape(slots, width)

    added = lambda *rows: functools.reduce(lambda p, q: p + q, [r.astype(F32) for r in rows])
    far = along(sums[half], half - 1)
    ahead = sums[half - 1]
    behind = sums[half + 1]
    for k in range(half - 2, 0, -1):
        last = [far] if k == 1 else []
        ahead = added(sums[k], along(ahead, 1), *last).astype(BF)
        behind = added(sums[depth - k], along(behind, -1)).astype(BF)
    share = added(sums[0], along(ahead, 1), along(behind, -1))
    flag = share[0, 0] > 0.5 * OVER
    new_first, new_second, new_part = adam_rows(old_rows, share, first_moment, second_moment)
    new_parts = spread(new_part)

    chunks = 4
    layer_out = call(
        functools.partial(out_kernel, per_token),
        jax.ShapeDtypeStruct((tok, out_width), BF),
        48,
        in_specs=[vmem] * 2 + [hbm],
        out_specs=hbm,
        scratch=[
            pltpu.VMEM(projectors.shape, BF),
            pltpu.VMEM((chunks, tok, out_width // chunks), BF),
            pltpu.SemaphoreType.DMA((chunks,)),
            pltpu.SemaphoreType.DMA((chunks,)),
        ],
        cost=cost(2 * width * (tok * proj_count * out_width + slots * total), 13000000),
    )(cols, returned, projectors)
    return flag, (layer_out, new_parts, new_first, new_second)


def join_kernel(x_ref, *refs):
    *pieces, out_ref = refs
    parts = len(pieces)
    rows = pieces[0].shape[0]
    for k, piece in enumerate(pieces):
        first = lax.rem(x_ref[0] + parts - k, parts) * rows
        out_ref[pl.ds(pl.multiple_of(first, rows), rows), :] = piece[...]


def on_device(*args):
    flag, outs = short_way(*args)
    layer_out, new_parts, new_first, new_second = lax.cond(
        flag, lambda given, done: long_way(*given), lambda given, done: done, args, outs
    )
    rows, width = new_parts[0].shape
    vmem = pl.BlockSpec(memory_space=pltpu.VMEM)
    new_values = call(
        join_kernel,
        jax.ShapeDtypeStruct((len(new_parts) * rows, width), BF),
        60,
        in_specs=[pl.BlockSpec(memory_space=pltpu.SMEM)] + [vmem] * len(new_parts),
        out_specs=vmem,
    )(lax.axis_index("x").reshape(1), *new_parts)
    return layer_out, new_values, new_first, new_second


def solution(mesh):
    mem, dp = mesh.devices.shape
    grid = Mesh(
        mesh.devices.reshape(mem // (Z_CHIPS * CORES), Z_CHIPS, CORES, dp), ("y", "z", "c", "x")
    )
    every = P(("y", "z", "c", "x"), None)
    slab = P(("y", "z", "c"), None)
    return jax.shard_map(
        on_device,
        mesh=grid,
        in_specs=(every, every, every, slab, every, every, P()),
        out_specs=(every, slab, every, every),
        check_vma=False,
    )
```
